32 devices in a mesh: groups: 2 (over x), expert: 16 (over z, y, core).
Axes of the slice: x: 2, y: 2, z: 4, core: 2. Of those that a mesh axis runs over, the one named last changes fastest.
Arguments:
- tokens: bfloat16 [4096, 1664], P(('groups', 'expert')), parts along dimension 0, may hold values from -6 to 6
- expert_ids: int32 [4096, 2], P(('groups', 'expert')), parts along dimension 0, may hold values from 0 to 15, all different within a row
- priority: int32 [32, 128], P(('groups', 'expert')), parts along dimension 0, may hold values from 0 to 127, each once within a row
- gates: float32 [4096, 2], P(('groups', 'expert')), parts along dimension 0, may hold values from 0.1 to 1
- w_in: bfloat16 [16, 1664, 6144], P('expert'), may hold values from -0.15625 to 0.15625
- w_out: bfloat16 [16, 6144, 1664], P('expert'), may hold values from -0.078125 to 0.078125
- cotangent: bfloat16 [4096, 1664], P(('groups', 'expert')), parts along dimension 0, may hold values from -6 to 6
Outputs:
- mixed: bfloat16 [4096, 1664], P(('groups', 'expert')), parts along dimension 0
- d_tokens: bfloat16 [4096, 1664], P(('groups', 'expert')), parts along dimension 0
- d_gates: float32 [4096, 2], P(('groups', 'expert')), parts along dimension 0
- d_w_in: bfloat16 [32, 1664, 6144], P(('groups', 'expert')), parts along dimension 0
- d_w_out: bfloat16 [32, 6144, 1664], P(('groups', 'expert')), parts along dimension 0
The draws below stay inside these ranges and needn't reach their ends.
There are 2 independent parts, one for each index of `groups`. The reference program is written for one: setup_inputs(seed, part) draws one part's arguments, and reference() takes and returns one part's arrays. A program takes and returns all parts, laid end to end along the dimension named above; an argument that names none is the same for every part. Nothing has to cross between parts.
Inputs may be any that keep to these rules, and one draw needn't show every extreme that they name: `expert_ids`: each token names two different experts. `priority`: each row holds every rank of its block once.
All inputs are finite; a program needn't handle non-finite values.
Results may differ from the reference program's by a relative error of at most 0.006.
Values may be sent and summed in bfloat16 or wider, within the bound.
No kernel may reach another device: no remote copies, remote signals or barrier semaphores. Data moves between devices by JAX's collectives and lax.ppermute only.
A program may use at most 192 MiB of HBM per device.

```python
import math
import jax
import jax.numpy as jnp
from jax import lax

D = 1664
FF = 6144
EXPERTS = 16
CAP = 4
TOK_DEV = 128
BLOCKS = 16
FF_WIN = 6144
TOKENS = 2048


def shard_levels(stream_key, shape, pieces, least, top_value):
    loudness = 1.0
    for axis_at, shards_of in pieces:
        steps = jax.random.uniform(jax.random.fold_in(jax.random.fold_in(stream_key, 6), axis_at), (shards_of,), jnp.float32, least / len(pieces), top_value / len(pieces))
        loudness = loudness * jnp.repeat(jnp.exp(steps), shape[axis_at] // shards_of).reshape((-1,) + (1,) * (len(shape) - 1 - axis_at))
    return loudness


def picks_of(own_key, rows, count, top, lift):
    sequence = jax.random.permutation(jax.random.fold_in(own_key, 1), count)
    pull = sequence
    for power in range(3):
        pull = pull * pull // count
    pull = pull * lift // count
    chance = jax.random.randint(jax.random.fold_in(own_key, 2), (rows, count), 0, 4096) + pull
    fixed_rows = jax.random.permutation(jax.random.fold_in(own_key, 3), rows)[jnp.arange(count) % rows]
    chance = jnp.where(jnp.arange(rows)[:, None] == fixed_rows[None, :], 1 << 14, chance)
    score = chance * count + jnp.arange(count)
    return lax.top_k(score.astype(jnp.int32), top)[1].astype(jnp.int32)


def noise(stream_key, dims, scale, bound, shards=(), kind=jnp.bfloat16):
    array = scale * jax.random.normal(stream_key, dims, jnp.float32)
    if shards:
        array = array * shard_levels(stream_key, dims, shards, -0.22, 0.18)
    return jnp.clip(array, -bound, bound).astype(kind)


def setup_inputs(seed: int = 0, part: int = 0) -> dict:
    streams_of = jax.random.split(jax.random.key(seed), 8)
    part_keys = jax.random.split(jax.random.fold_in(streams_of[7], part), 8)
    tokens = noise(part_keys[0], (TOKENS, D), 1.0, 6.0, ((0, 16),))
    expert_ids = picks_of(part_keys[1], TOKENS, EXPERTS, 2, 2048)
    priority = jax.vmap(lambda own: jax.random.permutation(own, TOK_DEV))(jax.random.split(part_keys[2], BLOCKS)).reshape((BLOCKS, TOK_DEV)).astype(jnp.int32)
    gates = jnp.clip(jnp.exp(math.log(1.0) - 2.3025851 * jax.random.uniform(part_keys[3], (TOKENS, 2), jnp.float32) ** shard_levels(part_keys[3], (TOKENS, 2), ((0, 16),), -0.2, 0.2)), 0.1, 1.0)
    w_in = noise(streams_of[4], (BLOCKS, D, FF_WIN), D ** -0.5, 0.15625, ((0, 16),))
    w_out = noise(streams_of[5], (BLOCKS, FF_WIN, D), FF ** -0.5, 0.078125, ((0, 16),))
    cotangent = noise(part_keys[6], (TOKENS, D), 1.0, 6.0, ((0, 16),))
    return {"tokens": tokens, "expert_ids": expert_ids, "priority": priority, "gates": gates, "w_in": w_in, "w_out": w_out, "cotangent": cotangent}


def gelu_parts(value):
    coef = math.sqrt(2.0 / math.pi)
    inner = coef * (value + 0.044715 * value * value * value)
    hyper = jnp.tanh(inner)
    result = 0.5 * value * (1.0 + hyper)
    slope = 0.5 * (1.0 + hyper) + 0.5 * value * (1.0 - hyper * hyper) * coef * (1.0 + 3.0 * 0.044715 * value * value)
    return (result, slope)

def slot_table(ids_blk, prio_blk, tok_count):
    count = ids_blk.shape[0]
    expert_of = jnp.transpose(ids_blk, (0, 2, 1)).reshape(count, 2 * tok_count)
    key_of = jnp.concatenate([prio_blk, prio_blk + tok_count], axis=1)
    same = expert_of[:, :, None] == expert_of[:, None, :]
    before = key_of[:, None, :] < key_of[:, :, None]
    slot = lax.optimization_barrier(jnp.sum((same & before).astype(jnp.int32), axis=2)).astype(jnp.int32)
    place = jnp.where(slot < CAP, expert_of * CAP + slot, -1)
    columns = jnp.arange(EXPERTS * CAP, dtype=jnp.int32)
    return (place[:, :, None] == columns[None, None, :]).astype(jnp.float32)

def reference(tokens, expert_ids, priority, gates, w_in, w_out, cotangent):
    high = lax.Precision.HIGHEST
    width = tokens.shape[1]
    slots_all = EXPERTS * CAP
    x_blk = tokens.reshape(BLOCKS, TOK_DEV, width).astype(jnp.float32)
    dy_blk = cotangent.reshape(BLOCKS, TOK_DEV, width).astype(jnp.float32)
    gate_blk = gates.reshape(BLOCKS, TOK_DEV, 2)
    onehot = slot_table(expert_ids.reshape(BLOCKS, TOK_DEV, 2), priority, TOK_DEV)
    disp = onehot.reshape(BLOCKS, 2, TOK_DEV, slots_all).sum(1)
    gate_of = jnp.transpose(gate_blk, (0, 2, 1)).reshape(BLOCKS, 2 * TOK_DEV)
    weighted = (onehot * gate_of[:, :, None]).reshape(BLOCKS, 2, TOK_DEV, slots_all).sum(1)
    rows = jnp.einsum('btc,btd->bcd', disp, x_blk, precision=high).astype(jnp.bfloat16)
    grad_rows = jnp.einsum('btc,btd->bcd', weighted, dy_blk, precision=high).astype(jnp.bfloat16)

    def window_step(carry, device):
        out_acc, back_acc = carry
        expert = (device % EXPERTS).astype(jnp.int32)
        start = (expert * CAP).astype(jnp.int32)
        x_rows = lax.dynamic_slice_in_dim(rows, start, CAP, 1).reshape(BLOCKS * CAP, width)
        g_rows = lax.dynamic_slice_in_dim(grad_rows, start, CAP, 1).reshape(BLOCKS * CAP, width)
        w_first = lax.dynamic_index_in_dim(w_in, device, 0, keepdims=False)
        w_second = lax.dynamic_index_in_dim(w_out, device, 0, keepdims=False)
        pre = jnp.dot(x_rows, w_first, preferred_element_type=jnp.float32)
        value, slope = gelu_parts(pre)
        act = value.astype(jnp.bfloat16)
        out_part = jnp.dot(act, w_second, preferred_element_type=jnp.float32).astype(jnp.bfloat16)
        d_act = jnp.dot(g_rows, w_second.T, preferred_element_type=jnp.float32)
        d_pre = (d_act * slope).astype(jnp.bfloat16)
        back_part = jnp.dot(d_pre, w_first.T, preferred_element_type=jnp.float32).astype(jnp.bfloat16)
        grad_first = jnp.dot(x_rows.T, d_pre, preferred_element_type=jnp.float32).astype(jnp.bfloat16)
        grad_second = jnp.dot(act.T, g_rows, preferred_element_type=jnp.float32).astype(jnp.bfloat16)
        old_out = lax.dynamic_slice_in_dim(out_acc, start, CAP, 1)
        old_back = lax.dynamic_slice_in_dim(back_acc, start, CAP, 1)
        new_out = old_out + out_part.reshape(BLOCKS, CAP, width).astype(jnp.float32)
        new_back = old_back + back_part.reshape(BLOCKS, CAP, width).astype(jnp.float32)
        out_acc = lax.dynamic_update_slice_in_dim(out_acc, new_out, start, 1)
        back_acc = lax.dynamic_update_slice_in_dim(back_acc, new_back, start, 1)
        return ((out_acc, back_acc), (grad_first, grad_second))
    empty = jnp.zeros((BLOCKS, slots_all, width), jnp.float32)
    (out_rows, back_rows), (d_w_in, d_w_out) = lax.scan(window_step, (empty, empty), jnp.arange(BLOCKS, dtype=jnp.int32))
    picked = jnp.einsum('bac,bcd->bad', onehot, out_rows, precision=high).reshape(BLOCKS, 2, TOK_DEV, width)
    mixed = gate_blk[:, :, 0, None] * picked[:, 0] + gate_blk[:, :, 1, None] * picked[:, 1]
    mixed = mixed.reshape(TOKENS, width).astype(jnp.bfloat16)
    d_gates = jnp.stack([lax.optimization_barrier(jnp.sum(dy_blk * picked[:, 0], axis=-1)), lax.optimization_barrier(jnp.sum(dy_blk * picked[:, 1], axis=-1))], axis=-1)
    d_gates = d_gates.reshape(TOKENS, 2)
    d_tokens = jnp.einsum('btc,bcd->btd', disp, back_rows, precision=high).reshape(TOKENS, width).astype(jnp.bfloat16)
    return (mixed, d_tokens, d_gates, d_w_in, d_w_out)
```

```python
import functools
import math

import jax
import jax.numpy as jnp
from jax import lax
from jax.experimental import pallas as pl
from jax.experimental.pallas import tpu as pltpu
from jax.sharding import PartitionSpec as P

EXPERTS = 16
CAP = 4
PAIR = 2 * CAP
VMEM_BYTES = 60 * 1024 * 1024
ROWS_DIM = (((0,), (0,)), ((), ()))
LAST_DIM = (((1,), (1,)), ((), ()))


def gelu_parts(value):
    coef = math.sqrt(2.0 / math.pi)
    square = value * value
    hyper = jnp.tanh(coef * value * (1.0 + 0.044715 * square))
    half = 0.5 * (1.0 + hyper)
    slope = half + 0.5 * value * (1.0 - hyper * hyper) * coef * (1.0 + 3.0 * 0.044715 * square)
    return (value * half, slope)


def place_rows(ids_t, prio):
    count = ids_t.shape[1]
    first = ids_t[0:1, :]
    second = ids_t[1:2, :]
    stack = jnp.concatenate([first, second, prio, jnp.zeros((5, count), jnp.int32)], axis=0)
    columns = jnp.transpose(stack.astype(jnp.float32), (1, 0)).astype(jnp.int32)
    first_c, second_c, prio_c = columns[:, 0:1], columns[:, 1:2], columns[:, 2:3]
    ahead = prio_c < prio
    one = jnp.float32(1.0)
    zero = jnp.float32(0.0)
    slot_0 = jnp.sum(jnp.where((first_c == first) & ahead, one, zero), axis=0, keepdims=True)
    slot_1 = jnp.sum(
        jnp.where((first_c == second) | ((second_c == second) & ahead), one, zero),
        axis=0,
        keepdims=True,
    )
    slot_0 = slot_0.astype(jnp.int32)
    slot_1 = slot_1.astype(jnp.int32)
    place_0 = jnp.where(slot_0 < CAP, first * CAP + slot_0, -1)
    place_1 = jnp.where(slot_1 < CAP, second * CAP + slot_1, -1)
    return place_0, place_1


def dispatch_kernel(ids_ref, prio_ref, gates_ref, tok_ref, cot_ref, send_ref):
    place_0, place_1 = place_rows(ids_ref[...], prio_ref[...])
    count = tok_ref.shape[0]
    rows = EXPERTS * PAIR
    row = lax.broadcasted_iota(jnp.int32, (rows, count), 0)
    slot = row // PAIR * CAP + row % CAP
    is_x = row % PAIR < CAP
    hit_0 = slot == place_0
    hit_1 = slot == place_1
    hit = jnp.where(hit_0 | hit_1, 1.0, 0.0)
    pick = jnp.concatenate(
        [jnp.where(is_x, hit, 0.0), jnp.where(is_x, 0.0, hit)], axis=1
    ).astype(jnp.bfloat16)
    gate = jnp.where(hit_0, gates_ref[0:1, :], 0.0) + jnp.where(hit_1, gates_ref[1:2, :], 0.0)
    scale = jnp.sum(gate, axis=1, keepdims=True)
    scale = jnp.where(is_x[:, 0:1], 1.0, scale)
    both = jnp.concatenate([tok_ref[...], cot_ref[...]], axis=0)
    found = jnp.dot(pick, both, preferred_element_type=jnp.float32)
    send_ref[...] = (found * scale).astype(jnp.bfloat16)


def tables_kernel(ids_ref, prio_ref, gates_ref, pick_ref, gate_ref):
    place_0, place_1 = place_rows(ids_ref[...], prio_ref[...])
    count = place_0.shape[1]
    rows = EXPERTS * PAIR
    row = lax.broadcasted_iota(jnp.int32, (rows, count), 0)
    slot = row // PAIR * CAP + row % CAP
    is_x = row % PAIR < CAP
    hit_0 = jnp.where(slot == place_0, 1.0, 0.0)
    hit_1 = jnp.where(slot == place_1, 1.0, 0.0)
    pick_0 = jnp.transpose(jnp.where(is_x, hit_0, 0.0), (1, 0))
    pick_1 = jnp.transpose(jnp.where(is_x, hit_1, 0.0), (1, 0))
    pick_b = jnp.transpose(jnp.where(is_x, 0.0, hit_0 + hit_1), (1, 0))
    pick_ref[...] = jnp.concatenate([pick_0, pick_1, pick_b], axis=0).astype(jnp.bfloat16)
    gates = jnp.concatenate([gates_ref[...], jnp.zeros((6, count), jnp.float32)], axis=0)
    gate_ref[...] = jnp.transpose(gates, (1, 0))


def row_picks(rows):
    half = rows // 2
    out = lax.broadcasted_iota(jnp.int32, (half, rows), 0)
    col = lax.broadcasted_iota(jnp.int32, (half, rows), 1)
    source = out // CAP * PAIR + out % CAP
    x_pick = jnp.where(col == source, 1.0, 0.0).astype(jnp.bfloat16)
    g_pick = jnp.where(col == source + CAP, 1.0, 0.0).astype(jnp.bfloat16)
    return x_pick, g_pick


def forward_kernel(
    steps, recv_ref, w_in_hbm, w_out_hbm, ret_ref, x_ref, g_ref, act_ref, d_pre_ref,
    w_in_ref, w_out_ref, out_acc, back_acc, sem_in, sem_out,
):
    depth = w_in_ref.shape[2]

    def copies(step):
        cols = pl.ds(pl.multiple_of(step * depth, depth), depth)
        return (
            pltpu.make_async_copy(w_in_hbm.at[:, cols], w_in_ref.at[step], sem_in.at[step]),
            pltpu.make_async_copy(w_out_hbm.at[cols, :], w_out_ref.at[step], sem_out.at[step]),
        )

    def begin(step, carry):
        for copy in copies(step):
            copy.start()
        return carry

    lax.fori_loop(0, steps, begin, 0)
    rows = recv_ref.shape[0]
    x_pick, g_pick = row_picks(rows)
    x_ref[...] = jnp.dot(x_pick, recv_ref[...], preferred_element_type=jnp.float32).astype(
        jnp.bfloat16
    )
    g_ref[...] = jnp.dot(g_pick, recv_ref[...], preferred_element_type=jnp.float32).astype(
        jnp.bfloat16
    )
    out_acc[...] = jnp.zeros_like(out_acc)
    back_acc[...] = jnp.zeros_like(back_acc)

    def front(step):
        for copy in copies(step):
            copy.wait()
        pre = jnp.dot(x_ref[...], w_in_ref[step], preferred_element_type=jnp.float32)
        d_act = lax.dot_general(
            g_ref[...], w_out_ref[step], LAST_DIM, preferred_element_type=jnp.float32
        )
        value, slope = gelu_parts(pre)
        act_ref[step] = value.astype(jnp.bfloat16)
        d_pre_ref[step] = (d_act * slope).astype(jnp.bfloat16)

    def back(step):
        out_acc[...] += jnp.dot(
            act_ref[step], w_out_ref[step], preferred_element_type=jnp.float32
        )
        back_acc[...] += lax.dot_general(
            d_pre_ref[step], w_in_ref[step], LAST_DIM, preferred_element_type=jnp.float32
        )

    front(0)

    def body(step, carry):
        back(step - 1)
        front(step)
        return carry

    lax.fori_loop(1, steps, body, 0)
    back(steps - 1)
    ret = lax.dot_general(
        x_pick, out_acc[...].astype(jnp.bfloat16), ROWS_DIM, preferred_element_type=jnp.float32
    ) + lax.dot_general(
        g_pick, back_acc[...].astype(jnp.bfloat16), ROWS_DIM, preferred_element_type=jnp.float32
    )
    ret_ref[...] = ret.astype(jnp.bfloat16)


def grads_kernel(x_ref, g_ref, act_ref, d_pre_ref, d_in_ref, d_out_ref):
    d_in_ref[...] = lax.dot_general(
        x_ref[...], d_pre_ref[0], ROWS_DIM, preferred_element_type=jnp.float32
    ).astype(jnp.bfloat16)
    d_out_ref[...] = lax.dot_general(
        act_ref[0], g_ref[...], ROWS_DIM, preferred_element_type=jnp.float32
    ).astype(jnp.bfloat16)


def combine_kernel(ret_ref, pick_ref, gate_ref, cot_ref, mixed_ref, d_tok_ref, d_gate_ref):
    count = cot_ref.shape[0]
    rows = pick_ref.shape[1]
    found = None
    for first in range(0, ret_ref.shape[0], rows):
        part = jnp.dot(
            pick_ref[...], ret_ref[first:first + rows, :], preferred_element_type=jnp.float32
        )
        found = part if found is None else found + part
    o_0, o_1 = found[:count], found[count:2 * count]
    mixed_ref[...] = (gate_ref[:, 0:1] * o_0 + gate_ref[:, 1:2] * o_1).astype(jnp.bfloat16)
    d_tok_ref[...] = found[2 * count:].astype(jnp.bfloat16)
    cot = cot_ref[...].astype(jnp.float32)
    d_0 = jnp.sum(cot * o_0, axis=1, keepdims=True)
    d_1 = jnp.sum(cot * o_1, axis=1, keepdims=True)
    lane = lax.broadcasted_iota(jnp.int32, (count, 8), 1)
    both = jnp.where(lane == 0, d_0, jnp.where(lane == 1, d_1, 0.0))
    d_gate_ref[...] = jnp.transpose(both, (1, 0))[0:2, :]


def params():
    return pltpu.CompilerParams(vmem_limit_bytes=VMEM_BYTES)


def chunk_of(hidden, want):
    return max(size for size in range(128, want + 1, 128) if hidden % size == 0)


def per_device(tokens, expert_ids, priority, gates, w_in, w_out, cotangent):
    count, width = tokens.shape
    repl = lax.axis_size("expert") // EXPERTS
    slots = EXPERTS * PAIR
    hidden = w_in.shape[2]
    ids_t = jnp.transpose(expert_ids, (1, 0))
    gates_t = jnp.transpose(gates, (1, 0))
    send = pl.pallas_call(
        dispatch_kernel,
        out_shape=jax.ShapeDtypeStruct((slots, width), jnp.bfloat16),
        compiler_params=params(),
        name="dispatch",
    )(ids_t, priority, gates_t, tokens, cotangent)
    pick, gate_cols = pl.pallas_call(
        tables_kernel,
        out_shape=(
            jax.ShapeDtypeStruct((3 * count, slots), jnp.bfloat16),
            jax.ShapeDtypeStruct((count, 8), jnp.float32),
        ),
        compiler_params=params(),
        name="tables",
    )(ids_t, priority, gates_t)
    send = jnp.tile(send.reshape(EXPERTS, PAIR, width), (repl, 1, 1))
    recv = lax.all_to_all(send, "expert", split_axis=0, concat_axis=0, tiled=True)
    rows = recv.shape[0] * PAIR
    recv = recv.reshape(rows, width)
    half = rows // 2
    chunk = chunk_of(hidden, 512)
    steps = hidden // chunk
    vmem = pl.BlockSpec(memory_space=pltpu.VMEM)
    hbm = pl.BlockSpec(memory_space=pl.ANY)
    low = jnp.bfloat16
    ret, x_rows, g_rows, act, d_pre = pl.pallas_call(
        functools.partial(forward_kernel, steps),
        out_shape=(
            jax.ShapeDtypeStruct((rows, width), low),
            jax.ShapeDtypeStruct((half, width), low),
            jax.ShapeDtypeStruct((half, width), low),
            jax.ShapeDtypeStruct((steps, half, chunk), low),
            jax.ShapeDtypeStruct((steps, half, chunk), low),
        ),
        in_specs=[vmem, hbm, hbm],
        out_specs=(vmem,) * 5,
        scratch_shapes=[
            pltpu.VMEM((steps, width, chunk), low),
            pltpu.VMEM((steps, chunk, width), low),
            pltpu.VMEM((half, width), jnp.float32),
            pltpu.VMEM((half, width), jnp.float32),
            pltpu.SemaphoreType.DMA((steps,)),
            pltpu.SemaphoreType.DMA((steps,)),
        ],
        compiler_params=params(),
        cost_estimate=pl.CostEstimate(
            flops=8 * half * width * hidden,
            bytes_accessed=4 * width * hidden,
            transcendentals=half * hidden,
        ),
        name="forward",
    )(recv, w_in[0], w_out[0])
    ret = lax.all_to_all(
        ret.reshape(rows // PAIR, PAIR, width), "expert", split_axis=0, concat_axis=0, tiled=True
    ).reshape(rows, width)
    whole = lambda i: (0, 0)
    d_w_in, d_w_out = pl.pallas_call(
        grads_kernel,
        grid=(steps,),
        out_shape=(
            jax.ShapeDtypeStruct((width, hidden), low),
            jax.ShapeDtypeStruct((hidden, width), low),
        ),
        in_specs=[
            pl.BlockSpec((half, width), whole),
            pl.BlockSpec((half, width), whole),
            pl.BlockSpec((1, half, chunk), lambda i: (i, 0, 0)),
            pl.BlockSpec((1, half, chunk), lambda i: (i, 0, 0)),
        ],
        out_specs=(
            pl.BlockSpec((width, chunk), lambda i: (0, i)),
            pl.BlockSpec((chunk, width), lambda i: (i, 0)),
        ),
        compiler_params=params(),
        cost_estimate=pl.CostEstimate(
            flops=4 * half * width * hidden,
            bytes_accessed=4 * width * hidden,
            transcendentals=0,
        ),
        name="grads",
    )(x_rows, g_rows, act, d_pre)
    mixed, d_tokens, d_gates_t = pl.pallas_call(
        combine_kernel,
        out_shape=(
            jax.ShapeDtypeStruct((count, width), low),
            jax.ShapeDtypeStruct((count, width), low),
            jax.ShapeDtypeStruct((2, count), jnp.float32),
        ),
        compiler_params=params(),
        name="combine",
    )(ret, pick, gate_cols, cotangent)
    return (mixed, d_tokens, jnp.transpose(d_gates_t, (1, 0)), d_w_in[None], d_w_out[None])


def solution(mesh):
    rows = P(("groups", "expert"), None)
    return jax.shard_map(
        per_device,
        mesh=mesh,
        in_specs=(rows, rows, rows, rows, P("expert", None, None), P("expert", None, None), rows),
        out_specs=(
            rows,
            rows,
            rows,
            P(("groups", "expert"), None, None),
            P(("groups", "expert"), None, None),
        ),
        check_vma=False,
    )
```

```python
import functools
import math

import jax
import jax.numpy as jnp
from jax import lax
from jax.experimental import pallas as pl
from jax.experimental.pallas import tpu as pltpu
from jax.sharding import PartitionSpec as P

EXPERTS = 16
CAP = 4
PAIR = 2 * CAP
VMEM_BYTES = 60 * 1024 * 1024
ROWS_DIM = (((0,), (0,)), ((), ()))
LAST_DIM = (((1,), (1,)), ((), ()))


def gelu_parts(value):
    coef = math.sqrt(2.0 / math.pi)
    square = value * value
    hyper = jnp.tanh(coef * value * (1.0 + 0.044715 * square))
    half = 0.5 * (1.0 + hyper)
    slope = half + 0.5 * value * (1.0 - hyper * hyper) * coef * (1.0 + 3.0 * 0.044715 * square)
    return (value * half, slope)


def place_rows(ids_t, prio):
    count = ids_t.shape[1]
    first = ids_t[0:1, :]
    second = ids_t[1:2, :]
    stack = jnp.concatenate([first, second, prio, jnp.zeros((5, count), jnp.int32)], axis=0)
    columns = jnp.transpose(stack.astype(jnp.float32), (1, 0)).astype(jnp.int32)
    first_c, second_c, prio_c = columns[:, 0:1], columns[:, 1:2], columns[:, 2:3]
    ahead = prio_c < prio
    one = jnp.float32(1.0)
    zero = jnp.float32(0.0)
    slot_0 = jnp.sum(jnp.where((first_c == first) & ahead, one, zero), axis=0, keepdims=True)
    slot_1 = jnp.sum(
        jnp.where((first_c == second) | ((second_c == second) & ahead), one, zero),
        axis=0,
        keepdims=True,
    )
    slot_0 = slot_0.astype(jnp.int32)
    slot_1 = slot_1.astype(jnp.int32)
    place_0 = jnp.where(slot_0 < CAP, first * CAP + slot_0, -1)
    place_1 = jnp.where(slot_1 < CAP, second * CAP + slot_1, -1)
    return place_0, place_1


def row_slots(count, pairwise):
    row = lax.broadcasted_iota(jnp.int32, (EXPERTS * PAIR, count), 0)
    block = row // PAIR
    if pairwise:
        block = block ^ lax.axis_index("expert")
    return block * CAP + row % CAP, row % PAIR < CAP


def joined(refs):
    if len(refs) == 1:
        return refs[0][...]
    return jnp.concatenate([ref[...].astype(jnp.float32) for ref in refs], axis=0).astype(
        jnp.bfloat16
    )


def store_blocks(refs, rows):
    depth = refs[0].shape[0]
    for block, ref in enumerate(refs):
        ref[...] = rows[block * depth:(block + 1) * depth].astype(jnp.bfloat16)


def dispatch_kernel(pairwise, ids_ref, prio_ref, gates_ref, tok_ref, cot_ref, *send_refs):
    place_0, place_1 = place_rows(ids_ref[...], prio_ref[...])
    count = tok_ref.shape[0]
    slot, is_x = row_slots(count, pairwise)
    hit_0 = slot == place_0
    hit_1 = slot == place_1
    hit = jnp.where(hit_0 | hit_1, 1.0, 0.0)
    pick = jnp.concatenate(
        [jnp.where(is_x, hit, 0.0), jnp.where(is_x, 0.0, hit)], axis=1
    ).astype(jnp.bfloat16)
    gate = jnp.where(hit_0, gates_ref[0:1, :], 0.0) + jnp.where(hit_1, gates_ref[1:2, :], 0.0)
    scale = jnp.sum(gate, axis=1, keepdims=True)
    scale = jnp.where(is_x[:, 0:1], 1.0, scale)
    both = jnp.concatenate([tok_ref[...], cot_ref[...]], axis=0)
    found = jnp.dot(pick, both, preferred_element_type=jnp.float32)
    store_blocks(send_refs, found * scale)


def tables(pairwise, ids_ref, prio_ref, gates_ref, pick_ref, gate_ref):
    place_0, place_1 = place_rows(ids_ref[...], prio_ref[...])
    count = place_0.shape[1]
    slot, is_x = row_slots(count, pairwise)
    hit_0 = jnp.where(slot == place_0, 1.0, 0.0)
    hit_1 = jnp.where(slot == place_1, 1.0, 0.0)
    pick_0 = jnp.transpose(jnp.where(is_x, hit_0, 0.0), (1, 0))
    pick_1 = jnp.transpose(jnp.where(is_x, hit_1, 0.0), (1, 0))
    pick_b = jnp.transpose(jnp.where(is_x, 0.0, hit_0 + hit_1), (1, 0))
    pick_ref[...] = jnp.concatenate([pick_0, pick_1, pick_b], axis=0).astype(jnp.bfloat16)
    gates = jnp.concatenate([gates_ref[...], jnp.zeros((6, count), jnp.float32)], axis=0)
    gate_ref[...] = jnp.transpose(gates, (1, 0))


def row_picks(rows):
    half = rows // 2
    out = lax.broadcasted_iota(jnp.int32, (half, rows), 0)
    col = lax.broadcasted_iota(jnp.int32, (half, rows), 1)
    source = out // CAP * PAIR + out % CAP
    x_pick = jnp.where(col == source, 1.0, 0.0).astype(jnp.bfloat16)
    g_pick = jnp.where(col == source + CAP, 1.0, 0.0).astype(jnp.bfloat16)
    return x_pick, g_pick


def forward_kernel(steps, blocks, pairwise, *refs):
    recv_refs, refs = refs[:blocks], refs[blocks:]
    ids_ref, prio_ref, gates_ref, w_in_hbm, w_out_hbm = refs[:5]
    ret_refs, refs = refs[5:5 + blocks], refs[5 + blocks:]
    x_t_ref, g_ref, act_ref, d_pre_ref, pick_ref, gate_ref = refs[:6]
    w_in_ref, w_out_ref, x_ref, out_acc, back_acc, sem_in, sem_out = refs[6:]
    depth = w_in_ref.shape[2]

    def copies(step):
        cols = pl.ds(pl.multiple_of(step * depth, depth), depth)
        return (
            pltpu.make_async_copy(w_in_hbm.at[:, cols], w_in_ref.at[step], sem_in.at[step]),
            pltpu.make_async_copy(w_out_hbm.at[cols, :], w_out_ref.at[step], sem_out.at[step]),
        )

    def begin(step, carry):
        for copy in copies(step):
            copy.start()
        return carry

    lax.fori_loop(0, steps, begin, 0)
    recv = joined(recv_refs)
    x_pick, g_pick = row_picks(recv.shape[0])
    x_rows = jnp.dot(x_pick, recv, preferred_element_type=jnp.float32)
    x_ref[...] = x_rows.astype(jnp.bfloat16)
    x_t_ref[...] = jnp.transpose(x_rows, (1, 0)).astype(jnp.bfloat16)
    g_ref[...] = jnp.dot(g_pick, recv, preferred_element_type=jnp.float32).astype(jnp.bfloat16)
    tables(pairwise, ids_ref, prio_ref, gates_ref, pick_ref, gate_ref)
    out_acc[...] = jnp.zeros_like(out_acc)
    back_acc[...] = jnp.zeros_like(back_acc)

    def front(step):
        for copy in copies(step):
            copy.wait()
        pre = jnp.dot(x_ref[...], w_in_ref[step], preferred_element_type=jnp.float32)
        d_act = jnp.transpose(
            lax.dot_general(
                w_out_ref[step], g_ref[...], LAST_DIM, preferred_element_type=jnp.float32
            ),
            (1, 0),
        )
        value, slope = gelu_parts(pre)
        act_ref[step] = value.astype(jnp.bfloat16)
        d_pre_ref[step] = (d_act * slope).astype(jnp.bfloat16)

    def back(step):
        out_acc[...] += jnp.dot(
            act_ref[step], w_out_ref[step], preferred_element_type=jnp.float32
        )
        back_acc[...] += lax.dot_general(
            w_in_ref[step], d_pre_ref[step], LAST_DIM, preferred_element_type=jnp.float32
        )

    front(0)

    def body(step, carry):
        back(step - 1)
        front(step)
        return carry

    lax.fori_loop(1, steps, body, 0)
    back(steps - 1)
    ret = lax.dot_general(
        x_pick, out_acc[...].astype(jnp.bfloat16), ROWS_DIM, preferred_element_type=jnp.float32
    ) + lax.dot_general(
        g_pick, jnp.transpose(back_acc[...], (1, 0)).astype(jnp.bfloat16), ROWS_DIM, preferred_element_type=jnp.float32
    )
    store_blocks(ret_refs, ret)


def grads_kernel(x_t_ref, g_ref, act_ref, d_pre_ref, d_in_ref, d_out_ref):
    d_in_ref[...] = jnp.dot(
        x_t_ref[...], d_pre_ref[0], preferred_element_type=jnp.float32
    ).astype(jnp.bfloat16)
    d_out_ref[...] = lax.dot_general(
        act_ref[0], g_ref[...], ROWS_DIM, preferred_element_type=jnp.float32
    ).astype(jnp.bfloat16)


def combine_kernel(blocks, *refs):
    pick_ref, gate_ref, cot_ref, mixed_ref, d_tok_ref, d_gate_ref = refs[blocks:]
    count = cot_ref.shape[0]
    rows = pick_ref.shape[1]
    ret = joined(refs[:blocks])
    found = None
    for first in range(0, ret.shape[0], rows):
        part = jnp.dot(
            pick_ref[...], ret[first:first + rows, :], preferred_element_type=jnp.float32
        )
        found = part if found is None else found + part
    o_0, o_1 = found[:count], found[count:2 * count]
    mixed_ref[...] = (gate_ref[:, 0:1] * o_0 + gate_ref[:, 1:2] * o_1).astype(jnp.bfloat16)
    d_tok_ref[...] = found[2 * count:].astype(jnp.bfloat16)
    cot = cot_ref[...].astype(jnp.float32)
    d_0 = jnp.sum(cot * o_0, axis=1, keepdims=True)
    d_1 = jnp.sum(cot * o_1, axis=1, keepdims=True)
    lane = lax.broadcasted_iota(jnp.int32, (count, 8), 1)
    both = jnp.where(lane == 0, d_0, jnp.where(lane == 1, d_1, 0.0))
    d_gate_ref[...] = jnp.transpose(both, (1, 0))[0:2, :]


def params():
    return pltpu.CompilerParams(vmem_limit_bytes=VMEM_BYTES)


def chunk_of(hidden, want):
    return max(size for size in range(128, want + 1, 128) if hidden % size == 0)


def exchange(parts):
    if len(parts) > 1:
        return [parts[0]] + [
            lax.ppermute(part, "expert", [(i, i ^ k) for i in range(len(parts))])
            for k, part in enumerate(parts)
            if k
        ]
    rows, width = parts[0].shape
    moved = lax.all_to_all(
        parts[0].reshape(rows // PAIR, PAIR, width), "expert", split_axis=0, concat_axis=0, tiled=True
    )
    return [moved.reshape(rows, width)]


def per_device(tokens, expert_ids, priority, gates, w_in, w_out, cotangent):
    count, width = tokens.shape
    repl = lax.axis_size("expert") // EXPERTS
    slots = EXPERTS * PAIR
    hidden = w_in.shape[2]
    ids_t = jnp.transpose(expert_ids, (1, 0))
    gates_t = jnp.transpose(gates, (1, 0))
    pairwise = repl == 1
    low = jnp.bfloat16
    parts = EXPERTS if pairwise else 1
    send = pl.pallas_call(
        functools.partial(dispatch_kernel, pairwise),
        out_shape=(jax.ShapeDtypeStruct((slots // parts, width), low),) * parts,
        compiler_params=params(),
        name="dispatch",
    )(ids_t, priority, gates_t, tokens, cotangent)
    if not pairwise:
        send = (jnp.tile(send[0], (repl, 1)),)
    recv = exchange(send)
    rows = slots * repl
    half = rows // 2
    chunk = chunk_of(hidden, 512)
    steps = hidden // chunk
    vmem = pl.BlockSpec(memory_space=pltpu.VMEM)
    hbm = pl.BlockSpec(memory_space=pl.ANY)
    *ret, x_t, g_rows, act, d_pre, pick, gate_cols = pl.pallas_call(
        functools.partial(forward_kernel, steps, parts, pairwise),
        out_shape=(jax.ShapeDtypeStruct((rows // parts, width), low),) * parts
        + (
            jax.ShapeDtypeStruct((width, half), low),
            jax.ShapeDtypeStruct((half, width), low),
            jax.ShapeDtypeStruct((steps, half, chunk), low),
            jax.ShapeDtypeStruct((steps, half, chunk), low),
            jax.ShapeDtypeStruct((3 * count, slots), low),
            jax.ShapeDtypeStruct((count, 8), jnp.float32),
        ),
        in_specs=[vmem] * (parts + 3) + [hbm, hbm],
        out_specs=(vmem,) * (parts + 6),
        scratch_shapes=[
            pltpu.VMEM((steps, width, chunk), low),
            pltpu.VMEM((steps, chunk, width), low),
            pltpu.VMEM((half, width), low),
            pltpu.VMEM((half, width), jnp.float32),
            pltpu.VMEM((width, half), jnp.float32),
            pltpu.SemaphoreType.DMA((steps,)),
            pltpu.SemaphoreType.DMA((steps,)),
        ],
        compiler_params=params(),
        cost_estimate=pl.CostEstimate(
            flops=8 * half * width * hidden,
            bytes_accessed=4 * width * hidden,
            transcendentals=half * hidden,
        ),
        name="forward",
    )(*recv, ids_t, priority, gates_t, w_in[0], w_out[0])
    ret = exchange(ret)
    whole = lambda i: (0, 0)
    d_w_in, d_w_out = pl.pallas_call(
        grads_kernel,
        grid=(steps,),
        out_shape=(
            jax.ShapeDtypeStruct((width, hidden), low),
            jax.ShapeDtypeStruct((hidden, width), low),
        ),
        in_specs=[
            pl.BlockSpec((width, half), whole),
            pl.BlockSpec((half, width), whole),
            pl.BlockSpec((1, half, chunk), lambda i: (i, 0, 0)),
            pl.BlockSpec((1, half, chunk), lambda i: (i, 0, 0)),
        ],
        out_specs=(
            pl.BlockSpec((width, chunk), lambda i: (0, i)),
            pl.BlockSpec((chunk, width), lambda i: (i, 0)),
        ),
        compiler_params=params(),
        cost_estimate=pl.CostEstimate(
            flops=4 * half * width * hidden,
            bytes_accessed=4 * width * hidden,
            transcendentals=0,
        ),
        name="grads",
    )(x_t, g_rows, act, d_pre)
    mixed, d_tokens, d_gates_t = pl.pallas_call(
        functools.partial(combine_kernel, parts),
        out_shape=(
            jax.ShapeDtypeStruct((count, width), low),
            jax.ShapeDtypeStruct((count, width), low),
            jax.ShapeDtypeStruct((2, count), jnp.float32),
        ),
        compiler_params=params(),
        name="combine",
    )(*ret, pick, gate_cols, cotangent)
    return (mixed, d_tokens, jnp.transpose(d_gates_t, (1, 0)), d_w_in[None], d_w_out[None])


def solution(mesh):
    rows = P(("groups", "expert"), None)
    return jax.shard_map(
        per_device,
        mesh=mesh,
        in_specs=(rows, rows, rows, rows, P("expert", None, None), P("expert", None, None), rows),
        out_specs=(
            rows,
            rows,
            rows,
            P(("groups", "expert"), None, None),
            P(("groups", "expert"), None, None),
        ),
        check_vma=False,
    )
```

```python
import functools
import math

import jax
import jax.numpy as jnp
from jax import lax
from jax.experimental import pallas as pl
from jax.experimental.pallas import tpu as pltpu
from jax.sharding import PartitionSpec as P

EXPERTS = 16
CAP = 4
PAIR = 2 * CAP
ROWS_DIM = (((0,), (0,)), ((), ()))
LAST_DIM = (((1,), (1,)), ((), ()))


def gelu_parts(value):
    coef = math.sqrt(2.0 / math.pi)
    square = value * value
    hyper = jnp.tanh(coef * value * (1.0 + 0.044715 * square))
    half = 0.5 * (1.0 + hyper)
    slope = half + 0.5 * value * (1.0 - hyper * hyper) * coef * (1.0 + 3.0 * 0.044715 * square)
    return (value * half, slope)


def place_rows(ids_t, prio):
    count = ids_t.shape[1]
    first = ids_t[0:1, :]
    second = ids_t[1:2, :]
    stack = jnp.concatenate([first, second, prio, jnp.zeros((5, count), jnp.int32)], axis=0)
    columns = jnp.transpose(stack.astype(jnp.float32), (1, 0)).astype(jnp.int32)
    first_c, second_c, prio_c = columns[:, 0:1], columns[:, 1:2], columns[:, 2:3]
    ahead = prio_c < prio
    one = jnp.float32(1.0)
    zero = jnp.float32(0.0)
    slot_0 = jnp.sum(jnp.where((first_c == first) & ahead, one, zero), axis=0, keepdims=True)
    slot_1 = jnp.sum(
        jnp.where((first_c == second) | ((second_c == second) & ahead), one, zero),
        axis=0,
        keepdims=True,
    )
    slot_0 = slot_0.astype(jnp.int32)
    slot_1 = slot_1.astype(jnp.int32)
    place_0 = jnp.where(slot_0 < CAP, first * CAP + slot_0, -1)
    place_1 = jnp.where(slot_1 < CAP, second * CAP + slot_1, -1)
    return place_0, place_1


def dispatch_kernel(ids_ref, prio_ref, gates_ref, tok_ref, cot_ref, send_ref, plan_ref):
    place_0, place_1 = place_rows(ids_ref[...], prio_ref[...])
    count = tok_ref.shape[0]
    rows = EXPERTS * PAIR
    row = lax.broadcasted_iota(jnp.int32, (rows, count), 0)
    slot = row // PAIR * CAP + row % CAP
    is_x = row % PAIR < CAP
    hit_0 = slot == place_0
    hit_1 = slot == place_1
    hit = jnp.where(hit_0 | hit_1, 1.0, 0.0)
    pick = jnp.concatenate(
        [jnp.where(is_x, hit, 0.0), jnp.where(is_x, 0.0, hit)], axis=1
    ).astype(jnp.bfloat16)
    gate = jnp.where(hit_0, gates_ref[0:1, :], 0.0) + jnp.where(hit_1, gates_ref[1:2, :], 0.0)
    scale = jnp.sum(gate, axis=1, keepdims=True)
    scale = jnp.where(is_x[:, 0:1], 1.0, scale)
    both = jnp.concatenate([tok_ref[...], cot_ref[...]], axis=0)
    found = jnp.dot(pick, both, preferred_element_type=jnp.float32)
    send_ref[...] = (found * scale).astype(jnp.bfloat16)
    plan_ref[...] = jnp.concatenate(
        [
            place_0.astype(jnp.float32),
            place_1.astype(jnp.float32),
            gates_ref[...],
            jnp.zeros((4, count), jnp.float32),
        ],
        axis=0,
    )


def tables(plan_ref, pick_ref, gate_ref):
    place_0 = plan_ref[0:1, :].astype(jnp.int32)
    place_1 = plan_ref[1:2, :].astype(jnp.int32)
    count = place_0.shape[1]
    rows = EXPERTS * PAIR
    row = lax.broadcasted_iota(jnp.int32, (rows, count), 0)
    slot = row // PAIR * CAP + row % CAP
    is_x = row % PAIR < CAP
    hit_0 = jnp.where(slot == place_0, 1.0, 0.0)
    hit_1 = jnp.where(slot == place_1, 1.0, 0.0)
    pick_0 = jnp.transpose(jnp.where(is_x, hit_0, 0.0), (1, 0))
    pick_1 = jnp.transpose(jnp.where(is_x, hit_1, 0.0), (1, 0))
    pick_b = jnp.transpose(jnp.where(is_x, 0.0, hit_0 + hit_1), (1, 0))
    pick_ref[...] = jnp.concatenate([pick_0, pick_1, pick_b], axis=0).astype(jnp.bfloat16)
    gate_ref[...] = jnp.transpose(plan_ref[...], (1, 0))


def row_picks(rows):
    half = rows // 2
    out = lax.broadcasted_iota(jnp.int32, (half, rows), 0)
    col = lax.broadcasted_iota(jnp.int32, (half, rows), 1)
    source = out // CAP * PAIR + out % CAP
    x_pick = jnp.where(col == source, 1.0, 0.0).astype(jnp.bfloat16)
    g_pick = jnp.where(col == source + CAP, 1.0, 0.0).astype(jnp.bfloat16)
    return x_pick, g_pick


def forward_kernel(
    steps, recv_ref, plan_ref, w_in_hbm, w_out_hbm,
    ret_ref, x_t_ref, g_ref, act_ref, d_pre_ref, pick_ref, gate_ref,
    w_in_ref, w_out_ref, x_ref, out_acc, back_acc, sem_in, sem_out,
):
    depth = w_in_ref.shape[2]

    def copies(step):
        cols = pl.ds(pl.multiple_of(step * depth, depth), depth)
        return (
            pltpu.make_async_copy(w_in_hbm.at[:, cols], w_in_ref.at[step], sem_in.at[step]),
            pltpu.make_async_copy(w_out_hbm.at[cols, :], w_out_ref.at[step], sem_out.at[step]),
        )

    def begin(step, carry):
        for copy in copies(step):
            copy.start()
        return carry

    lax.fori_loop(0, steps, begin, 0)
    recv = recv_ref[...]
    x_pick, g_pick = row_picks(recv.shape[0])
    x_rows = jnp.dot(x_pick, recv, preferred_element_type=jnp.float32)
    x_ref[...] = x_rows.astype(jnp.bfloat16)
    x_t_ref[...] = jnp.transpose(x_rows, (1, 0)).astype(jnp.bfloat16)
    g_ref[...] = jnp.dot(g_pick, recv, preferred_element_type=jnp.float32).astype(jnp.bfloat16)
    tables(plan_ref, pick_ref, gate_ref)
    out_acc[...] = jnp.zeros_like(out_acc)
    back_acc[...] = jnp.zeros_like(back_acc)

    def front(step):
        pre = jnp.dot(x_ref[...], w_in_ref[step], preferred_element_type=jnp.float32)
        d_act = lax.dot_general(
            g_ref[...], w_out_ref[step], LAST_DIM, preferred_element_type=jnp.float32
        )
        return pre, d_act

    def middle(step, pre, d_act):
        value, slope = gelu_parts(pre)
        act_ref[step] = value.astype(jnp.bfloat16)
        d_pre_ref[step] = (d_act * slope).astype(jnp.bfloat16)

    def back(step, act, d_pre):
        out_acc[...] += jnp.dot(act, w_out_ref[step], preferred_element_type=jnp.float32)
        back_acc[...] += lax.dot_general(
            d_pre, w_in_ref[step], LAST_DIM, preferred_element_type=jnp.float32
        )

    def arrive(step):
        for copy in copies(step):
            copy.wait()

    arrive(0)
    middle(0, *front(0))

    def body(step, carry):
        arrive(step)
        act, d_pre = act_ref[step - 1], d_pre_ref[step - 1]
        found = front(step)
        back(step - 1, act, d_pre)
        middle(step, *found)
        return carry

    lax.fori_loop(1, steps, body, 0)
    back(steps - 1, act_ref[steps - 1], d_pre_ref[steps - 1])
    ret = lax.dot_general(
        x_pick, out_acc[...].astype(jnp.bfloat16), ROWS_DIM, preferred_element_type=jnp.float32
    ) + lax.dot_general(
        g_pick, back_acc[...].astype(jnp.bfloat16), ROWS_DIM, preferred_element_type=jnp.float32
    )
    ret_ref[...] = ret.astype(jnp.bfloat16)


def grads_kernel(steps, x_t_ref, g_ref, act_ref, d_pre_ref, d_in_ref, d_out_ref):
    depth = act_ref.shape[2]
    piece = 128

    for step in range(steps):
        d_in_ref[:, step * depth:(step + 1) * depth] = jnp.dot(
            x_t_ref[...], d_pre_ref[step], preferred_element_type=jnp.float32
        ).astype(jnp.bfloat16)

    @pl.when(pl.program_id(0) < steps)
    def _():
        for first in range(0, depth, piece):
            d_out_ref[first:first + piece, :] = lax.dot_general(
                act_ref[0, :, first:first + piece],
                g_ref[...],
                ROWS_DIM,
                preferred_element_type=jnp.float32,
            ).astype(jnp.bfloat16)


def combine_kernel(ret_ref, pick_ref, gate_ref, cot_ref, mixed_ref, d_tok_ref, d_gate_ref):
    count = cot_ref.shape[0]
    rows = pick_ref.shape[1]
    found = None
    for first in range(0, ret_ref.shape[0], rows):
        part = jnp.dot(
            pick_ref[...], ret_ref[first:first + rows, :], preferred_element_type=jnp.float32
        )
        found = part if found is None else found + part
    o_0, o_1 = found[:count], found[count:2 * count]
    mixed_ref[...] = (gate_ref[:, 2:3] * o_0 + gate_ref[:, 3:4] * o_1).astype(jnp.bfloat16)
    d_tok_ref[...] = found[2 * count:].astype(jnp.bfloat16)
    cot = cot_ref[...].astype(jnp.float32)
    d_0 = jnp.sum(cot * o_0, axis=1, keepdims=True)
    d_1 = jnp.sum(cot * o_1, axis=1, keepdims=True)
    lane = lax.broadcasted_iota(jnp.int32, (count, 8), 1)
    both = jnp.where(lane == 0, d_0, jnp.where(lane == 1, d_1, 0.0))
    d_gate_ref[...] = jnp.transpose(both, (1, 0))[0:2, :]


def params(mib):
    return pltpu.CompilerParams(vmem_limit_bytes=mib * 1024 * 1024)


def chunk_of(hidden, want):
    return max(size for size in range(128, want + 1, 128) if hidden % size == 0)


def per_device(tokens, expert_ids, priority, gates, w_in, w_out, cotangent):
    count, width = tokens.shape
    repl = lax.axis_size("expert") // EXPERTS
    slots = EXPERTS * PAIR
    hidden = w_in.shape[2]
    ids_t = jnp.transpose(expert_ids, (1, 0))
    gates_t = jnp.transpose(gates, (1, 0))
    send, plan = pl.pallas_call(
        dispatch_kernel,
        out_shape=(
            jax.ShapeDtypeStruct((slots, width), jnp.bfloat16),
            jax.ShapeDtypeStruct((8, count), jnp.float32),
        ),
        compiler_params=params(60),
        name="dispatch",
    )(ids_t, priority, gates_t, tokens, cotangent)
    send = jnp.tile(send.reshape(EXPERTS, PAIR, width), (repl, 1, 1))
    recv = lax.all_to_all(send, "expert", split_axis=0, concat_axis=0, tiled=True)
    rows = recv.shape[0] * PAIR
    recv = recv.reshape(rows, width)
    half = rows // 2
    chunk = chunk_of(hidden, 512)
    steps = hidden // chunk
    vmem = pl.BlockSpec(memory_space=pltpu.VMEM)
    hbm = pl.BlockSpec(memory_space=pl.ANY)
    low = jnp.bfloat16
    ret, x_t, g_rows, act, d_pre, pick, gate_cols = pl.pallas_call(
        functools.partial(forward_kernel, steps),
        out_shape=(
            jax.ShapeDtypeStruct((rows, width), low),
            jax.ShapeDtypeStruct((width, half), low),
            jax.ShapeDtypeStruct((half, width), low),
            jax.ShapeDtypeStruct((steps, half, chunk), low),
            jax.ShapeDtypeStruct((steps, half, chunk), low),
            jax.ShapeDtypeStruct((3 * count, slots), low),
            jax.ShapeDtypeStruct((count, 8), jnp.float32),
        ),
        in_specs=[vmem] * 2 + [hbm] * 2,
        out_specs=(vmem,) * 7,
        scratch_shapes=[
            pltpu.VMEM((steps, width, chunk), low),
            pltpu.VMEM((steps, chunk, width), low),
            pltpu.VMEM((half, width), low),
            pltpu.VMEM((half, width), jnp.float32),
            pltpu.VMEM((half, width), jnp.float32),
            pltpu.SemaphoreType.DMA((steps,)),
            pltpu.SemaphoreType.DMA((steps,)),
        ],
        compiler_params=params(50),
        cost_estimate=pl.CostEstimate(
            flops=8 * half * width * hidden,
            bytes_accessed=4 * width * hidden,
            transcendentals=half * hidden,
        ),
        name="forward",
    )(recv, plan, w_in[0], w_out[0])
    ret = lax.all_to_all(
        ret.reshape(rows // PAIR, PAIR, width), "expert", split_axis=0, concat_axis=0, tiled=True
    ).reshape(rows, width)
    strip = 128
    d_w_in, d_w_out = pl.pallas_call(
        functools.partial(grads_kernel, steps),
        grid=(width // strip,),
        out_shape=(
            jax.ShapeDtypeStruct((width, hidden), low),
            jax.ShapeDtypeStruct((hidden, width), low),
        ),
        in_specs=[
            pl.BlockSpec((strip, half), lambda i: (i, 0)),
            pl.BlockSpec((half, width), lambda i: (0, 0)),
            pl.BlockSpec((1, half, chunk), lambda i: (jnp.minimum(i, steps - 1), 0, 0)),
            pl.BlockSpec((steps, half, chunk), lambda i: (0, 0, 0)),
        ],
        out_specs=(
            pl.BlockSpec((strip, hidden), lambda i: (i, 0)),
            pl.BlockSpec((chunk, width), lambda i: (jnp.minimum(i, steps - 1), 0)),
        ),
        compiler_params=params(24),
        cost_estimate=pl.CostEstimate(
            flops=4 * half * width * hidden,
            bytes_accessed=4 * width * hidden,
            transcendentals=0,
        ),
        name="grads",
    )(x_t, g_rows, act, d_pre)
    mixed, d_tokens, d_gates_t = pl.pallas_call(
        combine_kernel,
        out_shape=(
            jax.ShapeDtypeStruct((count, width), low),
            jax.ShapeDtypeStruct((count, width), low),
            jax.ShapeDtypeStruct((2, count), jnp.float32),
        ),
        compiler_params=params(12),
        name="combine",
    )(ret, pick, gate_cols, cotangent)
    return (mixed, d_tokens, jnp.transpose(d_gates_t, (1, 0)), d_w_in[None], d_w_out[None])


def solution(mesh):
    rows = P(("groups", "expert"), None)
    return jax.shard_map(
        per_device,
        mesh=mesh,
        in_specs=(rows, rows, rows, rows, P("expert", None, None), P("expert", None, None), rows),
        out_specs=(
            rows,
            rows,
            rows,
            P(("groups", "expert"), None, None),
            P(("groups", "expert"), None, None),
        ),
        check_vma=False,
    )
```

```python
import functools
import math

import jax
import jax.numpy as jnp
from jax import lax
from jax.experimental import pallas as pl
from jax.experimental.pallas import tpu as pltpu
from jax.sharding import PartitionSpec as P

EXPERTS = 16
CAP = 4
PAIR = 2 * CAP
AHEAD = 2
ROWS_DIM = (((0,), (0,)), ((), ()))
LAST_DIM = (((1,), (1,)), ((), ()))


def gelu_parts(value):
    coef = math.sqrt(2.0 / math.pi)
    square = value * value
    hyper = jnp.tanh(coef * value * (1.0 + 0.044715 * square))
    half = 0.5 * (1.0 + hyper)
    slope = half + 0.5 * value * (1.0 - hyper * hyper) * coef * (1.0 + 3.0 * 0.044715 * square)
    return (value * half, slope)


def place_rows(ids_t, prio):
    count = ids_t.shape[1]
    first = ids_t[0:1, :]
    second = ids_t[1:2, :]
    stack = jnp.concatenate([first, second, prio, jnp.zeros((5, count), jnp.int32)], axis=0)
    columns = jnp.transpose(stack.astype(jnp.float32), (1, 0)).astype(jnp.int32)
    first_c, second_c, prio_c = columns[:, 0:1], columns[:, 1:2], columns[:, 2:3]
    ahead = prio_c < prio
    one = jnp.float32(1.0)
    zero = jnp.float32(0.0)
    slot_0 = jnp.sum(jnp.where((first_c == first) & ahead, one, zero), axis=0, keepdims=True)
    slot_1 = jnp.sum(
        jnp.where((first_c == second) | ((second_c == second) & ahead), one, zero),
        axis=0,
        keepdims=True,
    )
    slot_0 = slot_0.astype(jnp.int32)
    slot_1 = slot_1.astype(jnp.int32)
    place_0 = jnp.where(slot_0 < CAP, first * CAP + slot_0, -1)
    place_1 = jnp.where(slot_1 < CAP, second * CAP + slot_1, -1)
    return place_0, place_1


def dispatch_kernel(ids_ref, prio_ref, gates_ref, tok_ref, cot_ref, send_ref, plan_ref):
    place_0, place_1 = place_rows(ids_ref[...], prio_ref[...])
    count = tok_ref.shape[0]
    rows = EXPERTS * PAIR
    row = lax.broadcasted_iota(jnp.int32, (rows, count), 0)
    slot = row // PAIR * CAP + row % CAP
    is_x = row % PAIR < CAP
    hit_0 = slot == place_0
    hit_1 = slot == place_1
    hit = jnp.where(hit_0 | hit_1, 1.0, 0.0)
    pick = jnp.concatenate(
        [jnp.where(is_x, hit, 0.0), jnp.where(is_x, 0.0, hit)], axis=1
    ).astype(jnp.bfloat16)
    gate = jnp.where(hit_0, gates_ref[0:1, :], 0.0) + jnp.where(hit_1, gates_ref[1:2, :], 0.0)
    scale = jnp.sum(gate, axis=1, keepdims=True)
    scale = jnp.where(is_x[:, 0:1], 1.0, scale)
    both = jnp.concatenate([tok_ref[...], cot_ref[...]], axis=0)
    found = jnp.dot(pick, both, preferred_element_type=jnp.float32)
    send_ref[...] = (found * scale).astype(jnp.bfloat16)
    plan_ref[...] = jnp.concatenate(
        [
            place_0.astype(jnp.float32),
            place_1.astype(jnp.float32),
            gates_ref[...],
            jnp.zeros((4, count), jnp.float32),
        ],
        axis=0,
    )


def tables(plan_ref, pick_ref, gate_ref):
    place_0 = plan_ref[0:1, :].astype(jnp.int32)
    place_1 = plan_ref[1:2, :].astype(jnp.int32)
    count = place_0.shape[1]
    rows = EXPERTS * PAIR
    row = lax.broadcasted_iota(jnp.int32, (rows, count), 0)
    slot = row // PAIR * CAP + row % CAP
    is_x = row % PAIR < CAP
    hit_0 = jnp.where(slot == place_0, 1.0, 0.0)
    hit_1 = jnp.where(slot == place_1, 1.0, 0.0)
    pick_0 = jnp.transpose(jnp.where(is_x, hit_0, 0.0), (1, 0))
    pick_1 = jnp.transpose(jnp.where(is_x, hit_1, 0.0), (1, 0))
    pick_b = jnp.transpose(jnp.where(is_x, 0.0, hit_0 + hit_1), (1, 0))
    pick_ref[...] = jnp.concatenate([pick_0, pick_1, pick_b], axis=0).astype(jnp.bfloat16)
    gate_ref[...] = jnp.transpose(plan_ref[...], (1, 0))


def row_picks(rows):
    half = rows // 2
    out = lax.broadcasted_iota(jnp.int32, (half, rows), 0)
    col = lax.broadcasted_iota(jnp.int32, (half, rows), 1)
    source = out // CAP * PAIR + out % CAP
    x_pick = jnp.where(col == source, 1.0, 0.0).astype(jnp.bfloat16)
    g_pick = jnp.where(col == source + CAP, 1.0, 0.0).astype(jnp.bfloat16)
    return x_pick, g_pick


def forward_kernel(
    steps, recv_ref, plan_ref, w_in_hbm, w_out_hbm,
    ret_ref, x_t_ref, g_ref, act_ref, d_pre_ref, pick_ref, gate_ref,
    w_in_ref, w_out_ref, x_ref, out_acc, back_acc, sem_in, sem_out,
):
    depth = w_in_ref.shape[2]

    def copies(step):
        cols = pl.ds(pl.multiple_of(step * depth, depth), depth)
        return (
            pltpu.make_async_copy(w_in_hbm.at[:, cols], w_in_ref.at[step], sem_in.at[step]),
            pltpu.make_async_copy(w_out_hbm.at[cols, :], w_out_ref.at[step], sem_out.at[step]),
        )

    def begin(step):
        for copy in copies(step):
            copy.start()

    for step in range(min(AHEAD, steps)):
        begin(step)
    recv = recv_ref[...]
    x_pick, g_pick = row_picks(recv.shape[0])
    x_rows = jnp.dot(x_pick, recv, preferred_element_type=jnp.float32)
    x_ref[...] = x_rows.astype(jnp.bfloat16)
    x_t_ref[...] = jnp.transpose(x_rows, (1, 0)).astype(jnp.bfloat16)
    g_ref[...] = jnp.dot(g_pick, recv, preferred_element_type=jnp.float32).astype(jnp.bfloat16)
    tables(plan_ref, pick_ref, gate_ref)
    out_acc[...] = jnp.zeros_like(out_acc)
    back_acc[...] = jnp.zeros_like(back_acc)

    def front(step):
        pre = jnp.dot(x_ref[...], w_in_ref[step], preferred_element_type=jnp.float32)
        d_act = lax.dot_general(
            g_ref[...], w_out_ref[step], LAST_DIM, preferred_element_type=jnp.float32
        )
        return pre, d_act

    def middle(step, pre, d_act):
        value, slope = gelu_parts(pre)
        act_ref[step] = value.astype(jnp.bfloat16)
        d_pre_ref[step] = (d_act * slope).astype(jnp.bfloat16)

    def back(step, act, d_pre):
        out_acc[...] += jnp.dot(act, w_out_ref[step], preferred_element_type=jnp.float32)
        back_acc[...] += lax.dot_general(
            d_pre, w_in_ref[step], LAST_DIM, preferred_element_type=jnp.float32
        )

    def arrive(step):
        for copy in copies(step):
            copy.wait()

    arrive(0)
    if steps > AHEAD:
        begin(AHEAD)
    middle(0, *front(0))

    def body(step, carry):
        arrive(step)

        @pl.when(step + AHEAD < steps)
        def _():
            begin(step + AHEAD)

        act, d_pre = act_ref[step - 1], d_pre_ref[step - 1]
        found = front(step)
        back(step - 1, act, d_pre)
        middle(step, *found)
        return carry

    lax.fori_loop(1, steps, body, 0)
    back(steps - 1, act_ref[steps - 1], d_pre_ref[steps - 1])
    ret = lax.dot_general(
        x_pick, out_acc[...].astype(jnp.bfloat16), ROWS_DIM, preferred_element_type=jnp.float32
    ) + lax.dot_general(
        g_pick, back_acc[...].astype(jnp.bfloat16), ROWS_DIM, preferred_element_type=jnp.float32
    )
    ret_ref[...] = ret.astype(jnp.bfloat16)


def product(out_ref, left, right, tall, wide):
    rows, cols = out_ref.shape
    for col in range(0, cols, wide):
        col_end = min(col + wide, cols)
        for row in range(0, rows, tall):
            row_end = min(row + tall, rows)
            out_ref[row:row_end, col:col_end] = jnp.dot(
                left[row:row_end], right[:, col:col_end], preferred_element_type=jnp.float32
            ).astype(jnp.bfloat16)


def grads_kernel(x_t_ref, g_ref, act_ref, d_pre_ref, d_in_ref, d_out_ref):
    act_t = jnp.transpose(act_ref[0].astype(jnp.float32), (1, 0)).astype(jnp.bfloat16)
    product(d_in_ref, x_t_ref[...], d_pre_ref[0], 208, 256)
    product(d_out_ref, act_t, g_ref[...], 256, 256)


def combine_kernel(ret_ref, pick_ref, gate_ref, cot_ref, mixed_ref, d_tok_ref, d_gate_ref):
    count = cot_ref.shape[0]
    rows = pick_ref.shape[1]
    found = None
    for first in range(0, ret_ref.shape[0], rows):
        part = jnp.dot(
            pick_ref[...], ret_ref[first:first + rows, :], preferred_element_type=jnp.float32
        )
        found = part if found is None else found + part
    o_0, o_1 = found[:count], found[count:2 * count]
    mixed_ref[...] = (gate_ref[:, 2:3] * o_0 + gate_ref[:, 3:4] * o_1).astype(jnp.bfloat16)
    d_tok_ref[...] = found[2 * count:].astype(jnp.bfloat16)
    cot = cot_ref[...].astype(jnp.float32)
    d_0 = jnp.sum(cot * o_0, axis=1, keepdims=True)
    d_1 = jnp.sum(cot * o_1, axis=1, keepdims=True)
    lane = lax.broadcasted_iota(jnp.int32, (count, 8), 1)
    both = jnp.where(lane == 0, d_0, jnp.where(lane == 1, d_1, 0.0))
    d_gate_ref[...] = jnp.transpose(both, (1, 0))[0:2, :]


def params(mib):
    return pltpu.CompilerParams(vmem_limit_bytes=mib * 1024 * 1024)


def chunk_of(hidden, want):
    return max(size for size in range(128, want + 1, 128) if hidden % size == 0)


def per_device(tokens, expert_ids, priority, gates, w_in, w_out, cotangent):
    count, width = tokens.shape
    repl = lax.axis_size("expert") // EXPERTS
    slots = EXPERTS * PAIR
    hidden = w_in.shape[2]
    ids_t = jnp.transpose(expert_ids, (1, 0))
    gates_t = jnp.transpose(gates, (1, 0))
    send, plan = pl.pallas_call(
        dispatch_kernel,
        out_shape=(
            jax.ShapeDtypeStruct((slots, width), jnp.bfloat16),
            pltpu.VMEM((8, count), jnp.float32),
        ),
        compiler_params=params(60),
        name="dispatch",
    )(ids_t, priority, gates_t, tokens, cotangent)
    send = jnp.tile(send.reshape(EXPERTS, PAIR, width), (repl, 1, 1))
    recv = lax.all_to_all(send, "expert", split_axis=0, concat_axis=0, tiled=True)
    rows = recv.shape[0] * PAIR
    recv = recv.reshape(rows, width)
    half = rows // 2
    chunk = chunk_of(hidden, 512)
    steps = hidden // chunk
    vmem = pl.BlockSpec(memory_space=pltpu.VMEM)
    hbm = pl.BlockSpec(memory_space=pl.ANY)
    low = jnp.bfloat16
    ret, x_t, g_rows, act, d_pre, pick, gate_cols = pl.pallas_call(
        functools.partial(forward_kernel, steps),
        out_shape=(
            jax.ShapeDtypeStruct((rows, width), low),
            jax.ShapeDtypeStruct((width, half), low),
            jax.ShapeDtypeStruct((half, width), low),
            jax.ShapeDtypeStruct((steps, half, chunk), low),
            jax.ShapeDtypeStruct((steps, half, chunk), low),
            jax.ShapeDtypeStruct((3 * count, slots), low),
            jax.ShapeDtypeStruct((count, 8), jnp.float32),
        ),
        in_specs=[vmem] * 2 + [hbm] * 2,
        out_specs=(vmem,) * 7,
        scratch_shapes=[
            pltpu.VMEM((steps, width, chunk), low),
            pltpu.VMEM((steps, chunk, width), low),
            pltpu.VMEM((half, width), low),
            pltpu.VMEM((half, width), jnp.float32),
            pltpu.VMEM((half, width), jnp.float32),
            pltpu.SemaphoreType.DMA((steps,)),
            pltpu.SemaphoreType.DMA((steps,)),
        ],
        compiler_params=params(50),
        cost_estimate=pl.CostEstimate(
            flops=8 * half * width * hidden,
            bytes_accessed=4 * width * hidden,
            transcendentals=half * hidden,
        ),
        name="forward",
    )(recv, plan, w_in[0], w_out[0])
    ret = lax.all_to_all(
        ret.reshape(rows // PAIR, PAIR, width), "expert", split_axis=0, concat_axis=0, tiled=True
    ).reshape(rows, width)
    d_w_in, d_w_out = pl.pallas_call(
        grads_kernel,
        grid=(steps,),
        out_shape=(
            jax.ShapeDtypeStruct((width, hidden), low),
            jax.ShapeDtypeStruct((hidden, width), low),
        ),
        in_specs=[
            pl.BlockSpec((width, half), lambda i: (0, 0)),
            pl.BlockSpec((half, width), lambda i: (0, 0)),
            pl.BlockSpec((1, half, chunk), lambda i: (i, 0, 0)),
            pl.BlockSpec((1, half, chunk), lambda i: (i, 0, 0)),
        ],
        out_specs=(
            pl.BlockSpec((width, chunk), lambda i: (0, i)),
            pl.BlockSpec((chunk, width), lambda i: (i, 0)),
        ),
        compiler_params=params(24),
        cost_estimate=pl.CostEstimate(
            flops=4 * half * width * hidden,
            bytes_accessed=4 * width * hidden,
            transcendentals=0,
        ),
        name="grads",
    )(x_t, g_rows, act, d_pre)
    mixed, d_tokens, d_gates_t = pl.pallas_call(
        combine_kernel,
        out_shape=(
            jax.ShapeDtypeStruct((count, width), low),
            jax.ShapeDtypeStruct((count, width), low),
            jax.ShapeDtypeStruct((2, count), jnp.float32),
        ),
        compiler_params=params(12),
        name="combine",
    )(ret, pick, gate_cols, cotangent)
    return (mixed, d_tokens, jnp.transpose(d_gates_t, (1, 0)), d_w_in[None], d_w_out[None])


def solution(mesh):
    rows = P(("groups", "expert"), None)
    return jax.shard_map(
        per_device,
        mesh=mesh,
        in_specs=(rows, rows, rows, rows, P("expert", None, None), P("expert", None, None), rows),
        out_specs=(
            rows,
            rows,
            rows,
            P(("groups", "expert"), None, None),
            P(("groups", "expert"), None, None),
        ),
        check_vma=False,
    )
```

```python
import functools
import math

import jax
import jax.numpy as jnp
from jax import lax
from jax.experimental import pallas as pl
from jax.experimental.pallas import tpu as pltpu
from jax.sharding import PartitionSpec as P

EXPERTS = 16
CAP = 4
PAIR = 2 * CAP
ROWS_DIM = (((0,), (0,)), ((), ()))
LAST_DIM = (((1,), (1,)), ((), ()))


def gelu_parts(value):
    coef = math.sqrt(2.0 / math.pi)
    square = value * value
    hyper = jnp.tanh(coef * value * (1.0 + 0.044715 * square))
    half = 0.5 * (1.0 + hyper)
    slope = half + 0.5 * value * (1.0 - hyper * hyper) * coef * (1.0 + 3.0 * 0.044715 * square)
    return (value * half, slope)


def place_rows(ids_t, prio):
    count = ids_t.shape[1]
    first = ids_t[0:1, :]
    second = ids_t[1:2, :]
    stack = jnp.concatenate([first, second, prio, jnp.zeros((5, count), jnp.int32)], axis=0)
    columns = jnp.transpose(stack.astype(jnp.float32), (1, 0)).astype(jnp.int32)
    first_c, second_c, prio_c = columns[:, 0:1], columns[:, 1:2], columns[:, 2:3]
    ahead = prio_c < prio
    one = jnp.float32(1.0)
    zero = jnp.float32(0.0)
    slot_0 = jnp.sum(jnp.where((first_c == first) & ahead, one, zero), axis=0, keepdims=True)
    slot_1 = jnp.sum(
        jnp.where((first_c == second) | ((second_c == second) & ahead), one, zero),
        axis=0,
        keepdims=True,
    )
    slot_0 = slot_0.astype(jnp.int32)
    slot_1 = slot_1.astype(jnp.int32)
    place_0 = jnp.where(slot_0 < CAP, first * CAP + slot_0, -1)
    place_1 = jnp.where(slot_1 < CAP, second * CAP + slot_1, -1)
    return place_0, place_1


def dispatch_kernel(
    ids_ref, prio_ref, gates_ref, tok_hbm, cot_hbm, send_ref, plan_ref, both_ref, sem
):
    count = tok_hbm.shape[0]
    copies = (
        pltpu.make_async_copy(tok_hbm, both_ref.at[0:count], sem.at[0]),
        pltpu.make_async_copy(cot_hbm, both_ref.at[count:2 * count], sem.at[1]),
    )
    for copy in copies:
        copy.start()
    place_0, place_1 = place_rows(ids_ref[...], prio_ref[...])
    rows = EXPERTS * PAIR
    row = lax.broadcasted_iota(jnp.int32, (rows, count), 0)
    slot = row // PAIR * CAP + row % CAP
    is_x = row % PAIR < CAP
    hit_0 = slot == place_0
    hit_1 = slot == place_1
    hit = jnp.where(hit_0 | hit_1, 1.0, 0.0)
    pick = jnp.concatenate(
        [jnp.where(is_x, hit, 0.0), jnp.where(is_x, 0.0, hit)], axis=1
    ).astype(jnp.bfloat16)
    gate = jnp.where(hit_0, gates_ref[0:1, :], 0.0) + jnp.where(hit_1, gates_ref[1:2, :], 0.0)
    scale = jnp.sum(gate, axis=1, keepdims=True)
    scale = jnp.where(is_x[:, 0:1], 1.0, scale)
    plan_ref[...] = jnp.concatenate(
        [
            place_0.astype(jnp.float32),
            place_1.astype(jnp.float32),
            gates_ref[...],
            jnp.zeros((4, count), jnp.float32),
        ],
        axis=0,
    )
    for copy in copies:
        copy.wait()
    found = jnp.dot(pick, both_ref[...], preferred_element_type=jnp.float32)
    send_ref[...] = (found * scale).astype(jnp.bfloat16)


def tables(plan_ref, pick_ref, gate_ref):
    place_0 = plan_ref[0:1, :].astype(jnp.int32)
    place_1 = plan_ref[1:2, :].astype(jnp.int32)
    count = place_0.shape[1]
    rows = EXPERTS * PAIR
    row = lax.broadcasted_iota(jnp.int32, (rows, count), 0)
    slot = row // PAIR * CAP + row % CAP
    is_x = row % PAIR < CAP
    hit_0 = jnp.where(slot == place_0, 1.0, 0.0)
    hit_1 = jnp.where(slot == place_1, 1.0, 0.0)
    pick_0 = jnp.transpose(jnp.where(is_x, hit_0, 0.0), (1, 0))
    pick_1 = jnp.transpose(jnp.where(is_x, hit_1, 0.0), (1, 0))
    pick_b = jnp.transpose(jnp.where(is_x, 0.0, hit_0 + hit_1), (1, 0))
    pick_ref[...] = jnp.concatenate([pick_0, pick_1, pick_b], axis=0).astype(jnp.bfloat16)
    gate_ref[...] = jnp.transpose(plan_ref[...], (1, 0))


def row_picks(rows):
    half = rows // 2
    out = lax.broadcasted_iota(jnp.int32, (half, rows), 0)
    col = lax.broadcasted_iota(jnp.int32, (half, rows), 1)
    source = out // CAP * PAIR + out % CAP
    x_pick = jnp.where(col == source, 1.0, 0.0).astype(jnp.bfloat16)
    g_pick = jnp.where(col == source + CAP, 1.0, 0.0).astype(jnp.bfloat16)
    return x_pick, g_pick


def forward_kernel(
    steps, recv_ref, plan_ref, w_in_hbm, w_out_hbm,
    ret_ref, x_t_ref, g_ref, act_ref, d_pre_ref, pick_ref, gate_ref,
    w_in_ref, w_out_ref, x_ref, out_acc, back_acc, sem_in, sem_out,
):
    depth = w_in_ref.shape[2]

    part = depth // 2

    def copies(step, first, size, slot):
        cols = pl.ds(pl.multiple_of(step * depth + first, size), size)
        near = pl.ds(first, size)
        return (
            pltpu.make_async_copy(
                w_in_hbm.at[:, cols], w_in_ref.at[step, :, near], sem_in.at[slot]
            ),
            pltpu.make_async_copy(
                w_out_hbm.at[cols, :], w_out_ref.at[step, near, :], sem_out.at[slot]
            ),
        )

    opening = [copies(0, 0, part, 0), copies(0, part, part, steps)]
    for pair in opening:
        for copy in pair:
            copy.start()

    def begin(step, carry):
        for copy in copies(step, 0, depth, step):
            copy.start()
        return carry

    lax.fori_loop(1, steps, begin, 0)
    recv = recv_ref[...]
    x_pick, g_pick = row_picks(recv.shape[0])
    x_rows = jnp.dot(x_pick, recv, preferred_element_type=jnp.float32)
    x_ref[...] = x_rows.astype(jnp.bfloat16)
    x_t_ref[...] = jnp.transpose(x_rows, (1, 0)).astype(jnp.bfloat16)
    g_ref[...] = jnp.dot(g_pick, recv, preferred_element_type=jnp.float32).astype(jnp.bfloat16)
    tables(plan_ref, pick_ref, gate_ref)
    out_acc[...] = jnp.zeros_like(out_acc)
    back_acc[...] = jnp.zeros_like(back_acc)

    def front(step, cols):
        pre = jnp.dot(x_ref[...], w_in_ref[step, :, cols], preferred_element_type=jnp.float32)
        d_act = lax.dot_general(
            g_ref[...], w_out_ref[step, cols, :], LAST_DIM, preferred_element_type=jnp.float32
        )
        return pre, d_act

    def middle(step, cols, pre, d_act):
        value, slope = gelu_parts(pre)
        act_ref[step, :, cols] = value.astype(jnp.bfloat16)
        d_pre_ref[step, :, cols] = (d_act * slope).astype(jnp.bfloat16)

    def back(step, act, d_pre):
        out_acc[...] += jnp.dot(act, w_out_ref[step], preferred_element_type=jnp.float32)
        back_acc[...] += lax.dot_general(
            d_pre, w_in_ref[step], LAST_DIM, preferred_element_type=jnp.float32
        )

    for first, pair in zip((0, part), opening):
        for copy in pair:
            copy.wait()
        cols = slice(first, first + part)
        middle(0, cols, *front(0, cols))

    def body(step, carry):
        for copy in copies(step, 0, depth, step):
            copy.wait()
        cols = slice(0, depth)
        act, d_pre = act_ref[step - 1], d_pre_ref[step - 1]
        found = front(step, cols)
        back(step - 1, act, d_pre)
        middle(step, cols, *found)
        return carry

    lax.fori_loop(1, steps, body, 0)
    back(steps - 1, act_ref[steps - 1], d_pre_ref[steps - 1])
    ret = lax.dot_general(
        x_pick, out_acc[...].astype(jnp.bfloat16), ROWS_DIM, preferred_element_type=jnp.float32
    ) + lax.dot_general(
        g_pick, back_acc[...].astype(jnp.bfloat16), ROWS_DIM, preferred_element_type=jnp.float32
    )
    ret_ref[...] = ret.astype(jnp.bfloat16)


def product(out_ref, left, right, tall, wide):
    rows, cols = out_ref.shape
    for col in range(0, cols, wide):
        col_end = min(col + wide, cols)
        for row in range(0, rows, tall):
            row_end = min(row + tall, rows)
            out_ref[row:row_end, col:col_end] = jnp.dot(
                left[row:row_end], right[:, col:col_end], preferred_element_type=jnp.float32
            ).astype(jnp.bfloat16)


def grads_kernel(x_t_ref, g_ref, act_ref, d_pre_ref, d_in_ref, d_out_ref):
    act_t = jnp.transpose(act_ref[0].astype(jnp.float32), (1, 0)).astype(jnp.bfloat16)
    product(d_in_ref, x_t_ref[...], d_pre_ref[0], 416, 256)
    product(d_out_ref, act_t, g_ref[...], 512, 256)


def combine_kernel(ret_ref, pick_ref, gate_ref, cot_ref, mixed_ref, d_tok_ref, d_gate_ref):
    count = cot_ref.shape[0]
    rows = pick_ref.shape[1]
    found = None
    for first in range(0, ret_ref.shape[0], rows):
        part = jnp.dot(
            pick_ref[...], ret_ref[first:first + rows, :], preferred_element_type=jnp.float32
        )
        found = part if found is None else found + part
    o_0, o_1 = found[:count], found[count:2 * count]
    mixed_ref[...] = (gate_ref[:, 2:3] * o_0 + gate_ref[:, 3:4] * o_1).astype(jnp.bfloat16)
    d_tok_ref[...] = found[2 * count:].astype(jnp.bfloat16)
    cot = cot_ref[...].astype(jnp.float32)
    d_0 = jnp.sum(cot * o_0, axis=1, keepdims=True)
    d_1 = jnp.sum(cot * o_1, axis=1, keepdims=True)
    lane = lax.broadcasted_iota(jnp.int32, (count, 8), 1)
    both = jnp.where(lane == 0, d_0, jnp.where(lane == 1, d_1, 0.0))
    d_gate_ref[...] = jnp.transpose(both, (1, 0))[0:2, :]


def params(mib):
    return pltpu.CompilerParams(vmem_limit_bytes=mib * 1024 * 1024)


def chunk_of(hidden, want):
    return max(size for size in range(128, want + 1, 128) if hidden % size == 0)


def per_device(tokens, expert_ids, priority, gates, w_in, w_out, cotangent):
    count, width = tokens.shape
    repl = lax.axis_size("expert") // EXPERTS
    slots = EXPERTS * PAIR
    hidden = w_in.shape[2]
    ids_t = jnp.transpose(expert_ids, (1, 0))
    gates_t = jnp.transpose(gates, (1, 0))
    low = jnp.bfloat16
    vmem = pl.BlockSpec(memory_space=pltpu.VMEM)
    hbm = pl.BlockSpec(memory_space=pl.ANY)
    send, plan = pl.pallas_call(
        dispatch_kernel,
        out_shape=(
            pltpu.VMEM((slots, width), low),
            pltpu.VMEM((8, count), jnp.float32),
        ),
        in_specs=[vmem] * 3 + [hbm] * 2,
        out_specs=(vmem,) * 2,
        scratch_shapes=[
            pltpu.VMEM((2 * count, width), low),
            pltpu.SemaphoreType.DMA((2,)),
        ],
        compiler_params=params(56),
        name="dispatch",
    )(ids_t, priority, gates_t, tokens, cotangent)
    send = jnp.tile(send.reshape(EXPERTS, PAIR, width), (repl, 1, 1))
    recv = lax.all_to_all(send, "expert", split_axis=0, concat_axis=0, tiled=True)
    rows = recv.shape[0] * PAIR
    recv = recv.reshape(rows, width)
    half = rows // 2
    chunk = chunk_of(hidden, 1024)
    steps = hidden // chunk
    part = chunk // 2
    ret, x_t, g_rows, act, d_pre, pick, gate_cols = pl.pallas_call(
        functools.partial(forward_kernel, steps),
        out_shape=(
            pltpu.VMEM((rows, width), low),
            jax.ShapeDtypeStruct((width, half), low),
            jax.ShapeDtypeStruct((half, width), low),
            jax.ShapeDtypeStruct((steps, half, chunk), low),
            jax.ShapeDtypeStruct((steps, half, chunk), low),
            jax.ShapeDtypeStruct((3 * count, slots), low),
            jax.ShapeDtypeStruct((count, 8), jnp.float32),
        ),
        in_specs=[vmem] * 2 + [hbm] * 2,
        out_specs=(vmem,) * 7,
        scratch_shapes=[
            pltpu.VMEM((steps, width, chunk), low),
            pltpu.VMEM((steps, chunk, width), low),
            pltpu.VMEM((half, width), low),
            pltpu.VMEM((half, width), jnp.float32),
            pltpu.VMEM((half, width), jnp.float32),
            pltpu.SemaphoreType.DMA((steps + 1,)),
            pltpu.SemaphoreType.DMA((steps + 1,)),
        ],
        compiler_params=params(50),
        cost_estimate=pl.CostEstimate(
            flops=8 * half * width * hidden,
            bytes_accessed=4 * width * hidden,
            transcendentals=half * hidden,
        ),
        name="forward",
    )(recv, plan, w_in[0], w_out[0])
    ret = lax.all_to_all(
        ret.reshape(rows // PAIR, PAIR, width), "expert", split_axis=0, concat_axis=0, tiled=True
    ).reshape(rows, width)
    d_w_in, d_w_out = pl.pallas_call(
        grads_kernel,
        grid=(2 * steps,),
        out_shape=(
            jax.ShapeDtypeStruct((width, hidden), low),
            jax.ShapeDtypeStruct((hidden, width), low),
        ),
        in_specs=[
            pl.BlockSpec((width, half), lambda i: (0, 0)),
            pl.BlockSpec((half, width), lambda i: (0, 0)),
            pl.BlockSpec((1, half, part), lambda i: (i // 2, 0, i % 2)),
            pl.BlockSpec((1, half, part), lambda i: (i // 2, 0, i % 2)),
        ],
        out_specs=(
            pl.BlockSpec((width, part), lambda i: (0, i)),
            pl.BlockSpec((part, width), lambda i: (i, 0)),
        ),
        compiler_params=params(24),
        cost_estimate=pl.CostEstimate(
            flops=4 * half * width * hidden,
            bytes_accessed=4 * width * hidden,
            transcendentals=0,
        ),
        name="grads",
    )(x_t, g_rows, act, d_pre)
    mixed, d_tokens, d_gates_t = pl.pallas_call(
        combine_kernel,
        out_shape=(
            jax.ShapeDtypeStruct((count, width), low),
            jax.ShapeDtypeStruct((count, width), low),
            jax.ShapeDtypeStruct((2, count), jnp.float32),
        ),
        compiler_params=params(12),
        name="combine",
    )(ret, pick, gate_cols, cotangent)
    return (mixed, d_tokens, jnp.transpose(d_gates_t, (1, 0)), d_w_in[None], d_w_out[None])


def solution(mesh):
    rows = P(("groups", "expert"), None)
    return jax.shard_map(
        per_device,
        mesh=mesh,
        in_specs=(rows, rows, rows, rows, P("expert", None, None), P("expert", None, None), rows),
        out_specs=(
            rows,
            rows,
            rows,
            P(("groups", "expert"), None, None),
            P(("groups", "expert"), None, None),
        ),
        check_vma=False,
    )
```

```python
import functools
import math

import jax
import jax.numpy as jnp
from jax import lax
from jax.experimental import pallas as pl
from jax.experimental.pallas import tpu as pltpu
from jax.sharding import PartitionSpec as P

EXPERTS = 16
CAP = 4
PAIR = 2 * CAP
ROWS_DIM = (((0,), (0,)), ((), ()))
LAST_DIM = (((1,), (1,)), ((), ()))


def gelu_parts(value):
    coef = math.sqrt(2.0 / math.pi)
    square = value * value
    hyper = jnp.tanh(coef * value * (1.0 + 0.044715 * square))
    half = 0.5 * (1.0 + hyper)
    slope = half + 0.5 * value * (1.0 - hyper * hyper) * coef * (1.0 + 3.0 * 0.044715 * square)
    return (value * half, slope)


def place_rows(ids_t, prio):
    count = ids_t.shape[1]
    first = ids_t[0:1, :]
    second = ids_t[1:2, :]
    stack = jnp.concatenate([first, second, prio, jnp.zeros((5, count), jnp.int32)], axis=0)
    columns = jnp.transpose(stack.astype(jnp.float32), (1, 0)).astype(jnp.int32)
    first_c, second_c, prio_c = columns[:, 0:1], columns[:, 1:2], columns[:, 2:3]
    ahead = prio_c < prio
    one = jnp.float32(1.0)
    zero = jnp.float32(0.0)
    slot_0 = jnp.sum(jnp.where((first_c == first) & ahead, one, zero), axis=0, keepdims=True)
    slot_1 = jnp.sum(
        jnp.where((first_c == second) | ((second_c == second) & ahead), one, zero),
        axis=0,
        keepdims=True,
    )
    slot_0 = slot_0.astype(jnp.int32)
    slot_1 = slot_1.astype(jnp.int32)
    place_0 = jnp.where(slot_0 < CAP, first * CAP + slot_0, -1)
    place_1 = jnp.where(slot_1 < CAP, second * CAP + slot_1, -1)
    return place_0, place_1


def dispatch_kernel(
    ids_ref, prio_ref, gates_ref, tok_hbm, cot_hbm, send_ref, plan_ref, both_ref, sem
):
    count = tok_hbm.shape[0]
    copies = (
        pltpu.make_async_copy(tok_hbm, both_ref.at[0:count], sem.at[0]),
        pltpu.make_async_copy(cot_hbm, both_ref.at[count:2 * count], sem.at[1]),
    )
    for copy in copies:
        copy.start()
    place_0, place_1 = place_rows(ids_ref[...], prio_ref[...])
    rows = EXPERTS * PAIR
    row = lax.broadcasted_iota(jnp.int32, (rows, count), 0)
    slot = row // PAIR * CAP + row % CAP
    is_x = row % PAIR < CAP
    hit_0 = slot == place_0
    hit_1 = slot == place_1
    hit = jnp.where(hit_0 | hit_1, 1.0, 0.0)
    pick = jnp.concatenate(
        [jnp.where(is_x, hit, 0.0), jnp.where(is_x, 0.0, hit)], axis=1
    ).astype(jnp.bfloat16)
    gate = jnp.where(hit_0, gates_ref[0:1, :], 0.0) + jnp.where(hit_1, gates_ref[1:2, :], 0.0)
    scale = jnp.sum(gate, axis=1, keepdims=True)
    scale = jnp.where(is_x[:, 0:1], 1.0, scale)
    plan_ref[...] = jnp.concatenate(
        [
            place_0.astype(jnp.float32),
            place_1.astype(jnp.float32),
            gates_ref[...],
            jnp.zeros((4, count), jnp.float32),
        ],
        axis=0,
    )
    for copy in copies:
        copy.wait()
    found = jnp.dot(pick, both_ref[...], preferred_element_type=jnp.float32)
    send_ref[...] = (found * scale).astype(jnp.bfloat16)


def tables(plan_ref, pick_ref, gate_ref):
    place_0 = plan_ref[0:1, :].astype(jnp.int32)
    place_1 = plan_ref[1:2, :].astype(jnp.int32)
    count = place_0.shape[1]
    rows = EXPERTS * PAIR
    row = lax.broadcasted_iota(jnp.int32, (rows, count), 0)
    slot = row // PAIR * CAP + row % CAP
    is_x = row % PAIR < CAP
    hit_0 = jnp.where(slot == place_0, 1.0, 0.0)
    hit_1 = jnp.where(slot == place_1, 1.0, 0.0)
    pick_0 = jnp.transpose(jnp.where(is_x, hit_0, 0.0), (1, 0))
    pick_1 = jnp.transpose(jnp.where(is_x, hit_1, 0.0), (1, 0))
    pick_b = jnp.transpose(jnp.where(is_x, 0.0, hit_0 + hit_1), (1, 0))
    pick_ref[...] = jnp.concatenate([pick_0, pick_1, pick_b], axis=0).astype(jnp.bfloat16)
    gate_ref[...] = jnp.transpose(plan_ref[...], (1, 0))


def row_picks(rows):
    half = rows // 2
    out = lax.broadcasted_iota(jnp.int32, (half, rows), 0)
    col = lax.broadcasted_iota(jnp.int32, (half, rows), 1)
    source = out // CAP * PAIR + out % CAP
    x_pick = jnp.where(col == source, 1.0, 0.0).astype(jnp.bfloat16)
    g_pick = jnp.where(col == source + CAP, 1.0, 0.0).astype(jnp.bfloat16)
    return x_pick, g_pick


def forward_kernel(
    steps, recv_ref, plan_ref, w_in_hbm, w_out_hbm,
    ret_ref, x_t_ref, d_pre_ref, pick_ref, gate_ref, d_out_hbm,
    w_in_ref, w_out_ref, x_ref, g_ref, act_ref, act_t_ref, stage, out_acc, back_acc,
    sem_in, sem_out, sem_left,
):
    width, depth = w_in_ref.shape[1:]
    low = jnp.bfloat16

    def copies(step):
        cols = pl.ds(pl.multiple_of(step * depth, depth), depth)
        return (
            pltpu.make_async_copy(w_in_hbm.at[:, cols], w_in_ref.at[step], sem_in.at[step]),
            pltpu.make_async_copy(w_out_hbm.at[cols, :], w_out_ref.at[step], sem_out.at[step]),
        )

    def leave(step):
        rows = pl.ds(pl.multiple_of(step * depth, depth), depth)
        slot = lax.rem(step, 2)
        return pltpu.make_async_copy(stage.at[slot], d_out_hbm.at[rows, :], sem_left.at[slot])

    def begin(step, carry):
        for copy in copies(step):
            copy.start()
        return carry

    lax.fori_loop(0, steps, begin, 0)
    recv = recv_ref[...]
    x_pick, g_pick = row_picks(recv.shape[0])
    x_rows = jnp.dot(x_pick, recv, preferred_element_type=jnp.float32)
    x_ref[...] = x_rows.astype(low)
    x_t_ref[...] = jnp.transpose(x_rows, (1, 0)).astype(low)
    g_ref[...] = jnp.dot(g_pick, recv, preferred_element_type=jnp.float32).astype(low)
    tables(plan_ref, pick_ref, gate_ref)
    out_acc[...] = jnp.zeros_like(out_acc)
    back_acc[...] = jnp.zeros_like(back_acc)

    def front_dots(step, found):
        for first in range(0, depth, 256):
            cols = slice(first, min(first + 256, depth))
            pre = []

            def one(cols=cols, pre=pre):
                pre.append(
                    jnp.dot(
                        x_ref[...], w_in_ref[step, :, cols], preferred_element_type=jnp.float32
                    )
                )

            def two(cols=cols, pre=pre):
                d_act = lax.dot_general(
                    g_ref[...],
                    w_out_ref[step, cols, :],
                    LAST_DIM,
                    preferred_element_type=jnp.float32,
                )
                found.append((cols, pre[0], d_act))

            yield one
            yield two

    def back_dots(step, act, d_pre):
        for first in range(0, width, 256):
            cols = slice(first, min(first + 256, width))

            def one(cols=cols):
                out_acc[:, cols] += jnp.dot(
                    act, w_out_ref[step, :, cols], preferred_element_type=jnp.float32
                )

            def two(cols=cols):
                back_acc[:, cols] += lax.dot_general(
                    d_pre,
                    w_in_ref[step, cols, :],
                    LAST_DIM,
                    preferred_element_type=jnp.float32,
                )

            yield one
            yield two

    def grad_dots(step, act_t):
        slot = lax.rem(step, 2)
        for first in range(0, width, 256):
            cols = slice(first, min(first + 256, width))
            for top in range(0, depth, 256):
                rows = slice(top, min(top + 256, depth))

                def one(cols=cols, rows=rows):
                    stage[slot, rows, cols] = jnp.dot(
                        act_t[rows], g_ref[:, cols], preferred_element_type=jnp.float32
                    ).astype(low)

                yield one

    def middle(step, found):
        for cols, pre, d_act in found:
            value, slope = gelu_parts(pre)
            act_ref[:, cols] = value.astype(low)
            act_t_ref[cols, :] = jnp.transpose(value, (1, 0)).astype(low)
            d_pre_ref[step, :, cols] = (d_act * slope).astype(low)

    def arrive(step):
        for copy in copies(step):
            copy.wait()

    def run(first, second):
        done = 0
        for index, thunk in enumerate(first):
            thunk()
            due = (index + 1) * len(second) // len(first)
            for other in second[done:due]:
                other()
            done = due

    arrive(0)
    found = []
    for thunk in front_dots(0, found):
        thunk()
    middle(0, found)

    def body(step, carry):
        arrive(step)

        @pl.when(step > 2)
        def _():
            leave(step - 3).wait()

        act, act_t, d_pre = act_ref[...], act_t_ref[...], d_pre_ref[step - 1]
        found = []
        run(
            [*front_dots(step, found), *back_dots(step - 1, act, d_pre)],
            [*grad_dots(step - 1, act_t)],
        )
        middle(step, found)
        leave(step - 1).start()
        return carry

    lax.fori_loop(1, steps, body, 0)
    last = steps - 1
    if steps > 2:
        leave(last - 2).wait()
    run([*back_dots(last, act_ref[...], d_pre_ref[last])], [*grad_dots(last, act_t_ref[...])])
    leave(last).start()
    ret = lax.dot_general(
        x_pick, out_acc[...].astype(low), ROWS_DIM, preferred_element_type=jnp.float32
    ) + lax.dot_general(
        g_pick, back_acc[...].astype(low), ROWS_DIM, preferred_element_type=jnp.float32
    )
    ret_ref[...] = ret.astype(low)
    if steps > 1:
        leave(last - 1).wait()
    leave(last).wait()


def product(out_ref, left, right, tall, wide):
    rows, cols = out_ref.shape
    for col in range(0, cols, wide):
        col_end = min(col + wide, cols)
        for row in range(0, rows, tall):
            row_end = min(row + tall, rows)
            out_ref[row:row_end, col:col_end] = jnp.dot(
                left[row:row_end], right[:, col:col_end], preferred_element_type=jnp.float32
            ).astype(jnp.bfloat16)


def grads_kernel(x_t_ref, d_pre_ref, d_in_ref):
    product(d_in_ref, x_t_ref[...], d_pre_ref[0], 208, 256)


def combine_kernel(ret_ref, pick_ref, gate_ref, cot_ref, mixed_ref, d_tok_ref, d_gate_ref):
    count = cot_ref.shape[0]
    rows = pick_ref.shape[1]
    found = None
    for first in range(0, ret_ref.shape[0], rows):
        part = jnp.dot(
            pick_ref[...], ret_ref[first:first + rows, :], preferred_element_type=jnp.float32
        )
        found = part if found is None else found + part
    o_0, o_1 = found[:count], found[count:2 * count]
    mixed_ref[...] = (gate_ref[:, 2:3] * o_0 + gate_ref[:, 3:4] * o_1).astype(jnp.bfloat16)
    d_tok_ref[...] = found[2 * count:].astype(jnp.bfloat16)
    cot = cot_ref[...].astype(jnp.float32)
    d_0 = jnp.sum(cot * o_0, axis=1, keepdims=True)
    d_1 = jnp.sum(cot * o_1, axis=1, keepdims=True)
    lane = lax.broadcasted_iota(jnp.int32, (count, 8), 1)
    both = jnp.where(lane == 0, d_0, jnp.where(lane == 1, d_1, 0.0))
    d_gate_ref[...] = jnp.transpose(both, (1, 0))[0:2, :]


def params(mib):
    return pltpu.CompilerParams(vmem_limit_bytes=mib * 1024 * 1024)


def chunk_of(hidden, want):
    return max(size for size in range(128, want + 1, 128) if hidden % size == 0)


def per_device(tokens, expert_ids, priority, gates, w_in, w_out, cotangent):
    count, width = tokens.shape
    repl = lax.axis_size("expert") // EXPERTS
    slots = EXPERTS * PAIR
    hidden = w_in.shape[2]
    ids_t = jnp.transpose(expert_ids, (1, 0))
    gates_t = jnp.transpose(gates, (1, 0))
    low = jnp.bfloat16
    vmem = pl.BlockSpec(memory_space=pltpu.VMEM)
    hbm = pl.BlockSpec(memory_space=pl.ANY)
    send, plan = pl.pallas_call(
        dispatch_kernel,
        out_shape=(
            pltpu.VMEM((slots, width), low),
            pltpu.VMEM((8, count), jnp.float32),
        ),
        in_specs=[vmem] * 3 + [hbm] * 2,
        out_specs=(vmem,) * 2,
        scratch_shapes=[
            pltpu.VMEM((2 * count, width), low),
            pltpu.SemaphoreType.DMA((2,)),
        ],
        compiler_params=params(56),
        name="dispatch",
    )(ids_t, priority, gates_t, tokens, cotangent)
    send = jnp.tile(send.reshape(EXPERTS, PAIR, width), (repl, 1, 1))
    recv = lax.all_to_all(send, "expert", split_axis=0, concat_axis=0, tiled=True)
    rows = recv.shape[0] * PAIR
    recv = recv.reshape(rows, width)
    half = rows // 2
    chunk = chunk_of(hidden, 512)
    steps = hidden // chunk
    ret, x_t, d_pre, pick, gate_cols, d_w_out = pl.pallas_call(
        functools.partial(forward_kernel, steps),
        out_shape=(
            pltpu.VMEM((rows, width), low),
            jax.ShapeDtypeStruct((width, half), low),
            jax.ShapeDtypeStruct((steps, half, chunk), low),
            jax.ShapeDtypeStruct((3 * count, slots), low),
            jax.ShapeDtypeStruct((count, 8), jnp.float32),
            jax.ShapeDtypeStruct((hidden, width), low),
        ),
        in_specs=[vmem] * 2 + [hbm] * 2,
        out_specs=(vmem,) * 5 + (hbm,),
        scratch_shapes=[
            pltpu.VMEM((steps, width, chunk), low),
            pltpu.VMEM((steps, chunk, width), low),
            pltpu.VMEM((half, width), low),
            pltpu.VMEM((half, width), low),
            pltpu.VMEM((half, chunk), low),
            pltpu.VMEM((chunk, half), low),
            pltpu.VMEM((2, chunk, width), low),
            pltpu.VMEM((half, width), jnp.float32),
            pltpu.VMEM((half, width), jnp.float32),
            pltpu.SemaphoreType.DMA((steps,)),
            pltpu.SemaphoreType.DMA((steps,)),
            pltpu.SemaphoreType.DMA((2,)),
        ],
        compiler_params=params(48),
        cost_estimate=pl.CostEstimate(
            flops=10 * half * width * hidden,
            bytes_accessed=6 * width * hidden,
            transcendentals=half * hidden,
        ),
        name="forward",
    )(recv, plan, w_in[0], w_out[0])
    ret = lax.all_to_all(
        ret.reshape(rows // PAIR, PAIR, width), "expert", split_axis=0, concat_axis=0, tiled=True
    ).reshape(rows, width)
    d_w_in = pl.pallas_call(
        grads_kernel,
        grid=(steps,),
        out_shape=jax.ShapeDtypeStruct((width, hidden), low),
        in_specs=[
            pl.BlockSpec((width, half), lambda i: (0, 0)),
            pl.BlockSpec((1, half, chunk), lambda i: (i, 0, 0)),
        ],
        out_specs=pl.BlockSpec((width, chunk), lambda i: (0, i)),
        compiler_params=params(24),
        cost_estimate=pl.CostEstimate(
            flops=2 * half * width * hidden,
            bytes_accessed=2 * width * hidden,
            transcendentals=0,
        ),
        name="grads",
    )(x_t, d_pre)
    mixed, d_tokens, d_gates_t = pl.pallas_call(
        combine_kernel,
        out_shape=(
            jax.ShapeDtypeStruct((count, width), low),
            jax.ShapeDtypeStruct((count, width), low),
            jax.ShapeDtypeStruct((2, count), jnp.float32),
        ),
        compiler_params=params(12),
        name="combine",
    )(ret, pick, gate_cols, cotangent)
    return (mixed, d_tokens, jnp.transpose(d_gates_t, (1, 0)), d_w_in[None], d_w_out[None])


def solution(mesh):
    rows = P(("groups", "expert"), None)
    return jax.shard_map(
        per_device,
        mesh=mesh,
        in_specs=(rows, rows, rows, rows, P("expert", None, None), P("expert", None, None), rows),
        out_specs=(
            rows,
            rows,
            rows,
            P(("groups", "expert"), None, None),
            P(("groups", "expert"), None, None),
        ),
        check_vma=False,
    )
```

```python
import functools
import math

import jax
import jax.numpy as jnp
from jax import lax
from jax.experimental import pallas as pl
from jax.experimental.pallas import tpu as pltpu
from jax.sharding import PartitionSpec as P

EXPERTS = 16
CAP = 4
PAIR = 2 * CAP
ROWS_DIM = (((0,), (0,)), ((), ()))
LAST_DIM = (((1,), (1,)), ((), ()))


def gelu_parts(value):
    coef = math.sqrt(2.0 / math.pi)
    square = value * value
    hyper = jnp.tanh(coef * value * (1.0 + 0.044715 * square))
    half = 0.5 * (1.0 + hyper)
    slope = half + 0.5 * value * (1.0 - hyper * hyper) * coef * (1.0 + 3.0 * 0.044715 * square)
    return (value * half, slope)


def place_rows(ids_t, prio):
    count = ids_t.shape[1]
    first = ids_t[0:1, :]
    second = ids_t[1:2, :]
    stack = jnp.concatenate([first, second, prio, jnp.zeros((5, count), jnp.int32)], axis=0)
    columns = jnp.transpose(stack.astype(jnp.float32), (1, 0)).astype(jnp.int32)
    first_c, second_c, prio_c = columns[:, 0:1], columns[:, 1:2], columns[:, 2:3]
    ahead = prio_c < prio
    one = jnp.float32(1.0)
    zero = jnp.float32(0.0)
    slot_0 = jnp.sum(jnp.where((first_c == first) & ahead, one, zero), axis=0, keepdims=True)
    slot_1 = jnp.sum(
        jnp.where((first_c == second) | ((second_c == second) & ahead), one, zero),
        axis=0,
        keepdims=True,
    )
    slot_0 = slot_0.astype(jnp.int32)
    slot_1 = slot_1.astype(jnp.int32)
    place_0 = jnp.where(slot_0 < CAP, first * CAP + slot_0, -1)
    place_1 = jnp.where(slot_1 < CAP, second * CAP + slot_1, -1)
    return place_0, place_1


def dispatch_kernel(
    ids_ref, prio_ref, gates_ref, tok_hbm, cot_hbm, send_ref, plan_ref, both_ref, sem
):
    count = tok_hbm.shape[0]
    copies = (
        pltpu.make_async_copy(tok_hbm, both_ref.at[0:count], sem.at[0]),
        pltpu.make_async_copy(cot_hbm, both_ref.at[count:2 * count], sem.at[1]),
    )
    for copy in copies:
        copy.start()
    place_0, place_1 = place_rows(ids_ref[...], prio_ref[...])
    rows = EXPERTS * PAIR
    row = lax.broadcasted_iota(jnp.int32, (rows, count), 0)
    slot = row // PAIR * CAP + row % CAP
    is_x = row % PAIR < CAP
    hit_0 = slot == place_0
    hit_1 = slot == place_1
    hit = jnp.where(hit_0 | hit_1, 1.0, 0.0)
    pick = jnp.concatenate(
        [jnp.where(is_x, hit, 0.0), jnp.where(is_x, 0.0, hit)], axis=1
    ).astype(jnp.bfloat16)
    gate = jnp.where(hit_0, gates_ref[0:1, :], 0.0) + jnp.where(hit_1, gates_ref[1:2, :], 0.0)
    scale = jnp.sum(gate, axis=1, keepdims=True)
    scale = jnp.where(is_x[:, 0:1], 1.0, scale)
    plan_ref[...] = jnp.concatenate(
        [
            place_0.astype(jnp.float32),
            place_1.astype(jnp.float32),
            gates_ref[...],
            jnp.zeros((4, count), jnp.float32),
        ],
        axis=0,
    )
    for copy in copies:
        copy.wait()
    found = jnp.dot(pick, both_ref[...], preferred_element_type=jnp.float32)
    send_ref[...] = (found * scale).astype(jnp.bfloat16)


def tables(plan_ref, pick_ref, gate_ref):
    place_0 = plan_ref[0:1, :].astype(jnp.int32)
    place_1 = plan_ref[1:2, :].astype(jnp.int32)
    count = place_0.shape[1]
    rows = EXPERTS * PAIR
    row = lax.broadcasted_iota(jnp.int32, (rows, count), 0)
    slot = row // PAIR * CAP + row % CAP
    is_x = row % PAIR < CAP
    hit_0 = jnp.where(slot == place_0, 1.0, 0.0)
    hit_1 = jnp.where(slot == place_1, 1.0, 0.0)
    pick_0 = jnp.transpose(jnp.where(is_x, hit_0, 0.0), (1, 0))
    pick_1 = jnp.transpose(jnp.where(is_x, hit_1, 0.0), (1, 0))
    pick_b = jnp.transpose(jnp.where(is_x, 0.0, hit_0 + hit_1), (1, 0))
    pick_ref[...] = jnp.concatenate([pick_0, pick_1, pick_b], axis=0).astype(jnp.bfloat16)
    gate_ref[...] = jnp.transpose(plan_ref[...], (1, 0))


def row_picks(rows):
    half = rows // 2
    out = lax.broadcasted_iota(jnp.int32, (half, rows), 0)
    col = lax.broadcasted_iota(jnp.int32, (half, rows), 1)
    source = out // CAP * PAIR + out % CAP
    x_pick = jnp.where(col == source, 1.0, 0.0).astype(jnp.bfloat16)
    g_pick = jnp.where(col == source + CAP, 1.0, 0.0).astype(jnp.bfloat16)
    return x_pick, g_pick


def forward_kernel(
    steps, recv_ref, plan_ref, w_in_hbm, w_out_hbm,
    ret_ref, x_t_ref, g_ref, act_t_ref, d_pre_ref, pick_ref, gate_ref,
    w_in_ref, w_out_ref, x_ref, act_ref, out_acc, back_acc, sem_in, sem_out,
):
    width, depth = w_in_ref.shape[1:]
    low = jnp.bfloat16

    def copies(step):
        cols = pl.ds(pl.multiple_of(step * depth, depth), depth)
        return (
            pltpu.make_async_copy(w_in_hbm.at[:, cols], w_in_ref.at[step], sem_in.at[step]),
            pltpu.make_async_copy(w_out_hbm.at[cols, :], w_out_ref.at[step], sem_out.at[step]),
        )

    def begin(step, carry):
        for copy in copies(step):
            copy.start()
        return carry

    lax.fori_loop(0, steps, begin, 0)
    recv = recv_ref[...]
    x_pick, g_pick = row_picks(recv.shape[0])
    x_rows = jnp.dot(x_pick, recv, preferred_element_type=jnp.float32)
    x_ref[...] = x_rows.astype(low)
    x_t_ref[...] = jnp.transpose(x_rows, (1, 0)).astype(low)
    g_ref[...] = jnp.dot(g_pick, recv, preferred_element_type=jnp.float32).astype(low)
    tables(plan_ref, pick_ref, gate_ref)
    out_acc[...] = jnp.zeros_like(out_acc)
    back_acc[...] = jnp.zeros_like(back_acc)

    def front_dots(step, found):
        for first in range(0, depth, 256):
            cols = slice(first, min(first + 256, depth))
            pre = []

            def one(cols=cols, pre=pre):
                pre.append(
                    jnp.dot(
                        x_ref[...], w_in_ref[step, :, cols], preferred_element_type=jnp.float32
                    )
                )

            def two(cols=cols, pre=pre):
                d_act = lax.dot_general(
                    g_ref[...],
                    w_out_ref[step, cols, :],
                    LAST_DIM,
                    preferred_element_type=jnp.float32,
                )
                found.append((cols, pre[0], d_act))

            yield one
            yield two

    def back_dots(step, act, d_pre):
        for first in range(0, width, 256):
            cols = slice(first, min(first + 256, width))

            def one(cols=cols):
                out_acc[:, cols] += jnp.dot(
                    act, w_out_ref[step, :, cols], preferred_element_type=jnp.float32
                )

            def two(cols=cols):
                back_acc[:, cols] += lax.dot_general(
                    d_pre,
                    w_in_ref[step, cols, :],
                    LAST_DIM,
                    preferred_element_type=jnp.float32,
                )

            yield one
            yield two

    def middle(step, found):
        for cols, pre, d_act in found:
            value, slope = gelu_parts(pre)
            act_ref[:, cols] = value.astype(low)
            act_t_ref[step, cols, :] = jnp.transpose(value, (1, 0)).astype(low)
            d_pre_ref[step, :, cols] = (d_act * slope).astype(low)

    def arrive(step):
        for copy in copies(step):
            copy.wait()

    arrive(0)
    found = []
    for thunk in front_dots(0, found):
        thunk()
    middle(0, found)

    def body(step, carry):
        arrive(step)
        act, d_pre = act_ref[...], d_pre_ref[step - 1]
        found = []
        for thunk in [*front_dots(step, found), *back_dots(step - 1, act, d_pre)]:
            thunk()
        middle(step, found)
        return carry

    lax.fori_loop(1, steps, body, 0)
    for thunk in back_dots(steps - 1, act_ref[...], d_pre_ref[steps - 1]):
        thunk()
    ret = lax.dot_general(
        x_pick, out_acc[...].astype(low), ROWS_DIM, preferred_element_type=jnp.float32
    ) + lax.dot_general(
        g_pick, back_acc[...].astype(low), ROWS_DIM, preferred_element_type=jnp.float32
    )
    ret_ref[...] = ret.astype(low)


def product(out_ref, left, right, tall, wide):
    rows, cols = out_ref.shape
    for col in range(0, cols, wide):
        col_end = min(col + wide, cols)
        for row in range(0, rows, tall):
            row_end = min(row + tall, rows)
            out_ref[row:row_end, col:col_end] = jnp.dot(
                left[row:row_end], right[:, col:col_end], preferred_element_type=jnp.float32
            ).astype(jnp.bfloat16)


def grads_kernel(
    x_t_ref, g_ref, act_t_ref, d_pre_ref, d_in_hbm, d_out_hbm, d_in_stage, d_out_stage, sem
):
    steps, depth = act_t_ref.shape[:2]
    width = x_t_ref.shape[0]
    slots = d_in_stage.shape[0]

    def leave(step):
        slot = lax.rem(step, slots)
        cols = pl.ds(pl.multiple_of(step * depth, depth), depth)
        pairs = []
        for index in range(2):
            some = pl.ds(index * (width // 2), width // 2)
            pairs.append((d_in_stage.at[slot, some], d_in_hbm.at[some, cols]))
        for index in range(2):
            here = pl.ds(index * (depth // 2), depth // 2)
            there = pl.ds(pl.multiple_of(step * depth + index * (depth // 2), 64), depth // 2)
            pairs.append((d_out_stage.at[slot, here], d_out_hbm.at[there]))
        return [
            pltpu.make_async_copy(*pair, sem.at[slot, index]) for index, pair in enumerate(pairs)
        ]

    def work(step, carry):
        @pl.when(step >= slots)
        def _():
            for copy in leave(step - slots):
                copy.wait()

        slot = lax.rem(step, slots)
        copies = leave(step)
        product(d_in_stage.at[slot], x_t_ref[...], d_pre_ref[step], 208, 256)
        for copy in copies[:2]:
            copy.start()
        product(d_out_stage.at[slot], act_t_ref[step], g_ref[...], 256, 256)
        for copy in copies[2:]:
            copy.start()
        return carry

    lax.fori_loop(0, steps, work, 0)
    for step in range(max(steps - slots, 0), steps):
        for copy in leave(step):
            copy.wait()


def combine_kernel(ret_ref, pick_ref, gate_ref, cot_ref, mixed_ref, d_tok_ref, d_gate_ref):
    count = cot_ref.shape[0]
    rows = pick_ref.shape[1]
    found = None
    for first in range(0, ret_ref.shape[0], rows):
        part = jnp.dot(
            pick_ref[...], ret_ref[first:first + rows, :], preferred_element_type=jnp.float32
        )
        found = part if found is None else found + part
    o_0, o_1 = found[:count], found[count:2 * count]
    mixed_ref[...] = (gate_ref[:, 2:3] * o_0 + gate_ref[:, 3:4] * o_1).astype(jnp.bfloat16)
    d_tok_ref[...] = found[2 * count:].astype(jnp.bfloat16)
    cot = cot_ref[...].astype(jnp.float32)
    d_0 = jnp.sum(cot * o_0, axis=1, keepdims=True)
    d_1 = jnp.sum(cot * o_1, axis=1, keepdims=True)
    lane = lax.broadcasted_iota(jnp.int32, (count, 8), 1)
    both = jnp.where(lane == 0, d_0, jnp.where(lane == 1, d_1, 0.0))
    d_gate_ref[...] = jnp.transpose(both, (1, 0))[0:2, :]


def params(mib):
    return pltpu.CompilerParams(vmem_limit_bytes=mib * 1024 * 1024)


def chunk_of(hidden, want):
    return max(size for size in range(128, want + 1, 128) if hidden % size == 0)


def per_device(tokens, expert_ids, priority, gates, w_in, w_out, cotangent):
    count, width = tokens.shape
    repl = lax.axis_size("expert") // EXPERTS
    slots = EXPERTS * PAIR
    hidden = w_in.shape[2]
    ids_t = jnp.transpose(expert_ids, (1, 0))
    gates_t = jnp.transpose(gates, (1, 0))
    low = jnp.bfloat16
    vmem = pl.BlockSpec(memory_space=pltpu.VMEM)
    hbm = pl.BlockSpec(memory_space=pl.ANY)
    send, plan = pl.pallas_call(
        dispatch_kernel,
        out_shape=(
            pltpu.VMEM((slots, width), low),
            pltpu.VMEM((8, count), jnp.float32),
        ),
        in_specs=[vmem] * 3 + [hbm] * 2,
        out_specs=(vmem,) * 2,
        scratch_shapes=[
            pltpu.VMEM((2 * count, width), low),
            pltpu.SemaphoreType.DMA((2,)),
        ],
        compiler_params=params(56),
        name="dispatch",
    )(ids_t, priority, gates_t, tokens, cotangent)
    send = jnp.tile(send.reshape(EXPERTS, PAIR, width), (repl, 1, 1))
    recv = lax.all_to_all(send, "expert", split_axis=0, concat_axis=0, tiled=True)
    rows = recv.shape[0] * PAIR
    recv = recv.reshape(rows, width)
    half = rows // 2
    chunk = chunk_of(hidden, 512)
    steps = hidden // chunk
    ret, x_t, g_rows, act_t, d_pre, pick, gate_cols = pl.pallas_call(
        functools.partial(forward_kernel, steps),
        out_shape=(
            pltpu.VMEM((rows, width), low),
            jax.ShapeDtypeStruct((width, half), low),
            jax.ShapeDtypeStruct((half, width), low),
            jax.ShapeDtypeStruct((steps, chunk, half), low),
            jax.ShapeDtypeStruct((steps, half, chunk), low),
            jax.ShapeDtypeStruct((3 * count, slots), low),
            jax.ShapeDtypeStruct((count, 8), jnp.float32),
        ),
        in_specs=[vmem] * 2 + [hbm] * 2,
        out_specs=(vmem,) * 7,
        scratch_shapes=[
            pltpu.VMEM((steps, width, chunk), low),
            pltpu.VMEM((steps, chunk, width), low),
            pltpu.VMEM((half, width), low),
            pltpu.VMEM((half, chunk), low),
            pltpu.VMEM((half, width), jnp.float32),
            pltpu.VMEM((half, width), jnp.float32),
            pltpu.SemaphoreType.DMA((steps,)),
            pltpu.SemaphoreType.DMA((steps,)),
        ],
        compiler_params=params(46),
        cost_estimate=pl.CostEstimate(
            flops=8 * half * width * hidden,
            bytes_accessed=4 * width * hidden,
            transcendentals=half * hidden,
        ),
        name="forward",
    )(recv, plan, w_in[0], w_out[0])
    ret = lax.all_to_all(
        ret.reshape(rows // PAIR, PAIR, width), "expert", split_axis=0, concat_axis=0, tiled=True
    ).reshape(rows, width)
    d_w_in, d_w_out = pl.pallas_call(
        grads_kernel,
        out_shape=(
            jax.ShapeDtypeStruct((width, hidden), low),
            jax.ShapeDtypeStruct((hidden, width), low),
        ),
        in_specs=[vmem] * 4,
        out_specs=(hbm,) * 2,
        scratch_shapes=[
            pltpu.VMEM((3, width, chunk), low),
            pltpu.VMEM((3, chunk, width), low),
            pltpu.SemaphoreType.DMA((3, 4)),
        ],
        compiler_params=params(24),
        cost_estimate=pl.CostEstimate(
            flops=4 * half * width * hidden,
            bytes_accessed=4 * width * hidden,
            transcendentals=0,
        ),
        name="grads",
    )(x_t, g_rows, act_t, d_pre)
    mixed, d_tokens, d_gates_t = pl.pallas_call(
        combine_kernel,
        out_shape=(
            jax.ShapeDtypeStruct((count, width), low),
            jax.ShapeDtypeStruct((count, width), low),
            jax.ShapeDtypeStruct((2, count), jnp.float32),
        ),
        compiler_params=params(12),
        name="combine",
    )(ret, pick, gate_cols, cotangent)
    return (mixed, d_tokens, jnp.transpose(d_gates_t, (1, 0)), d_w_in[None], d_w_out[None])


def solution(mesh):
    rows = P(("groups", "expert"), None)
    return jax.shard_map(
        per_device,
        mesh=mesh,
        in_specs=(rows, rows, rows, rows, P("expert", None, None), P("expert", None, None), rows),
        out_specs=(
            rows,
            rows,
            rows,
            P(("groups", "expert"), None, None),
            P(("groups", "expert"), None, None),
        ),
        check_vma=False,
    )
```

```python
import functools
import math

import jax
import jax.numpy as jnp
from jax import lax
from jax.experimental import pallas as pl
from jax.experimental.pallas import tpu as pltpu
from jax.sharding import PartitionSpec as P

EXPERTS = 16
CAP = 4
PAIR = 2 * CAP
EARLY = 128
ROWS_DIM = (((0,), (0,)), ((), ()))
LAST_DIM = (((1,), (1,)), ((), ()))


def gelu_parts(value):
    coef = math.sqrt(2.0 / math.pi)
    square = value * value
    hyper = jnp.tanh(coef * value * (1.0 + 0.044715 * square))
    half = 0.5 * (1.0 + hyper)
    slope = half + 0.5 * value * (1.0 - hyper * hyper) * coef * (1.0 + 3.0 * 0.044715 * square)
    return (value * half, slope)


def place_rows(ids_t, prio):
    count = ids_t.shape[1]
    first = ids_t[0:1, :]
    second = ids_t[1:2, :]
    stack = jnp.concatenate([first, second, prio, jnp.zeros((5, count), jnp.int32)], axis=0)
    columns = jnp.transpose(stack.astype(jnp.float32), (1, 0)).astype(jnp.int32)
    first_c, second_c, prio_c = columns[:, 0:1], columns[:, 1:2], columns[:, 2:3]
    ahead = prio_c < prio
    one = jnp.float32(1.0)
    zero = jnp.float32(0.0)
    slot_0 = jnp.sum(jnp.where((first_c == first) & ahead, one, zero), axis=0, keepdims=True)
    slot_1 = jnp.sum(
        jnp.where((first_c == second) | ((second_c == second) & ahead), one, zero),
        axis=0,
        keepdims=True,
    )
    slot_0 = slot_0.astype(jnp.int32)
    slot_1 = slot_1.astype(jnp.int32)
    place_0 = jnp.where(slot_0 < CAP, first * CAP + slot_0, -1)
    place_1 = jnp.where(slot_1 < CAP, second * CAP + slot_1, -1)
    return place_0, place_1


def dispatch_kernel(
    ids_hbm, prio_hbm, gates_hbm, tok_hbm, cot_hbm, w_in_hbm, w_out_hbm,
    send_ref, plan_ref, w_in_ref, w_out_ref,
    ids_ref, prio_ref, gates_ref, both_ref, sem,
):
    count = tok_hbm.shape[0]
    depth = w_in_ref.shape[1]
    pairs = (
        (ids_hbm, ids_ref),
        (prio_hbm, prio_ref),
        (gates_hbm, gates_ref),
        (tok_hbm, both_ref.at[0:count]),
        (cot_hbm, both_ref.at[count:2 * count]),
        (w_in_hbm.at[:, 0:depth], w_in_ref),
        (w_out_hbm.at[0:depth, :], w_out_ref),
    )
    copies = [pltpu.make_async_copy(*pair, sem.at[index]) for index, pair in enumerate(pairs)]
    for copy in copies:
        copy.start()
    for copy in copies[:3]:
        copy.wait()
    place_0, place_1 = place_rows(ids_ref[...], prio_ref[...])
    rows = EXPERTS * PAIR
    row = lax.broadcasted_iota(jnp.int32, (rows, count), 0)
    slot = row // PAIR * CAP + row % CAP
    is_x = row % PAIR < CAP
    hit_0 = slot == place_0
    hit_1 = slot == place_1
    hit = jnp.where(hit_0 | hit_1, 1.0, 0.0)
    pick = jnp.concatenate(
        [jnp.where(is_x, hit, 0.0), jnp.where(is_x, 0.0, hit)], axis=1
    ).astype(jnp.bfloat16)
    gate = jnp.where(hit_0, gates_ref[0:1, :], 0.0) + jnp.where(hit_1, gates_ref[1:2, :], 0.0)
    scale = jnp.sum(gate, axis=1, keepdims=True)
    scale = jnp.where(is_x[:, 0:1], 1.0, scale)
    plan_ref[...] = jnp.concatenate(
        [
            place_0.astype(jnp.float32),
            place_1.astype(jnp.float32),
            gates_ref[...],
            jnp.zeros((4, count), jnp.float32),
        ],
        axis=0,
    )
    for copy in copies[3:5]:
        copy.wait()
    found = jnp.dot(pick, both_ref[...], preferred_element_type=jnp.float32)
    send_ref[...] = (found * scale).astype(jnp.bfloat16)
    for copy in copies[5:]:
        copy.wait()


def tables(plan_ref, pick_ref, gate_ref):
    place_0 = plan_ref[0:1, :].astype(jnp.int32)
    place_1 = plan_ref[1:2, :].astype(jnp.int32)
    count = place_0.shape[1]
    rows = EXPERTS * PAIR
    row = lax.broadcasted_iota(jnp.int32, (rows, count), 0)
    slot = row // PAIR * CAP + row % CAP
    is_x = row % PAIR < CAP
    hit_0 = jnp.where(slot == place_0, 1.0, 0.0)
    hit_1 = jnp.where(slot == place_1, 1.0, 0.0)
    pick_0 = jnp.transpose(jnp.where(is_x, hit_0, 0.0), (1, 0))
    pick_1 = jnp.transpose(jnp.where(is_x, hit_1, 0.0), (1, 0))
    pick_b = jnp.transpose(jnp.where(is_x, 0.0, hit_0 + hit_1), (1, 0))
    pick_ref[...] = jnp.concatenate([pick_0, pick_1, pick_b], axis=0).astype(jnp.bfloat16)
    gate_ref[...] = jnp.transpose(plan_ref[...], (1, 0))


def row_picks(rows):
    half = rows // 2
    out = lax.broadcasted_iota(jnp.int32, (half, rows), 0)
    col = lax.broadcasted_iota(jnp.int32, (half, rows), 1)
    source = out // CAP * PAIR + out % CAP
    x_pick = jnp.where(col == source, 1.0, 0.0).astype(jnp.bfloat16)
    g_pick = jnp.where(col == source + CAP, 1.0, 0.0).astype(jnp.bfloat16)
    return x_pick, g_pick


def forward_kernel(
    steps, recv_ref, plan_ref, w_in_0, w_out_0, w_in_hbm, w_out_hbm,
    ret_ref, x_t_ref, g_ref, act_ref, d_pre_ref, pick_ref, gate_ref, d_out_hbm,
    w_in_ref, w_out_ref, x_ref, act_t_ref, stage, out_acc, back_acc, sem_in, sem_out, sem_left,
):
    width, depth = w_in_0.shape
    low = jnp.bfloat16

    def copies(step):
        cols = pl.ds(pl.multiple_of(step * depth, depth), depth)
        slot = step - 1
        return (
            pltpu.make_async_copy(w_in_hbm.at[:, cols], w_in_ref.at[slot], sem_in.at[slot]),
            pltpu.make_async_copy(w_out_hbm.at[cols, :], w_out_ref.at[slot], sem_out.at[slot]),
        )

    def leave(step):
        rows = pl.ds(pl.multiple_of(step * depth, depth), EARLY)
        slot = lax.rem(step, 2)
        return pltpu.make_async_copy(stage.at[slot], d_out_hbm.at[rows, :], sem_left.at[slot])

    def begin(step, carry):
        for copy in copies(step):
            copy.start()
        return carry

    lax.fori_loop(1, steps, begin, 0)
    recv = recv_ref[...]
    x_pick, g_pick = row_picks(recv.shape[0])
    x_rows = jnp.dot(x_pick, recv, preferred_element_type=jnp.float32)
    x_ref[...] = x_rows.astype(low)
    g_ref[...] = jnp.dot(g_pick, recv, preferred_element_type=jnp.float32).astype(low)
    out_acc[...] = jnp.zeros_like(out_acc)
    back_acc[...] = jnp.zeros_like(back_acc)

    def weights(step):
        if isinstance(step, int) and step == 0:
            return w_in_0, w_out_0
        return w_in_ref.at[step - 1], w_out_ref.at[step - 1]

    def front_dots(step, found):
        w_first, w_second = weights(step)
        for first in range(0, depth, 256):
            cols = slice(first, min(first + 256, depth))
            pre = []

            def one(cols=cols, pre=pre):
                pre.append(
                    jnp.dot(
                        x_ref[...], w_first[:, cols], preferred_element_type=jnp.float32
                    )
                )

            def two(cols=cols, pre=pre):
                d_act = lax.dot_general(
                    g_ref[...],
                    w_second[cols, :],
                    LAST_DIM,
                    preferred_element_type=jnp.float32,
                )
                found.append((cols, pre[0], d_act))

            yield one
            yield two

    def back_dots(step, act, d_pre):
        w_first, w_second = weights(step)
        for first in range(0, width, 256):
            cols = slice(first, min(first + 256, width))

            def one(cols=cols):
                out_acc[:, cols] += jnp.dot(
                    act, w_second[:, cols], preferred_element_type=jnp.float32
                )

            def two(cols=cols):
                back_acc[:, cols] += lax.dot_general(
                    d_pre,
                    w_first[cols, :],
                    LAST_DIM,
                    preferred_element_type=jnp.float32,
                )

            yield one
            yield two

    def grad_dots(step, act_t):
        slot = lax.rem(step, 2)
        for first in range(0, width, 256):
            cols = slice(first, min(first + 256, width))

            def one(cols=cols):
                stage[slot, :, cols] = jnp.dot(
                    act_t, g_ref[:, cols], preferred_element_type=jnp.float32
                ).astype(low)

            yield one

    def middle(step, found):
        for cols, pre, d_act in found:
            value, slope = gelu_parts(pre)
            act_ref[step, :, cols] = value.astype(low)
            d_pre_ref[step, :, cols] = (d_act * slope).astype(low)
            if cols.start == 0:
                act_t_ref[...] = jnp.transpose(value[:, 0:EARLY], (1, 0)).astype(low)

    def run(first, second):
        done = 0
        for index, thunk in enumerate(first):
            thunk()
            due = (index + 1) * len(second) // len(first)
            for other in second[done:due]:
                other()
            done = due

    def both(step):
        for copy in copies(step):
            copy.wait()
        act, act_t, d_pre = act_ref[step - 1], act_t_ref[...], d_pre_ref[step - 1]
        found = []
        run(
            [*front_dots(step, found), *back_dots(step - 1, act, d_pre)],
            [*grad_dots(step - 1, act_t)],
        )
        middle(step, found)
        leave(step - 1).start()

    found = []
    for thunk in front_dots(0, found):
        thunk()
    middle(0, found)
    if steps > 1:
        both(1)
    x_t_ref[...] = jnp.transpose(x_rows, (1, 0)).astype(low)
    tables(plan_ref, pick_ref, gate_ref)

    def body(step, carry):
        @pl.when(step > 2)
        def _():
            leave(step - 3).wait()

        both(step)
        return carry

    lax.fori_loop(2, steps, body, 0)
    last = steps - 1
    if steps > 2:
        leave(last - 2).wait()
    run(
        [*back_dots(last, act_ref[last], d_pre_ref[last])],
        [*grad_dots(last, act_t_ref[...])],
    )
    leave(last).start()
    ret = lax.dot_general(
        x_pick, out_acc[...].astype(low), ROWS_DIM, preferred_element_type=jnp.float32
    ) + lax.dot_general(
        g_pick, back_acc[...].astype(low), ROWS_DIM, preferred_element_type=jnp.float32
    )
    ret_ref[...] = ret.astype(low)
    if steps > 1:
        leave(last - 1).wait()
    leave(last).wait()


def product(out_ref, left, right, tall, wide):
    rows, cols = out_ref.shape
    for col in range(0, cols, wide):
        col_end = min(col + wide, cols)
        for row in range(0, rows, tall):
            row_end = min(row + tall, rows)
            out_ref[row:row_end, col:col_end] = jnp.dot(
                left[row:row_end], right[:, col:col_end], preferred_element_type=jnp.float32
            ).astype(jnp.bfloat16)


def grads_kernel(
    x_t_ref, g_ref, act_ref, d_pre_ref, _, d_in_hbm, d_out_hbm, d_in_stage, d_out_stage, sem
):
    steps, _, depth = act_ref.shape
    width = x_t_ref.shape[0]
    slots = d_in_stage.shape[0]
    later = depth - EARLY

    def leave(step):
        slot = lax.rem(step, slots)
        cols = pl.ds(pl.multiple_of(step * depth, depth), depth)
        pairs = []
        for index in range(2):
            some = pl.ds(index * (width // 2), width // 2)
            pairs.append((d_in_stage.at[slot, some], d_in_hbm.at[some, cols]))
        for index in range(2):
            first = index * (later // 2)
            here = pl.ds(first, later // 2)
            there = pl.ds(pl.multiple_of(step * depth + EARLY + first, 64), later // 2)
            pairs.append((d_out_stage.at[slot, here], d_out_hbm.at[there]))
        return [
            pltpu.make_async_copy(*pair, sem.at[slot, index]) for index, pair in enumerate(pairs)
        ]

    def work(step, carry):
        @pl.when(step >= slots)
        def _():
            for copy in leave(step - slots):
                copy.wait()

        slot = lax.rem(step, slots)
        copies = leave(step)
        act_t = jnp.transpose(act_ref[step].astype(jnp.float32), (1, 0)).astype(jnp.bfloat16)
        product(d_in_stage.at[slot], x_t_ref[...], d_pre_ref[step], 208, 256)
        for copy in copies[:2]:
            copy.start()
        product(d_out_stage.at[slot], act_t[EARLY:], g_ref[...], 192, 256)
        for copy in copies[2:]:
            copy.start()
        return carry

    lax.fori_loop(0, steps, work, 0)
    for step in range(max(steps - slots, 0), steps):
        for copy in leave(step):
            copy.wait()


def combine_kernel(ret_ref, pick_ref, gate_ref, cot_ref, mixed_ref, d_tok_ref, d_gate_ref):
    count = cot_ref.shape[0]
    rows = pick_ref.shape[1]
    found = None
    for first in range(0, ret_ref.shape[0], rows):
        part = jnp.dot(
            pick_ref[...], ret_ref[first:first + rows, :], preferred_element_type=jnp.float32
        )
        found = part if found is None else found + part
    o_0, o_1 = found[:count], found[count:2 * count]
    mixed_ref[...] = (gate_ref[:, 2:3] * o_0 + gate_ref[:, 3:4] * o_1).astype(jnp.bfloat16)
    d_tok_ref[...] = found[2 * count:].astype(jnp.bfloat16)
    cot = cot_ref[...].astype(jnp.float32)
    d_0 = jnp.sum(cot * o_0, axis=1, keepdims=True)
    d_1 = jnp.sum(cot * o_1, axis=1, keepdims=True)
    lane = lax.broadcasted_iota(jnp.int32, (count, 8), 1)
    both = jnp.where(lane == 0, d_0, jnp.where(lane == 1, d_1, 0.0))
    d_gate_ref[...] = jnp.transpose(both, (1, 0))[0:2, :]


def params(mib):
    return pltpu.CompilerParams(vmem_limit_bytes=mib * 1024 * 1024)


def chunk_of(hidden, want):
    return max(size for size in range(128, want + 1, 128) if hidden % size == 0)


def per_device(tokens, expert_ids, priority, gates, w_in, w_out, cotangent):
    count, width = tokens.shape
    repl = lax.axis_size("expert") // EXPERTS
    slots = EXPERTS * PAIR
    hidden = w_in.shape[2]
    ids_t = jnp.transpose(expert_ids, (1, 0))
    gates_t = jnp.transpose(gates, (1, 0))
    low = jnp.bfloat16
    vmem = pl.BlockSpec(memory_space=pltpu.VMEM)
    hbm = pl.BlockSpec(memory_space=pl.ANY)
    chunk = chunk_of(hidden, 512)
    steps = hidden // chunk
    send, plan, w_in_0, w_out_0 = pl.pallas_call(
        dispatch_kernel,
        out_shape=(
            pltpu.VMEM((slots, width), low),
            pltpu.VMEM((8, count), jnp.float32),
            pltpu.VMEM((width, chunk), low),
            pltpu.VMEM((chunk, width), low),
        ),
        in_specs=[hbm] * 7,
        out_specs=(vmem,) * 4,
        scratch_shapes=[
            pltpu.VMEM((2, count), jnp.int32),
            pltpu.VMEM((1, count), jnp.int32),
            pltpu.VMEM((2, count), jnp.float32),
            pltpu.VMEM((2 * count, width), low),
            pltpu.SemaphoreType.DMA((7,)),
        ],
        compiler_params=params(50),
        name="dispatch",
    )(*(pltpu.with_memory_space_constraint(array, pltpu.HBM) for array in (
        ids_t, priority, gates_t, tokens, cotangent, w_in[0], w_out[0]
    )))
    send = jnp.tile(send.reshape(EXPERTS, PAIR, width), (repl, 1, 1))
    recv = lax.all_to_all(send, "expert", split_axis=0, concat_axis=0, tiled=True)
    rows = recv.shape[0] * PAIR
    recv = recv.reshape(rows, width)
    half = rows // 2
    ret, x_t, g_rows, act, d_pre, pick, gate_cols, d_w_out = pl.pallas_call(
        functools.partial(forward_kernel, steps),
        out_shape=(
            pltpu.VMEM((rows, width), low),
            jax.ShapeDtypeStruct((width, half), low),
            jax.ShapeDtypeStruct((half, width), low),
            jax.ShapeDtypeStruct((steps, half, chunk), low),
            jax.ShapeDtypeStruct((steps, half, chunk), low),
            jax.ShapeDtypeStruct((3 * count, slots), low),
            jax.ShapeDtypeStruct((count, 8), jnp.float32),
            jax.ShapeDtypeStruct((hidden, width), low),
        ),
        in_specs=[vmem] * 4 + [hbm] * 2,
        out_specs=(vmem,) * 7 + (hbm,),
        scratch_shapes=[
            pltpu.VMEM((max(steps - 1, 1), width, chunk), low),
            pltpu.VMEM((max(steps - 1, 1), chunk, width), low),
            pltpu.VMEM((half, width), low),
            pltpu.VMEM((EARLY, half), low),
            pltpu.VMEM((2, EARLY, width), low),
            pltpu.VMEM((half, width), jnp.float32),
            pltpu.VMEM((half, width), jnp.float32),
            pltpu.SemaphoreType.DMA((max(steps - 1, 1),)),
            pltpu.SemaphoreType.DMA((max(steps - 1, 1),)),
            pltpu.SemaphoreType.DMA((2,)),
        ],
        compiler_params=params(43),
        cost_estimate=pl.CostEstimate(
            flops=8 * half * width * hidden,
            bytes_accessed=4 * width * hidden,
            transcendentals=half * hidden,
        ),
        name="forward",
    )(recv, plan, w_in_0, w_out_0, w_in[0], w_out[0])
    ret = lax.all_to_all(
        ret.reshape(rows // PAIR, PAIR, width), "expert", split_axis=0, concat_axis=0, tiled=True
    ).reshape(rows, width)
    d_w_in, d_w_out = pl.pallas_call(
        grads_kernel,
        out_shape=(
            jax.ShapeDtypeStruct((width, hidden), low),
            jax.ShapeDtypeStruct((hidden, width), low),
        ),
        in_specs=[vmem] * 4 + [hbm],
        out_specs=(hbm,) * 2,
        input_output_aliases={4: 1},
        scratch_shapes=[
            pltpu.VMEM((3, width, chunk), low),
            pltpu.VMEM((3, chunk - EARLY, width), low),
            pltpu.SemaphoreType.DMA((3, 4)),
        ],
        compiler_params=params(24),
        cost_estimate=pl.CostEstimate(
            flops=4 * half * width * hidden,
            bytes_accessed=4 * width * hidden,
            transcendentals=0,
        ),
        name="grads",
    )(x_t, g_rows, act, d_pre, d_w_out)
    mixed, d_tokens, d_gates_t = pl.pallas_call(
        combine_kernel,
        out_shape=(
            jax.ShapeDtypeStruct((count, width), low),
            jax.ShapeDtypeStruct((count, width), low),
            jax.ShapeDtypeStruct((2, count), jnp.float32),
        ),
        compiler_params=params(12),
        name="combine",
    )(ret, pick, gate_cols, cotangent)
    return (mixed, d_tokens, jnp.transpose(d_gates_t, (1, 0)), d_w_in[None], d_w_out[None])


def solution(mesh):
    rows = P(("groups", "expert"), None)
    return jax.shard_map(
        per_device,
        mesh=mesh,
        in_specs=(rows, rows, rows, rows, P("expert", None, None), P("expert", None, None), rows),
        out_specs=(
            rows,
            rows,
            rows,
            P(("groups", "expert"), None, None),
            P(("groups", "expert"), None, None),
        ),
        check_vma=False,
    )
```

```python
import functools
import math

import jax
import jax.numpy as jnp
from jax import lax
from jax.experimental import pallas as pl
from jax.experimental.pallas import tpu as pltpu
from jax.sharding import PartitionSpec as P

EXPERTS = 16
CAP = 4
PAIR = 2 * CAP
EARLY = 128
ROWS_DIM = (((0,), (0,)), ((), ()))
LAST_DIM = (((1,), (1,)), ((), ()))


def gelu_parts(value):
    coef = math.sqrt(2.0 / math.pi)
    square = value * value
    hyper = jnp.tanh(coef * value * (1.0 + 0.044715 * square))
    half = 0.5 * (1.0 + hyper)
    slope = half + 0.5 * value * (1.0 - hyper * hyper) * coef * (1.0 + 3.0 * 0.044715 * square)
    return (value * half, slope)


def place_rows(ids_t, prio):
    count = ids_t.shape[1]
    first = ids_t[0:1, :]
    second = ids_t[1:2, :]
    stack = jnp.concatenate([first, second, prio, jnp.zeros((5, count), jnp.int32)], axis=0)
    columns = jnp.transpose(stack.astype(jnp.float32), (1, 0)).astype(jnp.int32)
    first_c, second_c, prio_c = columns[:, 0:1], columns[:, 1:2], columns[:, 2:3]
    ahead = prio_c < prio
    one = jnp.float32(1.0)
    zero = jnp.float32(0.0)
    slot_0 = jnp.sum(jnp.where((first_c == first) & ahead, one, zero), axis=0, keepdims=True)
    slot_1 = jnp.sum(
        jnp.where((first_c == second) | ((second_c == second) & ahead), one, zero),
        axis=0,
        keepdims=True,
    )
    slot_0 = slot_0.astype(jnp.int32)
    slot_1 = slot_1.astype(jnp.int32)
    place_0 = jnp.where(slot_0 < CAP, first * CAP + slot_0, -1)
    place_1 = jnp.where(slot_1 < CAP, second * CAP + slot_1, -1)
    return place_0, place_1


def dispatch_kernel(
    ids_hbm, prio_hbm, gates_hbm, tok_hbm, cot_hbm, w_in_hbm, w_out_hbm,
    send_ref, plan_ref, w_in_ref, w_out_ref,
    ids_ref, prio_ref, gates_ref, both_ref, sem,
):
    count = tok_hbm.shape[0]
    depth = w_in_ref.shape[1]
    pairs = (
        (ids_hbm, ids_ref),
        (prio_hbm, prio_ref),
        (gates_hbm, gates_ref),
        (tok_hbm, both_ref.at[0:count]),
        (cot_hbm, both_ref.at[count:2 * count]),
        (w_in_hbm.at[:, 0:depth], w_in_ref),
        (w_out_hbm.at[0:depth, :], w_out_ref),
    )
    copies = [pltpu.make_async_copy(*pair, sem.at[index]) for index, pair in enumerate(pairs)]
    for copy in copies:
        copy.start()
    for copy in copies[:3]:
        copy.wait()
    place_0, place_1 = place_rows(ids_ref[...], prio_ref[...])
    rows = EXPERTS * PAIR
    row = lax.broadcasted_iota(jnp.int32, (rows, count), 0)
    slot = row // PAIR * CAP + row % CAP
    is_x = row % PAIR < CAP
    hit_0 = slot == place_0
    hit_1 = slot == place_1
    hit = jnp.where(hit_0 | hit_1, 1.0, 0.0)
    pick = jnp.concatenate(
        [jnp.where(is_x, hit, 0.0), jnp.where(is_x, 0.0, hit)], axis=1
    ).astype(jnp.bfloat16)
    gate = jnp.where(hit_0, gates_ref[0:1, :], 0.0) + jnp.where(hit_1, gates_ref[1:2, :], 0.0)
    scale = jnp.sum(gate, axis=1, keepdims=True)
    scale = jnp.where(is_x[:, 0:1], 1.0, scale)
    plan_ref[...] = jnp.concatenate(
        [
            place_0.astype(jnp.float32),
            place_1.astype(jnp.float32),
            gates_ref[...],
            jnp.zeros((4, count), jnp.float32),
        ],
        axis=0,
    )
    for copy in copies[3:5]:
        copy.wait()
    found = jnp.dot(pick, both_ref[...], preferred_element_type=jnp.float32)
    send_ref[...] = (found * scale).astype(jnp.bfloat16)
    for copy in copies[5:]:
        copy.wait()


def tables(plan_ref, pick_ref, gate_ref):
    place_0 = plan_ref[0:1, :].astype(jnp.int32)
    place_1 = plan_ref[1:2, :].astype(jnp.int32)
    count = place_0.shape[1]
    rows = EXPERTS * PAIR
    row = lax.broadcasted_iota(jnp.int32, (rows, count), 0)
    slot = row // PAIR * CAP + row % CAP
    is_x = row % PAIR < CAP
    hit_0 = jnp.where(slot == place_0, 1.0, 0.0)
    hit_1 = jnp.where(slot == place_1, 1.0, 0.0)
    pick_0 = jnp.transpose(jnp.where(is_x, hit_0, 0.0), (1, 0))
    pick_1 = jnp.transpose(jnp.where(is_x, hit_1, 0.0), (1, 0))
    pick_b = jnp.transpose(jnp.where(is_x, 0.0, hit_0 + hit_1), (1, 0))
    pick_ref[...] = jnp.concatenate([pick_0, pick_1, pick_b], axis=0).astype(jnp.bfloat16)
    gate_ref[...] = jnp.transpose(plan_ref[...], (1, 0))


def row_picks(rows):
    half = rows // 2
    out = lax.broadcasted_iota(jnp.int32, (half, rows), 0)
    col = lax.broadcasted_iota(jnp.int32, (half, rows), 1)
    source = out // CAP * PAIR + out % CAP
    x_pick = jnp.where(col == source, 1.0, 0.0).astype(jnp.bfloat16)
    g_pick = jnp.where(col == source + CAP, 1.0, 0.0).astype(jnp.bfloat16)
    return x_pick, g_pick


def forward_kernel(
    steps, recv_ref, plan_ref, w_in_0, w_out_0, w_in_hbm, w_out_hbm,
    ret_ref, x_t_ref, g_ref, act_ref, d_pre_ref, pick_ref, gate_ref, d_out_hbm,
    w_in_ref, w_out_ref, x_ref, act_t_ref, stage, out_acc, back_acc, sem_in, sem_out, sem_left,
):
    width, depth = w_in_0.shape
    low = jnp.bfloat16

    def copies(step):
        cols = pl.ds(pl.multiple_of(step * depth, depth), depth)
        slot = step - 1
        return (
            pltpu.make_async_copy(w_in_hbm.at[:, cols], w_in_ref.at[slot], sem_in.at[slot]),
            pltpu.make_async_copy(w_out_hbm.at[cols, :], w_out_ref.at[slot], sem_out.at[slot]),
        )

    def leave(step):
        rows = pl.ds(pl.multiple_of(step * depth, depth), EARLY)
        slot = lax.rem(step, 2)
        return pltpu.make_async_copy(stage.at[slot], d_out_hbm.at[rows, :], sem_left.at[slot])

    def begin(step, carry):
        for copy in copies(step):
            copy.start()
        return carry

    lax.fori_loop(1, steps, begin, 0)
    recv = recv_ref[...]
    x_pick, g_pick = row_picks(recv.shape[0])
    x_rows = jnp.dot(x_pick, recv, preferred_element_type=jnp.float32)
    x_ref[...] = x_rows.astype(low)
    g_ref[...] = jnp.dot(g_pick, recv, preferred_element_type=jnp.float32).astype(low)
    out_acc[...] = jnp.zeros_like(out_acc)
    back_acc[...] = jnp.zeros_like(back_acc)

    def weights(step):
        if isinstance(step, int) and step == 0:
            return w_in_0, w_out_0
        return w_in_ref.at[step - 1], w_out_ref.at[step - 1]

    def front_dots(step, found):
        w_first, w_second = weights(step)
        for first in range(0, depth, 256):
            cols = slice(first, min(first + 256, depth))
            pre = []

            def one(cols=cols, pre=pre):
                pre.append(
                    jnp.dot(
                        x_ref[...], w_first[:, cols], preferred_element_type=jnp.float32
                    )
                )

            def two(cols=cols, pre=pre):
                d_act = lax.dot_general(
                    g_ref[...],
                    w_second[cols, :],
                    LAST_DIM,
                    preferred_element_type=jnp.float32,
                )
                found.append((cols, pre[0], d_act))

            yield one
            yield two

    def back_dots(step, act, d_pre):
        w_first, w_second = weights(step)
        for first in range(0, width, 256):
            cols = slice(first, min(first + 256, width))

            def one(cols=cols):
                out_acc[:, cols] += jnp.dot(
                    act, w_second[:, cols], preferred_element_type=jnp.float32
                )

            def two(cols=cols):
                back_acc[:, cols] += lax.dot_general(
                    d_pre,
                    w_first[cols, :],
                    LAST_DIM,
                    preferred_element_type=jnp.float32,
                )

            yield one
            yield two

    def grad_dots(step, act_t):
        slot = lax.rem(step, 2)
        for first in range(0, width, 256):
            cols = slice(first, min(first + 256, width))

            def one(cols=cols):
                stage[slot, :, cols] = jnp.dot(
                    act_t, g_ref[:, cols], preferred_element_type=jnp.float32
                ).astype(low)

            yield one

    def middle(step, found):
        for cols, pre, d_act in found:
            value, slope = gelu_parts(pre)
            act_ref[step, :, cols] = value.astype(low)
            d_pre_ref[step, :, cols] = (d_act * slope).astype(low)
            if cols.start == 0:
                act_t_ref[...] = jnp.transpose(value[:, 0:EARLY], (1, 0)).astype(low)

    def run(first, second):
        done = 0
        for index, thunk in enumerate(first):
            thunk()
            due = (index + 1) * len(second) // len(first)
            for other in second[done:due]:
                other()
            done = due

    def both(step):
        for copy in copies(step):
            copy.wait()
        act, act_t, d_pre = act_ref[step - 1], act_t_ref[...], d_pre_ref[step - 1]
        found = []
        fronts = [*front_dots(step, found)]
        backs = [*back_dots(step - 1, act, d_pre)]
        blocks = len(fronts) // 2
        share = len(backs) // (blocks + 1)
        order = []
        for block in range(blocks):
            order += fronts[2 * block:2 * block + 2]
            order += backs[share * block:share * (block + 1)]
            order.append(lambda block=block: middle(step, found[block:block + 1]))
        order += backs[share * blocks:]
        run(order, [*grad_dots(step - 1, act_t)])
        leave(step - 1).start()

    found = []
    for thunk in front_dots(0, found):
        thunk()
    middle(0, found)
    if steps > 1:
        both(1)
    x_t_ref[...] = jnp.transpose(x_rows, (1, 0)).astype(low)
    tables(plan_ref, pick_ref, gate_ref)

    def body(step, carry):
        @pl.when(step > 2)
        def _():
            leave(step - 3).wait()

        both(step)
        return carry

    lax.fori_loop(2, steps, body, 0)
    last = steps - 1
    if steps > 2:
        leave(last - 2).wait()
    run(
        [*back_dots(last, act_ref[last], d_pre_ref[last])],
        [*grad_dots(last, act_t_ref[...])],
    )
    leave(last).start()
    ret = lax.dot_general(
        x_pick, out_acc[...].astype(low), ROWS_DIM, preferred_element_type=jnp.float32
    ) + lax.dot_general(
        g_pick, back_acc[...].astype(low), ROWS_DIM, preferred_element_type=jnp.float32
    )
    ret_ref[...] = ret.astype(low)
    if steps > 1:
        leave(last - 1).wait()
    leave(last).wait()


def product(out_ref, left, right, tall, wide):
    rows, cols = out_ref.shape
    for col in range(0, cols, wide):
        col_end = min(col + wide, cols)
        for row in range(0, rows, tall):
            row_end = min(row + tall, rows)
            out_ref[row:row_end, col:col_end] = jnp.dot(
                left[row:row_end], right[:, col:col_end], preferred_element_type=jnp.float32
            ).astype(jnp.bfloat16)


def grads_kernel(
    x_t_ref, g_ref, act_ref, d_pre_ref, _, d_in_hbm, d_out_hbm, d_in_stage, d_out_stage, sem
):
    steps, _, depth = act_ref.shape
    width = x_t_ref.shape[0]
    slots = d_in_stage.shape[0]
    later = depth - EARLY

    def leave(step):
        slot = lax.rem(step, slots)
        cols = pl.ds(pl.multiple_of(step * depth, depth), depth)
        pairs = []
        for index in range(2):
            some = pl.ds(index * (width // 2), width // 2)
            pairs.append((d_in_stage.at[slot, some], d_in_hbm.at[some, cols]))
        for index in range(2):
            first = index * (later // 2)
            here = pl.ds(first, later // 2)
            there = pl.ds(pl.multiple_of(step * depth + EARLY + first, 64), later // 2)
            pairs.append((d_out_stage.at[slot, here], d_out_hbm.at[there]))
        return [
            pltpu.make_async_copy(*pair, sem.at[slot, index]) for index, pair in enumerate(pairs)
        ]

    def work(step, carry):
        @pl.when(step >= slots)
        def _():
            for copy in leave(step - slots):
                copy.wait()

        slot = lax.rem(step, slots)
        copies = leave(step)
        act_t = jnp.transpose(act_ref[step].astype(jnp.float32), (1, 0)).astype(jnp.bfloat16)
        product(d_in_stage.at[slot], x_t_ref[...], d_pre_ref[step], 208, 256)
        for copy in copies[:2]:
            copy.start()
        product(d_out_stage.at[slot], act_t[EARLY:], g_ref[...], 192, 256)
        for copy in copies[2:]:
            copy.start()
        return carry

    lax.fori_loop(0, steps, work, 0)
    for step in range(max(steps - slots, 0), steps):
        for copy in leave(step):
            copy.wait()


def combine_kernel(
    ret_ref, pick_ref, gate_ref, cot_ref, mixed_hbm, d_tok_hbm, d_gate_ref,
    mixed_ref, d_tok_ref, sem,
):
    count, width = cot_ref.shape
    rows = pick_ref.shape[1]
    d_0 = jnp.zeros((count, 1), jnp.float32)
    d_1 = jnp.zeros((count, 1), jnp.float32)
    copies = []
    for block, left in enumerate(range(0, width, 512)):
        cols = slice(left, min(left + 512, width))
        found = None
        for first in range(0, ret_ref.shape[0], rows):
            part = jnp.dot(
                pick_ref[...],
                ret_ref[first:first + rows, cols],
                preferred_element_type=jnp.float32,
            )
            found = part if found is None else found + part
        o_0, o_1 = found[:count], found[count:2 * count]
        mixed_ref[:, cols] = (gate_ref[:, 2:3] * o_0 + gate_ref[:, 3:4] * o_1).astype(jnp.bfloat16)
        d_tok_ref[:, cols] = found[2 * count:].astype(jnp.bfloat16)
        copies += [
            pltpu.make_async_copy(mixed_ref.at[:, cols], mixed_hbm.at[:, cols], sem.at[block, 0]),
            pltpu.make_async_copy(d_tok_ref.at[:, cols], d_tok_hbm.at[:, cols], sem.at[block, 1]),
        ]
        for copy in copies[-2:]:
            copy.start()
        cot = cot_ref[:, cols].astype(jnp.float32)
        d_0 += jnp.sum(cot * o_0, axis=1, keepdims=True)
        d_1 += jnp.sum(cot * o_1, axis=1, keepdims=True)
    lane = lax.broadcasted_iota(jnp.int32, (count, 8), 1)
    both = jnp.where(lane == 0, d_0, jnp.where(lane == 1, d_1, 0.0))
    d_gate_ref[...] = jnp.transpose(both, (1, 0))[0:2, :]
    for copy in copies:
        copy.wait()


def params(mib):
    return pltpu.CompilerParams(vmem_limit_bytes=mib * 1024 * 1024)


def chunk_of(hidden, want):
    return max(size for size in range(128, want + 1, 128) if hidden % size == 0)


def per_device(tokens, expert_ids, priority, gates, w_in, w_out, cotangent):
    count, width = tokens.shape
    repl = lax.axis_size("expert") // EXPERTS
    slots = EXPERTS * PAIR
    hidden = w_in.shape[2]
    ids_t = jnp.transpose(expert_ids, (1, 0))
    gates_t = jnp.transpose(gates, (1, 0))
    low = jnp.bfloat16
    vmem = pl.BlockSpec(memory_space=pltpu.VMEM)
    hbm = pl.BlockSpec(memory_space=pl.ANY)
    chunk = chunk_of(hidden, 512)
    steps = hidden // chunk
    send, plan, w_in_0, w_out_0 = pl.pallas_call(
        dispatch_kernel,
        out_shape=(
            pltpu.VMEM((slots, width), low),
            pltpu.VMEM((8, count), jnp.float32),
            pltpu.VMEM((width, chunk), low),
            pltpu.VMEM((chunk, width), low),
        ),
        in_specs=[hbm] * 7,
        out_specs=(vmem,) * 4,
        scratch_shapes=[
            pltpu.VMEM((2, count), jnp.int32),
            pltpu.VMEM((1, count), jnp.int32),
            pltpu.VMEM((2, count), jnp.float32),
            pltpu.VMEM((2 * count, width), low),
            pltpu.SemaphoreType.DMA((7,)),
        ],
        compiler_params=params(50),
        name="dispatch",
    )(*(pltpu.with_memory_space_constraint(array, pltpu.HBM) for array in (
        ids_t, priority, gates_t, tokens, cotangent, w_in[0], w_out[0]
    )))
    send = jnp.tile(send.reshape(EXPERTS, PAIR, width), (repl, 1, 1))
    recv = lax.all_to_all(send, "expert", split_axis=0, concat_axis=0, tiled=True)
    rows = recv.shape[0] * PAIR
    recv = recv.reshape(rows, width)
    half = rows // 2
    ret, x_t, g_rows, act, d_pre, pick, gate_cols, d_w_out = pl.pallas_call(
        functools.partial(forward_kernel, steps),
        out_shape=(
            pltpu.VMEM((rows, width), low),
            jax.ShapeDtypeStruct((width, half), low),
            jax.ShapeDtypeStruct((half, width), low),
            jax.ShapeDtypeStruct((steps, half, chunk), low),
            jax.ShapeDtypeStruct((steps, half, chunk), low),
            jax.ShapeDtypeStruct((3 * count, slots), low),
            jax.ShapeDtypeStruct((count, 8), jnp.float32),
            jax.ShapeDtypeStruct((hidden, width), low),
        ),
        in_specs=[vmem] * 4 + [hbm] * 2,
        out_specs=(vmem,) * 7 + (hbm,),
        scratch_shapes=[
            pltpu.VMEM((max(steps - 1, 1), width, chunk), low),
            pltpu.VMEM((max(steps - 1, 1), chunk, width), low),
            pltpu.VMEM((half, width), low),
            pltpu.VMEM((EARLY, half), low),
            pltpu.VMEM((2, EARLY, width), low),
            pltpu.VMEM((half, width), jnp.float32),
            pltpu.VMEM((half, width), jnp.float32),
            pltpu.SemaphoreType.DMA((max(steps - 1, 1),)),
            pltpu.SemaphoreType.DMA((max(steps - 1, 1),)),
            pltpu.SemaphoreType.DMA((2,)),
        ],
        compiler_params=params(43),
        cost_estimate=pl.CostEstimate(
            flops=8 * half * width * hidden,
            bytes_accessed=4 * width * hidden,
            transcendentals=half * hidden,
        ),
        name="forward",
    )(recv, plan, w_in_0, w_out_0, w_in[0], w_out[0])
    ret = lax.all_to_all(
        ret.reshape(rows // PAIR, PAIR, width), "expert", split_axis=0, concat_axis=0, tiled=True
    ).reshape(rows, width)
    d_w_in, d_w_out = pl.pallas_call(
        grads_kernel,
        out_shape=(
            jax.ShapeDtypeStruct((width, hidden), low),
            jax.ShapeDtypeStruct((hidden, width), low),
        ),
        in_specs=[vmem] * 4 + [hbm],
        out_specs=(hbm,) * 2,
        input_output_aliases={4: 1},
        scratch_shapes=[
            pltpu.VMEM((3, width, chunk), low),
            pltpu.VMEM((3, chunk - EARLY, width), low),
            pltpu.SemaphoreType.DMA((3, 4)),
        ],
        compiler_params=params(24),
        cost_estimate=pl.CostEstimate(
            flops=4 * half * width * hidden,
            bytes_accessed=4 * width * hidden,
            transcendentals=0,
        ),
        name="grads",
    )(x_t, g_rows, act, d_pre, d_w_out)
    mixed, d_tokens, d_gates_t = pl.pallas_call(
        combine_kernel,
        out_shape=(
            jax.ShapeDtypeStruct((count, width), low),
            jax.ShapeDtypeStruct((count, width), low),
            jax.ShapeDtypeStruct((2, count), jnp.float32),
        ),
        in_specs=[vmem] * 4,
        out_specs=(hbm, hbm, vmem),
        scratch_shapes=[
            pltpu.VMEM((count, width), low),
            pltpu.VMEM((count, width), low),
            pltpu.SemaphoreType.DMA((pl.cdiv(width, 512), 2)),
        ],
        compiler_params=params(12),
        name="combine",
    )(ret, pick, gate_cols, cotangent)
    return (mixed, d_tokens, jnp.transpose(d_gates_t, (1, 0)), d_w_in[None], d_w_out[None])


def solution(mesh):
    rows = P(("groups", "expert"), None)
    return jax.shard_map(
        per_device,
        mesh=mesh,
        in_specs=(rows, rows, rows, rows, P("expert", None, None), P("expert", None, None), rows),
        out_specs=(
            rows,
            rows,
            rows,
            P(("groups", "expert"), None, None),
            P(("groups", "expert"), None, None),
        ),
        check_vma=False,
    )
```

```python
import functools
import math

import jax
import jax.numpy as jnp
from jax import lax
from jax.experimental import pallas as pl
from jax.experimental.pallas import tpu as pltpu
from jax.sharding import PartitionSpec as P

EXPERTS = 16
CAP = 4
PAIR = 2 * CAP
EARLY = 128
ROWS_DIM = (((0,), (0,)), ((), ()))
LAST_DIM = (((1,), (1,)), ((), ()))


def gelu_parts(value):
    coef = math.sqrt(2.0 / math.pi)
    square = value * value
    hyper = jnp.tanh(coef * value * (1.0 + 0.044715 * square))
    half = 0.5 * (1.0 + hyper)
    slope = half + 0.5 * value * (1.0 - hyper * hyper) * coef * (1.0 + 3.0 * 0.044715 * square)
    return (value * half, slope)


def place_rows(ids_t, prio):
    count = ids_t.shape[1]
    first = ids_t[0:1, :]
    second = ids_t[1:2, :]
    stack = jnp.concatenate([first, second, prio, jnp.zeros((5, count), jnp.int32)], axis=0)
    columns = jnp.transpose(stack.astype(jnp.float32), (1, 0)).astype(jnp.int32)
    first_c, second_c, prio_c = columns[:, 0:1], columns[:, 1:2], columns[:, 2:3]
    ahead = prio_c < prio
    one = jnp.float32(1.0)
    zero = jnp.float32(0.0)
    slot_0 = jnp.sum(jnp.where((first_c == first) & ahead, one, zero), axis=0, keepdims=True)
    slot_1 = jnp.sum(
        jnp.where((first_c == second) | ((second_c == second) & ahead), one, zero),
        axis=0,
        keepdims=True,
    )
    slot_0 = slot_0.astype(jnp.int32)
    slot_1 = slot_1.astype(jnp.int32)
    place_0 = jnp.where(slot_0 < CAP, first * CAP + slot_0, -1)
    place_1 = jnp.where(slot_1 < CAP, second * CAP + slot_1, -1)
    return place_0, place_1


def row_slots(count):
    row = lax.broadcasted_iota(jnp.int32, (EXPERTS * PAIR, count), 0)
    return ((row >> 3) << 2) | (row & (CAP - 1)), (row & CAP) == 0


def dispatch_kernel(
    ids_hbm, prio_hbm, gates_hbm, tok_hbm, cot_hbm, w_in_hbm, w_out_hbm,
    send_ref, plan_ref, w_in_ref, w_out_ref,
    ids_ref, prio_ref, gates_ref, both_ref, sem,
):
    count = tok_hbm.shape[0]
    depth = w_in_ref.shape[1]
    pairs = (
        (ids_hbm, ids_ref),
        (prio_hbm, prio_ref),
        (gates_hbm, gates_ref),
        (tok_hbm, both_ref.at[0:count]),
        (cot_hbm, both_ref.at[count:2 * count]),
        (w_in_hbm.at[:, 0:depth], w_in_ref),
        (w_out_hbm.at[0:depth, :], w_out_ref),
    )
    copies = [pltpu.make_async_copy(*pair, sem.at[index]) for index, pair in enumerate(pairs)]
    for copy in copies[:5]:
        copy.start()
    for copy in copies[:3]:
        copy.wait()
    for copy in copies[5:]:
        copy.start()
    place_0, place_1 = place_rows(ids_ref[...], prio_ref[...])
    slot, is_x = row_slots(count)
    hit_0 = slot == place_0
    hit_1 = slot == place_1
    hit = jnp.where(hit_0 | hit_1, 1.0, 0.0)
    pick = jnp.concatenate(
        [jnp.where(is_x, hit, 0.0), jnp.where(is_x, 0.0, hit)], axis=1
    ).astype(jnp.bfloat16)
    gate = jnp.where(hit_0, gates_ref[0:1, :], 0.0) + jnp.where(hit_1, gates_ref[1:2, :], 0.0)
    scale = jnp.sum(gate, axis=1, keepdims=True)
    scale = jnp.where(is_x[:, 0:1], 1.0, scale)
    plan_ref[...] = jnp.concatenate(
        [
            place_0.astype(jnp.float32),
            place_1.astype(jnp.float32),
            gates_ref[...],
            jnp.zeros((4, count), jnp.float32),
        ],
        axis=0,
    )
    for copy in copies[3:5]:
        copy.wait()
    found = jnp.dot(pick, both_ref[...], preferred_element_type=jnp.float32)
    send_ref[...] = (found * scale).astype(jnp.bfloat16)
    for copy in copies[5:]:
        copy.wait()


def tables(plan_ref, pick_ref, gate_ref):
    place_0 = plan_ref[0:1, :].astype(jnp.int32)
    place_1 = plan_ref[1:2, :].astype(jnp.int32)
    count = place_0.shape[1]
    slot, is_x = row_slots(count)
    hit_0 = jnp.where(slot == place_0, 1.0, 0.0)
    hit_1 = jnp.where(slot == place_1, 1.0, 0.0)
    pick_0 = jnp.transpose(jnp.where(is_x, hit_0, 0.0), (1, 0))
    pick_1 = jnp.transpose(jnp.where(is_x, hit_1, 0.0), (1, 0))
    pick_b = jnp.transpose(jnp.where(is_x, 0.0, hit_0 + hit_1), (1, 0))
    pick_ref[...] = jnp.concatenate([pick_0, pick_1, pick_b], axis=0).astype(jnp.bfloat16)
    gate_ref[...] = jnp.transpose(plan_ref[...], (1, 0))


def row_picks(rows):
    half = rows // 2
    out = lax.broadcasted_iota(jnp.int32, (half, rows), 0)
    col = lax.broadcasted_iota(jnp.int32, (half, rows), 1)
    source = ((out >> 2) << 3) | (out & (CAP - 1))
    x_pick = jnp.where(col == source, 1.0, 0.0).astype(jnp.bfloat16)
    g_pick = jnp.where(col == source + CAP, 1.0, 0.0).astype(jnp.bfloat16)
    return x_pick, g_pick


def forward_kernel(
    steps, recv_ref, plan_ref, w_in_0, w_out_0, w_in_hbm, w_out_hbm,
    ret_ref, x_t_ref, g_ref, act_ref, d_pre_ref, pick_ref, gate_ref, d_out_hbm,
    w_in_ref, w_out_ref, x_ref, act_t_ref, stage, out_acc, back_acc, sem_in, sem_out, sem_left,
):
    width, depth = w_in_0.shape
    low = jnp.bfloat16

    def copies(step):
        cols = pl.ds(pl.multiple_of(step * depth, depth), depth)
        slot = step - 1
        return (
            pltpu.make_async_copy(w_in_hbm.at[:, cols], w_in_ref.at[slot], sem_in.at[slot]),
            pltpu.make_async_copy(w_out_hbm.at[cols, :], w_out_ref.at[slot], sem_out.at[slot]),
        )

    def leave(step):
        rows = pl.ds(pl.multiple_of(step * depth, depth), EARLY)
        slot = lax.rem(step, 2)
        return pltpu.make_async_copy(stage.at[slot], d_out_hbm.at[rows, :], sem_left.at[slot])

    def begin(step, carry):
        for copy in copies(step):
            copy.start()
        return carry

    lax.fori_loop(1, steps, begin, 0)
    recv = recv_ref[...]
    x_pick, g_pick = row_picks(recv.shape[0])
    x_rows = jnp.dot(x_pick, recv, preferred_element_type=jnp.float32)
    x_ref[...] = x_rows.astype(low)
    g_ref[...] = jnp.dot(g_pick, recv, preferred_element_type=jnp.float32).astype(low)
    out_acc[...] = jnp.zeros_like(out_acc)
    back_acc[...] = jnp.zeros_like(back_acc)

    def weights(step):
        if isinstance(step, int) and step == 0:
            return w_in_0, w_out_0
        return w_in_ref.at[step - 1], w_out_ref.at[step - 1]

    def front_dots(step, found):
        w_first, w_second = weights(step)
        for first in range(0, depth, 256):
            cols = slice(first, min(first + 256, depth))
            pre = []

            def one(cols=cols, pre=pre):
                pre.append(
                    jnp.dot(
                        x_ref[...], w_first[:, cols], preferred_element_type=jnp.float32
                    )
                )

            def two(cols=cols, pre=pre):
                d_act = lax.dot_general(
                    g_ref[...],
                    w_second[cols, :],
                    LAST_DIM,
                    preferred_element_type=jnp.float32,
                )
                found.append((cols, pre[0], d_act))

            yield one
            yield two

    def back_dots(step, act, d_pre):
        w_first, w_second = weights(step)
        for first in range(0, width, 256):
            cols = slice(first, min(first + 256, width))

            def one(cols=cols):
                out_acc[:, cols] += jnp.dot(
                    act, w_second[:, cols], preferred_element_type=jnp.float32
                )

            def two(cols=cols):
                back_acc[:, cols] += lax.dot_general(
                    d_pre,
                    w_first[cols, :],
                    LAST_DIM,
                    preferred_element_type=jnp.float32,
                )

            yield one
            yield two

    def grad_dots(step, act_t):
        slot = lax.rem(step, 2)
        for first in range(0, width, 256):
            cols = slice(first, min(first + 256, width))

            def one(cols=cols):
                stage[slot, :, cols] = jnp.dot(
                    act_t, g_ref[:, cols], preferred_element_type=jnp.float32
                ).astype(low)

            yield one

    def middle(step, found):
        for cols, pre, d_act in found:
            value, slope = gelu_parts(pre)
            act_ref[step, :, cols] = value.astype(low)
            d_pre_ref[step, :, cols] = (d_act * slope).astype(low)
            if cols.start == 0:
                act_t_ref[...] = jnp.transpose(value[:, 0:EARLY], (1, 0)).astype(low)

    def run(first, second):
        done = 0
        for index, thunk in enumerate(first):
            thunk()
            due = (index + 1) * len(second) // len(first)
            for other in second[done:due]:
                other()
            done = due

    def both(step, extra=()):
        for copy in copies(step):
            copy.wait()
        act, act_t, d_pre = act_ref[step - 1], act_t_ref[...], d_pre_ref[step - 1]
        found = []
        fronts = [*front_dots(step, found)]
        backs = [*back_dots(step - 1, act, d_pre)]
        blocks = len(fronts) // 2
        share = len(backs) // (blocks + 1)
        order = []
        for block in range(blocks):
            order += fronts[2 * block:2 * block + 2]
            order += backs[share * block:share * (block + 1)]
            order.append(lambda block=block: middle(step, found[block:block + 1]))
        order += [*extra, *backs[share * blocks:]]
        run(order, [*grad_dots(step - 1, act_t)])
        leave(step - 1).start()

    found = []
    for thunk in front_dots(0, found):
        thunk()
    middle(0, found)

    def aside():
        x_t_ref[...] = jnp.transpose(x_rows, (1, 0)).astype(low)
        tables(plan_ref, pick_ref, gate_ref)

    if steps > 1:
        both(1, (aside,))
    else:
        aside()

    def body(step, carry):
        @pl.when(step > 2)
        def _():
            leave(step - 3).wait()

        both(step)
        return carry

    lax.fori_loop(2, steps, body, 0)
    last = steps - 1
    if steps > 2:
        leave(last - 2).wait()
    for thunk in grad_dots(last, act_t_ref[...]):
        thunk()
    leave(last).start()
    for thunk in back_dots(last, act_ref[last], d_pre_ref[last]):
        thunk()
    ret = lax.dot_general(
        x_pick, out_acc[...].astype(low), ROWS_DIM, preferred_element_type=jnp.float32
    ) + lax.dot_general(
        g_pick, back_acc[...].astype(low), ROWS_DIM, preferred_element_type=jnp.float32
    )
    ret_ref[...] = ret.astype(low)
    if steps > 1:
        leave(last - 1).wait()
    leave(last).wait()


def product(out_ref, left, right, tall, wide):
    rows, cols = out_ref.shape
    for col in range(0, cols, wide):
        col_end = min(col + wide, cols)
        for row in range(0, rows, tall):
            row_end = min(row + tall, rows)
            out_ref[row:row_end, col:col_end] = jnp.dot(
                left[row:row_end], right[:, col:col_end], preferred_element_type=jnp.float32
            ).astype(jnp.bfloat16)


def grads_kernel(
    x_t_ref, g_ref, act_ref, d_pre_ref, _, d_in_hbm, d_out_hbm, d_in_stage, d_out_stage, sem
):
    steps, _, depth = act_ref.shape
    width = x_t_ref.shape[0]
    slots = d_in_stage.shape[0]
    later = depth - EARLY

    def leave(step):
        slot = lax.rem(step, slots)
        cols = pl.ds(pl.multiple_of(step * depth, depth), depth)
        pairs = []
        for index in range(2):
            some = pl.ds(index * (width // 2), width // 2)
            pairs.append((d_in_stage.at[slot, some], d_in_hbm.at[some, cols]))
        for index in range(2):
            first = index * (later // 2)
            here = pl.ds(first, later // 2)
            there = pl.ds(pl.multiple_of(step * depth + EARLY + first, 64), later // 2)
            pairs.append((d_out_stage.at[slot, here], d_out_hbm.at[there]))
        return [
            pltpu.make_async_copy(*pair, sem.at[slot, index]) for index, pair in enumerate(pairs)
        ]

    def work(step, carry):
        @pl.when(step >= slots)
        def _():
            for copy in leave(step - slots):
                copy.wait()

        slot = lax.rem(step, slots)
        copies = leave(step)
        act_t = jnp.transpose(act_ref[step].astype(jnp.float32), (1, 0)).astype(jnp.bfloat16)
        product(d_in_stage.at[slot], x_t_ref[...], d_pre_ref[step], 208, 256)
        for copy in copies[:2]:
            copy.start()
        product(d_out_stage.at[slot], act_t[EARLY:], g_ref[...], 192, 256)
        for copy in copies[2:]:
            copy.start()
        return carry

    lax.fori_loop(0, steps, work, 0)
    for step in range(max(steps - slots, 0), steps):
        for copy in leave(step):
            copy.wait()


def combine_kernel(ret_ref, pick_ref, gate_ref, cot_ref, mixed_ref, d_tok_ref, d_gate_ref):
    count = cot_ref.shape[0]
    rows = pick_ref.shape[1]
    found = None
    for first in range(0, ret_ref.shape[0], rows):
        part = jnp.dot(
            pick_ref[...], ret_ref[first:first + rows, :], preferred_element_type=jnp.float32
        )
        found = part if found is None else found + part
    o_0, o_1 = found[:count], found[count:2 * count]
    mixed_ref[...] = (gate_ref[:, 2:3] * o_0 + gate_ref[:, 3:4] * o_1).astype(jnp.bfloat16)
    d_tok_ref[...] = found[2 * count:].astype(jnp.bfloat16)
    cot = cot_ref[...].astype(jnp.float32)
    d_0 = jnp.sum(cot * o_0, axis=1, keepdims=True)
    d_1 = jnp.sum(cot * o_1, axis=1, keepdims=True)
    lane = lax.broadcasted_iota(jnp.int32, (count, 8), 1)
    both = jnp.where(lane == 0, d_0, jnp.where(lane == 1, d_1, 0.0))
    d_gate_ref[...] = jnp.transpose(both, (1, 0))[0:2, :]


def params(mib):
    return pltpu.CompilerParams(vmem_limit_bytes=mib * 1024 * 1024)


def chunk_of(hidden, want):
    return max(size for size in range(128, want + 1, 128) if hidden % size == 0)


def per_device(tokens, expert_ids, priority, gates, w_in, w_out, cotangent):
    count, width = tokens.shape
    repl = lax.axis_size("expert") // EXPERTS
    slots = EXPERTS * PAIR
    hidden = w_in.shape[2]
    ids_t = jnp.transpose(expert_ids, (1, 0))
    gates_t = jnp.transpose(gates, (1, 0))
    low = jnp.bfloat16
    vmem = pl.BlockSpec(memory_space=pltpu.VMEM)
    hbm = pl.BlockSpec(memory_space=pl.ANY)
    chunk = chunk_of(hidden, 512)
    steps = hidden // chunk
    send, plan, w_in_0, w_out_0 = pl.pallas_call(
        dispatch_kernel,
        out_shape=(
            pltpu.VMEM((slots, width), low),
            pltpu.VMEM((8, count), jnp.float32),
            pltpu.VMEM((width, chunk), low),
            pltpu.VMEM((chunk, width), low),
        ),
        in_specs=[hbm] * 7,
        out_specs=(vmem,) * 4,
        scratch_shapes=[
            pltpu.VMEM((2, count), jnp.int32),
            pltpu.VMEM((1, count), jnp.int32),
            pltpu.VMEM((2, count), jnp.float32),
            pltpu.VMEM((2 * count, width), low),
            pltpu.SemaphoreType.DMA((7,)),
        ],
        compiler_params=params(50),
        name="dispatch",
    )(*(pltpu.with_memory_space_constraint(array, pltpu.HBM) for array in (
        ids_t, priority, gates_t, tokens, cotangent, w_in[0], w_out[0]
    )))
    send = jnp.tile(send.reshape(EXPERTS, PAIR, width), (repl, 1, 1))
    recv = lax.all_to_all(send, "expert", split_axis=0, concat_axis=0, tiled=True)
    rows = recv.shape[0] * PAIR
    recv = recv.reshape(rows, width)
    half = rows // 2
    ret, x_t, g_rows, act, d_pre, pick, gate_cols, d_w_out = pl.pallas_call(
        functools.partial(forward_kernel, steps),
        out_shape=(
            pltpu.VMEM((rows, width), low),
            jax.ShapeDtypeStruct((width, half), low),
            jax.ShapeDtypeStruct((half, width), low),
            jax.ShapeDtypeStruct((steps, half, chunk), low),
            jax.ShapeDtypeStruct((steps, half, chunk), low),
            jax.ShapeDtypeStruct((3 * count, slots), low),
            jax.ShapeDtypeStruct((count, 8), jnp.float32),
            jax.ShapeDtypeStruct((hidden, width), low),
        ),
        in_specs=[vmem] * 4 + [hbm] * 2,
        out_specs=(vmem,) * 7 + (hbm,),
        scratch_shapes=[
            pltpu.VMEM((max(steps - 1, 1), width, chunk), low),
            pltpu.VMEM((max(steps - 1, 1), chunk, width), low),
            pltpu.VMEM((half, width), low),
            pltpu.VMEM((EARLY, half), low),
            pltpu.VMEM((2, EARLY, width), low),
            pltpu.VMEM((half, width), jnp.float32),
            pltpu.VMEM((half, width), jnp.float32),
            pltpu.SemaphoreType.DMA((max(steps - 1, 1),)),
            pltpu.SemaphoreType.DMA((max(steps - 1, 1),)),
            pltpu.SemaphoreType.DMA((2,)),
        ],
        compiler_params=params(43),
        cost_estimate=pl.CostEstimate(
            flops=8 * half * width * hidden,
            bytes_accessed=4 * width * hidden,
            transcendentals=half * hidden,
        ),
        name="forward",
    )(recv, plan, w_in_0, w_out_0, w_in[0], w_out[0])
    ret = lax.all_to_all(
        ret.reshape(rows // PAIR, PAIR, width), "expert", split_axis=0, concat_axis=0, tiled=True
    ).reshape(rows, width)
    d_w_in, d_w_out = pl.pallas_call(
        grads_kernel,
        out_shape=(
            jax.ShapeDtypeStruct((width, hidden), low),
            jax.ShapeDtypeStruct((hidden, width), low),
        ),
        in_specs=[vmem] * 4 + [hbm],
        out_specs=(hbm,) * 2,
        input_output_aliases={4: 1},
        scratch_shapes=[
            pltpu.VMEM((3, width, chunk), low),
            pltpu.VMEM((3, chunk - EARLY, width), low),
            pltpu.SemaphoreType.DMA((3, 4)),
        ],
        compiler_params=params(24),
        cost_estimate=pl.CostEstimate(
            flops=4 * half * width * hidden,
            bytes_accessed=4 * width * hidden,
            transcendentals=0,
        ),
        name="grads",
    )(x_t, g_rows, act, d_pre, d_w_out)
    mixed, d_tokens, d_gates_t = pl.pallas_call(
        combine_kernel,
        out_shape=(
            jax.ShapeDtypeStruct((count, width), low),
            jax.ShapeDtypeStruct((count, width), low),
            jax.ShapeDtypeStruct((2, count), jnp.float32),
        ),
        compiler_params=params(12),
        name="combine",
    )(ret, pick, gate_cols, cotangent)
    return (mixed, d_tokens, jnp.transpose(d_gates_t, (1, 0)), d_w_in[None], d_w_out[None])


def solution(mesh):
    rows = P(("groups", "expert"), None)
    return jax.shard_map(
        per_device,
        mesh=mesh,
        in_specs=(rows, rows, rows, rows, P("expert", None, None), P("expert", None, None), rows),
        out_specs=(
            rows,
            rows,
            rows,
            P(("groups", "expert"), None, None),
            P(("groups", "expert"), None, None),
        ),
        check_vma=False,
    )
```

```python
import functools
import math

import jax
import jax.numpy as jnp
from jax import lax
from jax.experimental import pallas as pl
from jax.experimental.pallas import tpu as pltpu
from jax.sharding import PartitionSpec as P

EXPERTS = 16
CAP = 4
PAIR = 2 * CAP
EARLY = 128
ROWS_DIM = (((0,), (0,)), ((), ()))
LAST_DIM = (((1,), (1,)), ((), ()))


def gelu_parts(value):
    coef = math.sqrt(2.0 / math.pi)
    square = value * value
    hyper = jnp.tanh(coef * value * (1.0 + 0.044715 * square))
    half = 0.5 * (1.0 + hyper)
    slope = half + 0.5 * value * (1.0 - hyper * hyper) * coef * (1.0 + 3.0 * 0.044715 * square)
    return (value * half, slope)


def place_rows(ids_t, prio):
    count = ids_t.shape[1]
    first = ids_t[0:1, :]
    second = ids_t[1:2, :]
    stack = jnp.concatenate([first, second, prio, jnp.zeros((5, count), jnp.int32)], axis=0)
    columns = jnp.transpose(stack.astype(jnp.float32), (1, 0)).astype(jnp.int32)
    first_c, second_c, prio_c = columns[:, 0:1], columns[:, 1:2], columns[:, 2:3]
    ahead = prio_c < prio
    one = jnp.float32(1.0)
    zero = jnp.float32(0.0)
    slot_0 = jnp.sum(jnp.where((first_c == first) & ahead, one, zero), axis=0, keepdims=True)
    slot_1 = jnp.sum(
        jnp.where((first_c == second) | ((second_c == second) & ahead), one, zero),
        axis=0,
        keepdims=True,
    )
    slot_0 = slot_0.astype(jnp.int32)
    slot_1 = slot_1.astype(jnp.int32)
    place_0 = jnp.where(slot_0 < CAP, first * CAP + slot_0, -1)
    place_1 = jnp.where(slot_1 < CAP, second * CAP + slot_1, -1)
    return place_0, place_1


def row_slots(count):
    row = lax.broadcasted_iota(jnp.int32, (EXPERTS * PAIR, count), 0)
    return ((row >> 3) << 2) | (row & (CAP - 1)), (row & CAP) == 0


def dispatch_kernel(
    ids_hbm, prio_hbm, gates_hbm, tok_hbm, cot_hbm, w_in_hbm, w_out_hbm,
    send_ref, plan_ref, w_in_ref, w_out_ref,
    ids_ref, prio_ref, gates_ref, both_ref, sem,
):
    count = tok_hbm.shape[0]
    depth = w_in_ref.shape[1]
    pairs = (
        (ids_hbm, ids_ref),
        (prio_hbm, prio_ref),
        (gates_hbm, gates_ref),
        (tok_hbm, both_ref.at[0:count]),
        (cot_hbm, both_ref.at[count:2 * count]),
        (w_in_hbm.at[:, 0:depth], w_in_ref),
        (w_out_hbm.at[0:depth, :], w_out_ref),
    )
    copies = [pltpu.make_async_copy(*pair, sem.at[index]) for index, pair in enumerate(pairs)]
    for copy in copies:
        copy.start()
    for copy in copies[:3]:
        copy.wait()
    place_0, place_1 = place_rows(ids_ref[...], prio_ref[...])
    slot, is_x = row_slots(count)
    hit_0 = slot == place_0
    hit_1 = slot == place_1
    hit = jnp.where(hit_0 | hit_1, 1.0, 0.0)
    pick = jnp.concatenate(
        [jnp.where(is_x, hit, 0.0), jnp.where(is_x, 0.0, hit)], axis=1
    ).astype(jnp.bfloat16)
    gate = jnp.where(hit_0, gates_ref[0:1, :], 0.0) + jnp.where(hit_1, gates_ref[1:2, :], 0.0)
    scale = jnp.sum(gate, axis=1, keepdims=True)
    scale = jnp.where(is_x[:, 0:1], 1.0, scale)
    plan_ref[...] = jnp.concatenate(
        [
            place_0.astype(jnp.float32),
            place_1.astype(jnp.float32),
            gates_ref[...],
            jnp.zeros((4, count), jnp.float32),
        ],
        axis=0,
    )
    for copy in copies[3:5]:
        copy.wait()
    found = jnp.dot(pick, both_ref[...], preferred_element_type=jnp.float32)
    send_ref[...] = (found * scale).astype(jnp.bfloat16)
    for copy in copies[5:]:
        copy.wait()


def tables(plan_ref, pick_ref, gate_ref):
    place_0 = plan_ref[0:1, :].astype(jnp.int32)
    place_1 = plan_ref[1:2, :].astype(jnp.int32)
    count = place_0.shape[1]
    slot, is_x = row_slots(count)
    hit_0 = jnp.where(slot == place_0, 1.0, 0.0)
    hit_1 = jnp.where(slot == place_1, 1.0, 0.0)
    pick_0 = jnp.transpose(jnp.where(is_x, hit_0, 0.0), (1, 0))
    pick_1 = jnp.transpose(jnp.where(is_x, hit_1, 0.0), (1, 0))
    pick_b = jnp.transpose(jnp.where(is_x, 0.0, hit_0 + hit_1), (1, 0))
    pick_ref[...] = jnp.concatenate([pick_0, pick_1, pick_b], axis=0).astype(jnp.bfloat16)
    gate_ref[...] = jnp.transpose(plan_ref[...], (1, 0))


def row_order(rows):
    half = rows // 2
    out = lax.broadcasted_iota(jnp.int32, (rows, rows), 0)
    col = lax.broadcasted_iota(jnp.int32, (rows, rows), 1)
    place = jnp.where(out < half, out, out - half)
    source = ((place >> 2) << 3) | (place & (CAP - 1)) | jnp.where(out < half, 0, CAP)
    return jnp.where(col == source, 1.0, 0.0).astype(jnp.bfloat16)


def forward_kernel(
    steps, recv_ref, plan_ref, w_in_0, w_out_0, w_in_hbm, w_out_hbm,
    ret_ref, x_t_ref, g_ref, act_ref, d_pre_ref, pick_ref, gate_ref, d_out_hbm,
    w_in_ref, w_out_ref, x_ref, act_t_ref, stage, out_acc, back_acc, sem_in, sem_out, sem_left,
):
    width, depth = w_in_0.shape
    low = jnp.bfloat16

    def copies(step):
        cols = pl.ds(pl.multiple_of(step * depth, depth), depth)
        slot = step - 1
        return (
            pltpu.make_async_copy(w_in_hbm.at[:, cols], w_in_ref.at[slot], sem_in.at[slot]),
            pltpu.make_async_copy(w_out_hbm.at[cols, :], w_out_ref.at[slot], sem_out.at[slot]),
        )

    def leave(step):
        rows = pl.ds(pl.multiple_of(step * depth, depth), EARLY)
        slot = lax.rem(step, 2)
        return pltpu.make_async_copy(stage.at[slot], d_out_hbm.at[rows, :], sem_left.at[slot])

    def begin(step, carry):
        for copy in copies(step):
            copy.start()
        return carry

    lax.fori_loop(1, steps, begin, 0)
    order = row_order(recv_ref.shape[0])
    half = recv_ref.shape[0] // 2
    found = jnp.dot(order, recv_ref[...], preferred_element_type=jnp.float32)
    x_rows = found[:half]
    x_ref[...] = x_rows.astype(low)
    g_ref[...] = found[half:].astype(low)
    out_acc[...] = jnp.zeros_like(out_acc)
    back_acc[...] = jnp.zeros_like(back_acc)

    def weights(step):
        if isinstance(step, int) and step == 0:
            return w_in_0, w_out_0
        return w_in_ref.at[step - 1], w_out_ref.at[step - 1]

    def front_dots(step, found):
        w_first, w_second = weights(step)
        for first in range(0, depth, 256):
            cols = slice(first, min(first + 256, depth))
            pre = []

            def one(cols=cols, pre=pre):
                pre.append(
                    jnp.dot(
                        x_ref[...], w_first[:, cols], preferred_element_type=jnp.float32
                    )
                )

            def two(cols=cols, pre=pre):
                d_act = lax.dot_general(
                    g_ref[...],
                    w_second[cols, :],
                    LAST_DIM,
                    preferred_element_type=jnp.float32,
                )
                found.append((cols, pre[0], d_act))

            yield one
            yield two

    def back_dots(step, act, d_pre):
        w_first, w_second = weights(step)
        for first in range(0, width, 256):
            cols = slice(first, min(first + 256, width))

            def one(cols=cols):
                out_acc[:, cols] += jnp.dot(
                    act, w_second[:, cols], preferred_element_type=jnp.float32
                )

            def two(cols=cols):
                back_acc[:, cols] += lax.dot_general(
                    d_pre,
                    w_first[cols, :],
                    LAST_DIM,
                    preferred_element_type=jnp.float32,
                )

            yield one
            yield two

    def grad_dots(step, act_t):
        slot = lax.rem(step, 2)
        for first in range(0, width, 256):
            cols = slice(first, min(first + 256, width))

            def one(cols=cols):
                stage[slot, :, cols] = jnp.dot(
                    act_t, g_ref[:, cols], preferred_element_type=jnp.float32
                ).astype(low)

            yield one

    def middle(step, found):
        for cols, pre, d_act in found:
            value, slope = gelu_parts(pre)
            act_ref[step, :, cols] = value.astype(low)
            d_pre_ref[step, :, cols] = (d_act * slope).astype(low)
            if cols.start == 0:
                act_t_ref[...] = jnp.transpose(value[:, 0:EARLY], (1, 0)).astype(low)

    def run(first, second):
        done = 0
        for index, thunk in enumerate(first):
            thunk()
            due = (index + 1) * len(second) // len(first)
            for other in second[done:due]:
                other()
            done = due

    def both(step, extra=()):
        for copy in copies(step):
            copy.wait()
        act, act_t, d_pre = act_ref[step - 1], act_t_ref[...], d_pre_ref[step - 1]
        found = []
        fronts = [*front_dots(step, found)]
        backs = [*back_dots(step - 1, act, d_pre)]
        blocks = len(fronts) // 2
        share = len(backs) // (blocks + 1)
        turns = []
        for block in range(blocks):
            turns += fronts[2 * block:2 * block + 2]
            turns += backs[share * block:share * (block + 1)]
            turns.append(lambda block=block: middle(step, found[block:block + 1]))
        turns += [*extra, *backs[share * blocks:]]
        run(turns, [*grad_dots(step - 1, act_t)])
        leave(step - 1).start()

    found = []
    for thunk in front_dots(0, found):
        thunk()
    middle(0, found)

    def aside():
        x_t_ref[...] = jnp.transpose(x_rows, (1, 0)).astype(low)
        tables(plan_ref, pick_ref, gate_ref)

    if steps > 1:
        both(1, (aside,))
    else:
        aside()

    def body(step, carry):
        @pl.when(step > 2)
        def _():
            leave(step - 3).wait()

        both(step)
        return carry

    lax.fori_loop(2, steps, body, 0)
    last = steps - 1
    if steps > 2:
        leave(last - 2).wait()
    for thunk in grad_dots(last, act_t_ref[...]):
        thunk()
    leave(last).start()
    for thunk in back_dots(last, act_ref[last], d_pre_ref[last]):
        thunk()
    sums = jnp.concatenate([out_acc[...], back_acc[...]], axis=0).astype(low)
    ret = lax.dot_general(order, sums, ROWS_DIM, preferred_element_type=jnp.float32)
    ret_ref[...] = ret.astype(low)
    if steps > 1:
        leave(last - 1).wait()
    leave(last).wait()


def product(out_ref, left, right, tall, wide):
    rows, cols = out_ref.shape
    for col in range(0, cols, wide):
        col_end = min(col + wide, cols)
        for row in range(0, rows, tall):
            row_end = min(row + tall, rows)
            out_ref[row:row_end, col:col_end] = jnp.dot(
                left[row:row_end], right[:, col:col_end], preferred_element_type=jnp.float32
            ).astype(jnp.bfloat16)


def grads_kernel(
    x_t_ref, g_ref, act_ref, d_pre_ref, _, d_in_hbm, d_out_hbm, d_in_stage, d_out_stage, sem
):
    steps, _, depth = act_ref.shape
    width = x_t_ref.shape[0]
    slots = d_in_stage.shape[0]
    later = depth - EARLY

    def leave(step):
        slot = lax.rem(step, slots)
        cols = pl.ds(pl.multiple_of(step * depth, depth), depth)
        pairs = []
        for index in range(2):
            some = pl.ds(index * (width // 2), width // 2)
            pairs.append((d_in_stage.at[slot, some], d_in_hbm.at[some, cols]))
        for index in range(2):
            first = index * (later // 2)
            here = pl.ds(first, later // 2)
            there = pl.ds(pl.multiple_of(step * depth + EARLY + first, 64), later // 2)
            pairs.append((d_out_stage.at[slot, here], d_out_hbm.at[there]))
        return [
            pltpu.make_async_copy(*pair, sem.at[slot, index]) for index, pair in enumerate(pairs)
        ]

    def work(step, carry):
        @pl.when(step >= slots)
        def _():
            for copy in leave(step - slots):
                copy.wait()

        slot = lax.rem(step, slots)
        copies = leave(step)
        act_t = jnp.transpose(act_ref[step].astype(jnp.float32), (1, 0)).astype(jnp.bfloat16)
        product(d_in_stage.at[slot], x_t_ref[...], d_pre_ref[step], 208, 256)
        for copy in copies[:2]:
            copy.start()
        product(d_out_stage.at[slot], act_t[EARLY:], g_ref[...], 192, 256)
        for copy in copies[2:]:
            copy.start()
        return carry

    lax.fori_loop(0, steps, work, 0)
    for step in range(max(steps - slots, 0), steps):
        for copy in leave(step):
            copy.wait()


def combine_kernel(ret_ref, pick_ref, gate_ref, cot_ref, mixed_ref, d_tok_ref, d_gate_ref):
    count = cot_ref.shape[0]
    rows = pick_ref.shape[1]
    found = None
    for first in range(0, ret_ref.shape[0], rows):
        part = jnp.dot(
            pick_ref[...], ret_ref[first:first + rows, :], preferred_element_type=jnp.float32
        )
        found = part if found is None else found + part
    o_0, o_1 = found[:count], found[count:2 * count]
    mixed_ref[...] = (gate_ref[:, 2:3] * o_0 + gate_ref[:, 3:4] * o_1).astype(jnp.bfloat16)
    d_tok_ref[...] = found[2 * count:].astype(jnp.bfloat16)
    cot = cot_ref[...].astype(jnp.float32)
    d_0 = jnp.sum(cot * o_0, axis=1, keepdims=True)
    d_1 = jnp.sum(cot * o_1, axis=1, keepdims=True)
    lane = lax.broadcasted_iota(jnp.int32, (count, 8), 1)
    both = jnp.where(lane == 0, d_0, jnp.where(lane == 1, d_1, 0.0))
    d_gate_ref[...] = jnp.transpose(both, (1, 0))[0:2, :]


def params(mib):
    return pltpu.CompilerParams(vmem_limit_bytes=mib * 1024 * 1024)


def chunk_of(hidden, want):
    return max(size for size in range(128, want + 1, 128) if hidden % size == 0)


def per_device(tokens, expert_ids, priority, gates, w_in, w_out, cotangent):
    count, width = tokens.shape
    repl = lax.axis_size("expert") // EXPERTS
    slots = EXPERTS * PAIR
    hidden = w_in.shape[2]
    ids_t = jnp.transpose(expert_ids, (1, 0))
    gates_t = jnp.transpose(gates, (1, 0))
    low = jnp.bfloat16
    vmem = pl.BlockSpec(memory_space=pltpu.VMEM)
    hbm = pl.BlockSpec(memory_space=pl.ANY)
    chunk = chunk_of(hidden, 512)
    steps = hidden // chunk
    send, plan, w_in_0, w_out_0 = pl.pallas_call(
        dispatch_kernel,
        out_shape=(
            pltpu.VMEM((slots, width), low),
            pltpu.VMEM((8, count), jnp.float32),
            pltpu.VMEM((width, chunk), low),
            pltpu.VMEM((chunk, width), low),
        ),
        in_specs=[hbm] * 7,
        out_specs=(vmem,) * 4,
        scratch_shapes=[
            pltpu.VMEM((2, count), jnp.int32),
            pltpu.VMEM((1, count), jnp.int32),
            pltpu.VMEM((2, count), jnp.float32),
            pltpu.VMEM((2 * count, width), low),
            pltpu.SemaphoreType.DMA((7,)),
        ],
        compiler_params=params(50),
        name="dispatch",
    )(*(pltpu.with_memory_space_constraint(array, pltpu.HBM) for array in (
        ids_t, priority, gates_t, tokens, cotangent, w_in[0], w_out[0]
    )))
    send = jnp.tile(send.reshape(EXPERTS, PAIR, width), (repl, 1, 1))
    recv = lax.all_to_all(send, "expert", split_axis=0, concat_axis=0, tiled=True)
    rows = recv.shape[0] * PAIR
    recv = recv.reshape(rows, width)
    half = rows // 2
    ret, x_t, g_rows, act, d_pre, pick, gate_cols, d_w_out = pl.pallas_call(
        functools.partial(forward_kernel, steps),
        out_shape=(
            pltpu.VMEM((rows, width), low),
            jax.ShapeDtypeStruct((width, half), low),
            jax.ShapeDtypeStruct((half, width), low),
            jax.ShapeDtypeStruct((steps, half, chunk), low),
            jax.ShapeDtypeStruct((steps, half, chunk), low),
            jax.ShapeDtypeStruct((3 * count, slots), low),
            jax.ShapeDtypeStruct((count, 8), jnp.float32),
            jax.ShapeDtypeStruct((hidden, width), low),
        ),
        in_specs=[vmem] * 4 + [hbm] * 2,
        out_specs=(vmem,) * 7 + (hbm,),
        scratch_shapes=[
            pltpu.VMEM((max(steps - 1, 1), width, chunk), low),
            pltpu.VMEM((max(steps - 1, 1), chunk, width), low),
            pltpu.VMEM((half, width), low),
            pltpu.VMEM((EARLY, half), low),
            pltpu.VMEM((2, EARLY, width), low),
            pltpu.VMEM((half, width), jnp.float32),
            pltpu.VMEM((half, width), jnp.float32),
            pltpu.SemaphoreType.DMA((max(steps - 1, 1),)),
            pltpu.SemaphoreType.DMA((max(steps - 1, 1),)),
            pltpu.SemaphoreType.DMA((2,)),
        ],
        compiler_params=params(43),
        cost_estimate=pl.CostEstimate(
            flops=8 * half * width * hidden,
            bytes_accessed=4 * width * hidden,
            transcendentals=half * hidden,
        ),
        name="forward",
    )(recv, plan, w_in_0, w_out_0, w_in[0], w_out[0])
    ret = lax.all_to_all(
        ret.reshape(rows // PAIR, PAIR, width), "expert", split_axis=0, concat_axis=0, tiled=True
    ).reshape(rows, width)
    d_w_in, d_w_out = pl.pallas_call(
        grads_kernel,
        out_shape=(
            jax.ShapeDtypeStruct((width, hidden), low),
            jax.ShapeDtypeStruct((hidden, width), low),
        ),
        in_specs=[vmem] * 4 + [hbm],
        out_specs=(hbm,) * 2,
        input_output_aliases={4: 1},
        scratch_shapes=[
            pltpu.VMEM((3, width, chunk), low),
            pltpu.VMEM((3, chunk - EARLY, width), low),
            pltpu.SemaphoreType.DMA((3, 4)),
        ],
        compiler_params=params(24),
        cost_estimate=pl.CostEstimate(
            flops=4 * half * width * hidden,
            bytes_accessed=4 * width * hidden,
            transcendentals=0,
        ),
        name="grads",
    )(x_t, g_rows, act, d_pre, d_w_out)
    mixed, d_tokens, d_gates_t = pl.pallas_call(
        combine_kernel,
        out_shape=(
            jax.ShapeDtypeStruct((count, width), low),
            jax.ShapeDtypeStruct((count, width), low),
            jax.ShapeDtypeStruct((2, count), jnp.float32),
        ),
        compiler_params=params(12),
        name="combine",
    )(ret, pick, gate_cols, cotangent)
    return (mixed, d_tokens, jnp.transpose(d_gates_t, (1, 0)), d_w_in[None], d_w_out[None])


def solution(mesh):
    rows = P(("groups", "expert"), None)
    return jax.shard_map(
        per_device,
        mesh=mesh,
        in_specs=(rows, rows, rows, rows, P("expert", None, None), P("expert", None, None), rows),
        out_specs=(
            rows,
            rows,
            rows,
            P(("groups", "expert"), None, None),
            P(("groups", "expert"), None, None),
        ),
        check_vma=False,
    )
```

```python
import functools
import math

import jax
import jax.numpy as jnp
from jax import lax
from jax.experimental import pallas as pl
from jax.experimental.pallas import tpu as pltpu
from jax.sharding import PartitionSpec as P

EXPERTS = 16
CAP = 4
PAIR = 2 * CAP
EARLY = 128
LAST_DIM = (((1,), (1,)), ((), ()))


def gelu_parts(value):
    coef = math.sqrt(2.0 / math.pi)
    square = value * value
    hyper = jnp.tanh(coef * value * (1.0 + 0.044715 * square))
    half = 0.5 * (1.0 + hyper)
    slope = half + 0.5 * value * (1.0 - hyper * hyper) * coef * (1.0 + 3.0 * 0.044715 * square)
    return (value * half, slope)


def place_rows(ids_t, prio):
    count = ids_t.shape[1]
    first = ids_t[0:1, :]
    second = ids_t[1:2, :]
    stack = jnp.concatenate([first, second, prio, jnp.zeros((5, count), jnp.int32)], axis=0)
    columns = jnp.transpose(stack.astype(jnp.float32), (1, 0)).astype(jnp.int32)
    first_c, second_c, prio_c = columns[:, 0:1], columns[:, 1:2], columns[:, 2:3]
    ahead = prio_c < prio
    one = jnp.float32(1.0)
    zero = jnp.float32(0.0)
    slot_0 = jnp.sum(jnp.where((first_c == first) & ahead, one, zero), axis=0, keepdims=True)
    slot_1 = jnp.sum(
        jnp.where((first_c == second) | ((second_c == second) & ahead), one, zero),
        axis=0,
        keepdims=True,
    )
    slot_0 = slot_0.astype(jnp.int32)
    slot_1 = slot_1.astype(jnp.int32)
    place_0 = jnp.where(slot_0 < CAP, first * CAP + slot_0, -1)
    place_1 = jnp.where(slot_1 < CAP, second * CAP + slot_1, -1)
    return place_0, place_1


def row_slots(count):
    row = lax.broadcasted_iota(jnp.int32, (EXPERTS * PAIR, count), 0)
    return ((row >> 3) << 2) | (row & (CAP - 1)), (row & CAP) == 0


def dispatch_kernel(
    ids_hbm, prio_hbm, gates_hbm, tok_hbm, cot_hbm, w_in_hbm, w_out_hbm,
    send_ref, plan_ref, w_in_ref, w_out_ref,
    ids_ref, prio_ref, gates_ref, both_ref, sem,
):
    count = tok_hbm.shape[0]
    depth = w_in_ref.shape[1]
    pairs = (
        (ids_hbm, ids_ref),
        (prio_hbm, prio_ref),
        (gates_hbm, gates_ref),
        (tok_hbm, both_ref.at[0:count]),
        (cot_hbm, both_ref.at[count:2 * count]),
        (w_in_hbm.at[:, 0:depth], w_in_ref),
        (w_out_hbm.at[0:depth, :], w_out_ref),
    )
    copies = [pltpu.make_async_copy(*pair, sem.at[index]) for index, pair in enumerate(pairs)]
    for copy in copies:
        copy.start()
    for copy in copies[:3]:
        copy.wait()
    place_0, place_1 = place_rows(ids_ref[...], prio_ref[...])
    slot, is_x = row_slots(count)
    hit_0 = slot == place_0
    hit_1 = slot == place_1
    hit = jnp.where(hit_0 | hit_1, 1.0, 0.0)
    pick = jnp.concatenate(
        [jnp.where(is_x, hit, 0.0), jnp.where(is_x, 0.0, hit)], axis=1
    ).astype(jnp.bfloat16)
    gate = jnp.where(hit_0, gates_ref[0:1, :], 0.0) + jnp.where(hit_1, gates_ref[1:2, :], 0.0)
    scale = jnp.sum(gate, axis=1, keepdims=True)
    scale = jnp.where(is_x[:, 0:1], 1.0, scale)
    plan_ref[...] = jnp.concatenate(
        [
            place_0.astype(jnp.float32),
            place_1.astype(jnp.float32),
            gates_ref[...],
            jnp.zeros((4, count), jnp.float32),
        ],
        axis=0,
    )
    for copy in copies[3:5]:
        copy.wait()
    found = jnp.dot(pick, both_ref[...], preferred_element_type=jnp.float32)
    send_ref[...] = (found * scale).astype(jnp.bfloat16)
    for copy in copies[5:]:
        copy.wait()


def tables(plan_ref, pick_ref, gate_ref):
    place_0 = plan_ref[0:1, :].astype(jnp.int32)
    place_1 = plan_ref[1:2, :].astype(jnp.int32)
    count = place_0.shape[1]
    slot, is_x = row_slots(count)
    hit_0 = jnp.where(slot == place_0, 1.0, 0.0)
    hit_1 = jnp.where(slot == place_1, 1.0, 0.0)
    pick_0 = jnp.transpose(jnp.where(is_x, hit_0, 0.0), (1, 0))
    pick_1 = jnp.transpose(jnp.where(is_x, hit_1, 0.0), (1, 0))
    pick_b = jnp.transpose(jnp.where(is_x, 0.0, hit_0 + hit_1), (1, 0))
    pick_ref[...] = jnp.concatenate([pick_0, pick_1, pick_b], axis=0).astype(jnp.bfloat16)
    gate_ref[...] = jnp.transpose(plan_ref[...], (1, 0))


def row_order(rows, dim):
    half = rows // 2
    out = lax.broadcasted_iota(jnp.int32, (rows, rows), dim)
    col = lax.broadcasted_iota(jnp.int32, (rows, rows), 1 - dim)
    place = jnp.where(out < half, out, out - half)
    source = ((place >> 2) << 3) | (place & (CAP - 1)) | jnp.where(out < half, 0, CAP)
    return jnp.where(col == source, 1.0, 0.0).astype(jnp.bfloat16)


def forward_kernel(
    steps, recv_ref, plan_ref, w_in_0, w_out_0, w_in_hbm, w_out_hbm,
    ret_ref, x_t_ref, g_ref, act_ref, d_pre_ref, pick_ref, gate_ref, d_out_hbm,
    w_in_ref, w_out_ref, x_ref, act_t_ref, stage, out_acc, back_acc, sem_in, sem_out, sem_left,
):
    width, depth = w_in_0.shape
    low = jnp.bfloat16

    def copies(step):
        cols = pl.ds(pl.multiple_of(step * depth, depth), depth)
        slot = step - 1
        return (
            pltpu.make_async_copy(w_in_hbm.at[:, cols], w_in_ref.at[slot], sem_in.at[slot]),
            pltpu.make_async_copy(w_out_hbm.at[cols, :], w_out_ref.at[slot], sem_out.at[slot]),
        )

    def leave(step):
        rows = pl.ds(pl.multiple_of(step * depth, depth), EARLY)
        slot = lax.rem(step, 2)
        return pltpu.make_async_copy(stage.at[slot], d_out_hbm.at[rows, :], sem_left.at[slot])

    def begin(step):
        for copy in copies(step):
            copy.start()

    for step in range(1, min(4, steps)):
        begin(step)
    rows = recv_ref.shape[0]
    half = rows // 2
    found = jnp.dot(row_order(rows, 0), recv_ref[...], preferred_element_type=jnp.float32)
    x_rows = found[:half]
    x_ref[...] = x_rows.astype(low)
    g_ref[...] = found[half:].astype(low)
    out_acc[...] = jnp.zeros_like(out_acc)
    back_acc[...] = jnp.zeros_like(back_acc)

    def weights(step):
        if isinstance(step, int) and step == 0:
            return w_in_0, w_out_0
        return w_in_ref.at[step - 1], w_out_ref.at[step - 1]

    def front_dots(step, found):
        w_first, w_second = weights(step)
        for first in range(0, depth, 256):
            cols = slice(first, min(first + 256, depth))
            pre = []

            def one(cols=cols, pre=pre):
                pre.append(
                    jnp.dot(
                        x_ref[...], w_first[:, cols], preferred_element_type=jnp.float32
                    )
                )

            def two(cols=cols, pre=pre):
                d_act = lax.dot_general(
                    g_ref[...],
                    w_second[cols, :],
                    LAST_DIM,
                    preferred_element_type=jnp.float32,
                )
                found.append((cols, pre[0], d_act))

            yield one
            yield two

    def back_dots(step, act, d_pre):
        w_first, w_second = weights(step)
        for first in range(0, width, 256):
            cols = slice(first, min(first + 256, width))

            def one(cols=cols):
                out_acc[:, cols] += jnp.dot(
                    act, w_second[:, cols], preferred_element_type=jnp.float32
                )

            def two(cols=cols):
                back_acc[:, cols] += lax.dot_general(
                    d_pre,
                    w_first[cols, :],
                    LAST_DIM,
                    preferred_element_type=jnp.float32,
                )

            yield one
            yield two

    def grad_dots(step, act_t):
        slot = lax.rem(step, 2)
        for first in range(0, width, 256):
            cols = slice(first, min(first + 256, width))

            def one(cols=cols):
                stage[slot, :, cols] = jnp.dot(
                    act_t, g_ref[:, cols], preferred_element_type=jnp.float32
                ).astype(low)

            yield one

    def middle(step, found):
        for cols, pre, d_act in found:
            value, slope = gelu_parts(pre)
            act_ref[step, :, cols] = value.astype(low)
            d_pre_ref[step, :, cols] = (d_act * slope).astype(low)
            if cols.start == 0:
                act_t_ref[...] = jnp.transpose(value[:, 0:EARLY], (1, 0)).astype(low)

    def run(first, second):
        done = 0
        for index, thunk in enumerate(first):
            thunk()
            due = (index + 1) * len(second) // len(first)
            for other in second[done:due]:
                other()
            done = due

    def both(step, extra=()):
        for copy in copies(step):
            copy.wait()
        act, act_t, d_pre = act_ref[step - 1], act_t_ref[...], d_pre_ref[step - 1]
        found = []
        fronts = [*front_dots(step, found)]
        backs = [*back_dots(step - 1, act, d_pre)]
        blocks = len(fronts) // 2
        share = len(backs) // (blocks + 1)
        turns = []
        for block in range(blocks):
            turns += fronts[2 * block:2 * block + 2]
            turns += backs[share * block:share * (block + 1)]
            turns.append(lambda block=block: middle(step, found[block:block + 1]))
        turns += [*extra, *backs[share * blocks:]]
        run(turns, [*grad_dots(step - 1, act_t)])
        leave(step - 1).start()

    found = []
    run(
        [*front_dots(0, found)],
        [lambda step=step: begin(step) for step in range(4, steps)],
    )
    middle(0, found)

    def aside():
        x_t_ref[...] = jnp.transpose(x_rows, (1, 0)).astype(low)
        tables(plan_ref, pick_ref, gate_ref)

    if steps > 1:
        both(1, (aside,))
    else:
        aside()

    def body(step, carry):
        @pl.when(step > 2)
        def _():
            leave(step - 3).wait()

        both(step)
        return carry

    lax.fori_loop(2, steps, body, 0)
    last = steps - 1
    if steps > 2:
        leave(last - 2).wait()
    for thunk in grad_dots(last, act_t_ref[...]):
        thunk()
    leave(last).start()
    for thunk in back_dots(last, act_ref[last], d_pre_ref[last]):
        thunk()
    sums = jnp.concatenate([out_acc[...], back_acc[...]], axis=0).astype(low)
    ret = jnp.dot(row_order(rows, 1), sums, preferred_element_type=jnp.float32)
    ret_ref[...] = ret.astype(low)
    if steps > 1:
        leave(last - 1).wait()
    leave(last).wait()


def product(out_ref, left, right, tall, wide):
    rows, cols = out_ref.shape
    for col in range(0, cols, wide):
        col_end = min(col + wide, cols)
        for row in range(0, rows, tall):
            row_end = min(row + tall, rows)
            out_ref[row:row_end, col:col_end] = jnp.dot(
                left[row:row_end], right[:, col:col_end], preferred_element_type=jnp.float32
            ).astype(jnp.bfloat16)


def grads_kernel(
    x_t_ref, g_ref, act_ref, d_pre_ref, _, d_in_hbm, d_out_hbm, d_in_stage, d_out_stage, sem
):
    steps, _, depth = act_ref.shape
    width = x_t_ref.shape[0]
    slots = d_in_stage.shape[0]
    later = depth - EARLY

    def leave(step):
        slot = lax.rem(step, slots)
        cols = pl.ds(pl.multiple_of(step * depth, depth), depth)
        pairs = []
        for index in range(2):
            some = pl.ds(index * (width // 2), width // 2)
            pairs.append((d_in_stage.at[slot, some], d_in_hbm.at[some, cols]))
        for index in range(2):
            first = index * (later // 2)
            here = pl.ds(first, later // 2)
            there = pl.ds(pl.multiple_of(step * depth + EARLY + first, 64), later // 2)
            pairs.append((d_out_stage.at[slot, here], d_out_hbm.at[there]))
        return [
            pltpu.make_async_copy(*pair, sem.at[slot, index]) for index, pair in enumerate(pairs)
        ]

    def work(step, carry):
        @pl.when(step >= slots)
        def _():
            for copy in leave(step - slots):
                copy.wait()

        slot = lax.rem(step, slots)
        copies = leave(step)
        act_t = jnp.transpose(act_ref[step].astype(jnp.float32), (1, 0)).astype(jnp.bfloat16)
        product(d_in_stage.at[slot], x_t_ref[...], d_pre_ref[step], 208, 256)
        for copy in copies[:2]:
            copy.start()
        product(d_out_stage.at[slot], act_t[EARLY:], g_ref[...], 192, 256)
        for copy in copies[2:]:
            copy.start()
        return carry

    lax.fori_loop(0, steps, work, 0)
    for step in range(max(steps - slots, 0), steps):
        for copy in leave(step):
            copy.wait()


def combine_kernel(ret_ref, pick_ref, gate_ref, cot_ref, mixed_ref, d_tok_ref, d_gate_ref):
    count = cot_ref.shape[0]
    rows = pick_ref.shape[1]
    found = None
    for first in range(0, ret_ref.shape[0], rows):
        part = jnp.dot(
            pick_ref[...], ret_ref[first:first + rows, :], preferred_element_type=jnp.float32
        )
        found = part if found is None else found + part
    o_0, o_1 = found[:count], found[count:2 * count]
    mixed_ref[...] = (gate_ref[:, 2:3] * o_0 + gate_ref[:, 3:4] * o_1).astype(jnp.bfloat16)
    d_tok_ref[...] = found[2 * count:].astype(jnp.bfloat16)
    cot = cot_ref[...].astype(jnp.float32)
    d_0 = jnp.sum(cot * o_0, axis=1, keepdims=True)
    d_1 = jnp.sum(cot * o_1, axis=1, keepdims=True)
    lane = lax.broadcasted_iota(jnp.int32, (count, 8), 1)
    both = jnp.where(lane == 0, d_0, jnp.where(lane == 1, d_1, 0.0))
    d_gate_ref[...] = jnp.transpose(both, (1, 0))[0:2, :]


def params(mib):
    return pltpu.CompilerParams(vmem_limit_bytes=mib * 1024 * 1024)


def chunk_of(hidden, want):
    return max(size for size in range(128, want + 1, 128) if hidden % size == 0)


def per_device(tokens, expert_ids, priority, gates, w_in, w_out, cotangent):
    count, width = tokens.shape
    repl = lax.axis_size("expert") // EXPERTS
    slots = EXPERTS * PAIR
    hidden = w_in.shape[2]
    ids_t = jnp.transpose(expert_ids, (1, 0))
    gates_t = jnp.transpose(gates, (1, 0))
    low = jnp.bfloat16
    vmem = pl.BlockSpec(memory_space=pltpu.VMEM)
    hbm = pl.BlockSpec(memory_space=pl.ANY)
    chunk = chunk_of(hidden, 512)
    steps = hidden // chunk
    send, plan, w_in_0, w_out_0 = pl.pallas_call(
        dispatch_kernel,
        out_shape=(
            pltpu.VMEM((slots, width), low),
            pltpu.VMEM((8, count), jnp.float32),
            pltpu.VMEM((width, chunk), low),
            pltpu.VMEM((chunk, width), low),
        ),
        in_specs=[hbm] * 7,
        out_specs=(vmem,) * 4,
        scratch_shapes=[
            pltpu.VMEM((2, count), jnp.int32),
            pltpu.VMEM((1, count), jnp.int32),
            pltpu.VMEM((2, count), jnp.float32),
            pltpu.VMEM((2 * count, width), low),
            pltpu.SemaphoreType.DMA((7,)),
        ],
        compiler_params=params(50),
        name="dispatch",
    )(*(pltpu.with_memory_space_constraint(array, pltpu.HBM) for array in (
        ids_t, priority, gates_t, tokens, cotangent, w_in[0], w_out[0]
    )))
    send = jnp.tile(send.reshape(EXPERTS, PAIR, width), (repl, 1, 1))
    recv = lax.all_to_all(send, "expert", split_axis=0, concat_axis=0, tiled=True)
    rows = recv.shape[0] * PAIR
    recv = recv.reshape(rows, width)
    half = rows // 2
    ret, x_t, g_rows, act, d_pre, pick, gate_cols, d_w_out = pl.pallas_call(
        functools.partial(forward_kernel, steps),
        out_shape=(
            pltpu.VMEM((rows, width), low),
            jax.ShapeDtypeStruct((width, half), low),
            jax.ShapeDtypeStruct((half, width), low),
            jax.ShapeDtypeStruct((steps, half, chunk), low),
            jax.ShapeDtypeStruct((steps, half, chunk), low),
            jax.ShapeDtypeStruct((3 * count, slots), low),
            jax.ShapeDtypeStruct((count, 8), jnp.float32),
            jax.ShapeDtypeStruct((hidden, width), low),
        ),
        in_specs=[vmem] * 4 + [hbm] * 2,
        out_specs=(vmem,) * 7 + (hbm,),
        scratch_shapes=[
            pltpu.VMEM((max(steps - 1, 1), width, chunk), low),
            pltpu.VMEM((max(steps - 1, 1), chunk, width), low),
            pltpu.VMEM((half, width), low),
            pltpu.VMEM((EARLY, half), low),
            pltpu.VMEM((2, EARLY, width), low),
            pltpu.VMEM((half, width), jnp.float32),
            pltpu.VMEM((half, width), jnp.float32),
            pltpu.SemaphoreType.DMA((max(steps - 1, 1),)),
            pltpu.SemaphoreType.DMA((max(steps - 1, 1),)),
            pltpu.SemaphoreType.DMA((2,)),
        ],
        compiler_params=params(43),
        cost_estimate=pl.CostEstimate(
            flops=8 * half * width * hidden,
            bytes_accessed=4 * width * hidden,
            transcendentals=half * hidden,
        ),
        name="forward",
    )(recv, plan, w_in_0, w_out_0, w_in[0], w_out[0])
    ret = lax.all_to_all(
        ret.reshape(rows // PAIR, PAIR, width), "expert", split_axis=0, concat_axis=0, tiled=True
    ).reshape(rows, width)
    d_w_in, d_w_out = pl.pallas_call(
        grads_kernel,
        out_shape=(
            jax.ShapeDtypeStruct((width, hidden), low),
            jax.ShapeDtypeStruct((hidden, width), low),
        ),
        in_specs=[vmem] * 4 + [hbm],
        out_specs=(hbm,) * 2,
        input_output_aliases={4: 1},
        scratch_shapes=[
            pltpu.VMEM((3, width, chunk), low),
            pltpu.VMEM((3, chunk - EARLY, width), low),
            pltpu.SemaphoreType.DMA((3, 4)),
        ],
        compiler_params=params(24),
        cost_estimate=pl.CostEstimate(
            flops=4 * half * width * hidden,
            bytes_accessed=4 * width * hidden,
            transcendentals=0,
        ),
        name="grads",
    )(x_t, g_rows, act, d_pre, d_w_out)
    mixed, d_tokens, d_gates_t = pl.pallas_call(
        combine_kernel,
        out_shape=(
            jax.ShapeDtypeStruct((count, width), low),
            jax.ShapeDtypeStruct((count, width), low),
            jax.ShapeDtypeStruct((2, count), jnp.float32),
        ),
        compiler_params=params(12),
        name="combine",
    )(ret, pick, gate_cols, cotangent)
    return (mixed, d_tokens, jnp.transpose(d_gates_t, (1, 0)), d_w_in[None], d_w_out[None])


def solution(mesh):
    rows = P(("groups", "expert"), None)
    return jax.shard_map(
        per_device,
        mesh=mesh,
        in_specs=(rows, rows, rows, rows, P("expert", None, None), P("expert", None, None), rows),
        out_specs=(
            rows,
            rows,
            rows,
            P(("groups", "expert"), None, None),
            P(("groups", "expert"), None, None),
        ),
        check_vma=False,
    )
```

```python
import functools
import math

import jax
import jax.numpy as jnp
from jax import lax
from jax.experimental import pallas as pl
from jax.experimental.pallas import tpu as pltpu
from jax.sharding import PartitionSpec as P

EXPERTS = 16
CAP = 4
PAIR = 2 * CAP
EARLY = 128
LAST_DIM = (((1,), (1,)), ((), ()))


def gelu_parts(value):
    coef = math.sqrt(2.0 / math.pi)
    square = value * value
    hyper = jnp.tanh(coef * value * (1.0 + 0.044715 * square))
    half = 0.5 * (1.0 + hyper)
    slope = half + 0.5 * value * (1.0 - hyper * hyper) * coef * (1.0 + 3.0 * 0.044715 * square)
    return (value * half, slope)


def place_rows(ids_t, prio):
    count = ids_t.shape[1]
    first = ids_t[0:1, :]
    second = ids_t[1:2, :]
    stack = jnp.concatenate([first, second, prio, jnp.zeros((5, count), jnp.int32)], axis=0)
    columns = jnp.transpose(stack.astype(jnp.float32), (1, 0)).astype(jnp.int32)
    first_c, second_c, prio_c = columns[:, 0:1], columns[:, 1:2], columns[:, 2:3]
    ahead = prio_c < prio
    one = jnp.float32(1.0)
    zero = jnp.float32(0.0)
    slot_0 = jnp.sum(jnp.where((first_c == first) & ahead, one, zero), axis=0, keepdims=True)
    slot_1 = jnp.sum(
        jnp.where((first_c == second) | ((second_c == second) & ahead), one, zero),
        axis=0,
        keepdims=True,
    )
    slot_0 = slot_0.astype(jnp.int32)
    slot_1 = slot_1.astype(jnp.int32)
    place_0 = jnp.where(slot_0 < CAP, first * CAP + slot_0, -1)
    place_1 = jnp.where(slot_1 < CAP, second * CAP + slot_1, -1)
    return place_0, place_1


def row_slots(count):
    row = lax.broadcasted_iota(jnp.int32, (EXPERTS * PAIR, count), 0)
    return ((row >> 3) << 2) | (row & (CAP - 1)), (row & CAP) == 0


def dispatch_kernel(
    ids_hbm, prio_hbm, gates_hbm, tok_hbm, cot_hbm, w_in_hbm, w_out_hbm,
    send_ref, plan_ref, w_in_ref, w_out_ref,
    ids_ref, prio_ref, gates_ref, both_ref, sem,
):
    count = tok_hbm.shape[0]
    depth = w_in_ref.shape[1]
    pairs = (
        (ids_hbm, ids_ref),
        (prio_hbm, prio_ref),
        (gates_hbm, gates_ref),
        (tok_hbm, both_ref.at[0:count]),
        (cot_hbm, both_ref.at[count:2 * count]),
        (w_in_hbm.at[:, 0:depth], w_in_ref),
        (w_out_hbm.at[0:depth, :], w_out_ref),
    )
    copies = [pltpu.make_async_copy(*pair, sem.at[index]) for index, pair in enumerate(pairs)]
    for copy in copies:
        copy.start()
    for copy in copies[:3]:
        copy.wait()
    place_0, place_1 = place_rows(ids_ref[...], prio_ref[...])
    slot, is_x = row_slots(count)
    hit_0 = slot == place_0
    hit_1 = slot == place_1
    hit = jnp.where(hit_0 | hit_1, 1.0, 0.0)
    pick = jnp.concatenate(
        [jnp.where(is_x, hit, 0.0), jnp.where(is_x, 0.0, hit)], axis=1
    ).astype(jnp.bfloat16)
    gate = jnp.where(hit_0, gates_ref[0:1, :], 0.0) + jnp.where(hit_1, gates_ref[1:2, :], 0.0)
    scale = jnp.sum(gate, axis=1, keepdims=True)
    scale = jnp.where(is_x[:, 0:1], 1.0, scale)
    plan_ref[...] = jnp.concatenate(
        [
            place_0.astype(jnp.float32),
            place_1.astype(jnp.float32),
            gates_ref[...],
            jnp.zeros((4, count), jnp.float32),
        ],
        axis=0,
    )
    for copy in copies[3:5]:
        copy.wait()
    found = jnp.dot(pick, both_ref[...], preferred_element_type=jnp.float32)
    send_ref[...] = (found * scale).astype(jnp.bfloat16)
    for copy in copies[5:]:
        copy.wait()


def tables(plan_ref, pick_ref, gate_ref):
    place_0 = plan_ref[0:1, :].astype(jnp.int32)
    place_1 = plan_ref[1:2, :].astype(jnp.int32)
    count = place_0.shape[1]
    slot, is_x = row_slots(count)
    hit_0 = jnp.where(slot == place_0, 1.0, 0.0)
    hit_1 = jnp.where(slot == place_1, 1.0, 0.0)
    pick_0 = jnp.transpose(jnp.where(is_x, hit_0, 0.0), (1, 0))
    pick_1 = jnp.transpose(jnp.where(is_x, hit_1, 0.0), (1, 0))
    pick_b = jnp.transpose(jnp.where(is_x, 0.0, hit_0 + hit_1), (1, 0))
    pick_ref[...] = jnp.concatenate([pick_0, pick_1, pick_b], axis=0).astype(jnp.bfloat16)
    gate_ref[...] = jnp.transpose(plan_ref[...], (1, 0))


def row_order(rows, dim):
    half = rows // 2
    out = lax.broadcasted_iota(jnp.int32, (rows, rows), dim)
    col = lax.broadcasted_iota(jnp.int32, (rows, rows), 1 - dim)
    place = jnp.where(out < half, out, out - half)
    source = ((place >> 2) << 3) | (place & (CAP - 1)) | jnp.where(out < half, 0, CAP)
    return jnp.where(col == source, 1.0, 0.0).astype(jnp.bfloat16)


def forward_kernel(
    steps, recv_ref, plan_ref, w_in_0, w_out_0, w_in_hbm, w_out_hbm,
    ret_ref, x_t_ref, g_ref, act_ref, d_pre_ref, pick_ref, gate_ref, d_out_hbm,
    w_in_ref, w_out_ref, x_ref, act_t_ref, stage, out_acc, back_acc, sem_in, sem_out, sem_left,
):
    width, depth = w_in_0.shape
    low = jnp.bfloat16

    def copies(step):
        cols = pl.ds(pl.multiple_of(step * depth, depth), depth)
        slot = step - 1
        return (
            pltpu.make_async_copy(w_in_hbm.at[:, cols], w_in_ref.at[slot], sem_in.at[slot]),
            pltpu.make_async_copy(w_out_hbm.at[cols, :], w_out_ref.at[slot], sem_out.at[slot]),
        )

    def leave(step):
        rows = pl.ds(pl.multiple_of(step * depth, depth), EARLY)
        slot = lax.rem(step, 2)
        return pltpu.make_async_copy(stage.at[slot], d_out_hbm.at[rows, :], sem_left.at[slot])

    def begin(step, carry):
        for copy in copies(step):
            copy.start()
        return carry

    lax.fori_loop(1, steps, begin, 0)
    rows = recv_ref.shape[0]
    half = rows // 2
    found = jnp.dot(row_order(rows, 0), recv_ref[...], preferred_element_type=jnp.float32)
    x_rows = found[:half]
    x_ref[...] = x_rows.astype(low)
    g_ref[...] = found[half:].astype(low)
    out_acc[...] = jnp.zeros_like(out_acc)
    back_acc[...] = jnp.zeros_like(back_acc)

    def weights(step):
        if isinstance(step, int) and step == 0:
            return w_in_0, w_out_0
        return w_in_ref.at[step - 1], w_out_ref.at[step - 1]

    def front_dots(step, found):
        w_first, w_second = weights(step)
        for first in range(0, depth, 512):
            cols = slice(first, min(first + 512, depth))
            pre = []

            def one(cols=cols, pre=pre):
                pre.append(
                    jnp.dot(
                        x_ref[...], w_first[:, cols], preferred_element_type=jnp.float32
                    )
                )

            def two(cols=cols, pre=pre):
                d_act = lax.dot_general(
                    g_ref[...],
                    w_second[cols, :],
                    LAST_DIM,
                    preferred_element_type=jnp.float32,
                )
                found.append((cols, pre[0], d_act))

            yield one
            yield two

    def back_dots(step, act, d_pre):
        w_first, w_second = weights(step)
        for first in range(0, width, 256):
            cols = slice(first, min(first + 256, width))

            def one(cols=cols):
                out_acc[:, cols] += jnp.dot(
                    act, w_second[:, cols], preferred_element_type=jnp.float32
                )

            def two(cols=cols):
                back_acc[:, cols] += lax.dot_general(
                    d_pre,
                    w_first[cols, :],
                    LAST_DIM,
                    preferred_element_type=jnp.float32,
                )

            yield one
            yield two

    def grad_dots(step, act_t):
        slot = lax.rem(step, 2)
        for first in range(0, width, 256):
            cols = slice(first, min(first + 256, width))

            def one(cols=cols):
                stage[slot, :, cols] = jnp.dot(
                    act_t, g_ref[:, cols], preferred_element_type=jnp.float32
                ).astype(low)

            yield one

    def middle(step, found):
        for cols, pre, d_act in found:
            value, slope = gelu_parts(pre)
            act_ref[step, :, cols] = value.astype(low)
            d_pre_ref[step, :, cols] = (d_act * slope).astype(low)
            if cols.start == 0:
                act_t_ref[...] = jnp.transpose(value[:, 0:EARLY], (1, 0)).astype(low)

    def run(first, second):
        done = 0
        for index, thunk in enumerate(first):
            thunk()
            due = (index + 1) * len(second) // len(first)
            for other in second[done:due]:
                other()
            done = due

    def both(step, extra=()):
        for copy in copies(step):
            copy.wait()
        act, act_t, d_pre = act_ref[step - 1], act_t_ref[...], d_pre_ref[step - 1]
        found = []
        fronts = [*front_dots(step, found)]
        backs = [*back_dots(step - 1, act, d_pre)]
        blocks = len(fronts) // 2
        share = len(backs) // (blocks + 1)
        turns = []
        for block in range(blocks):
            turns += fronts[2 * block:2 * block + 2]
            turns += backs[share * block:share * (block + 1)]
            turns.append(lambda block=block: middle(step, found[block:block + 1]))
        turns += [*extra, *backs[share * blocks:]]
        run(turns, [*grad_dots(step - 1, act_t)])
        leave(step - 1).start()

    found = []
    for thunk in front_dots(0, found):
        thunk()
    middle(0, found)

    def aside():
        x_t_ref[...] = jnp.transpose(x_rows, (1, 0)).astype(low)
        tables(plan_ref, pick_ref, gate_ref)

    if steps > 1:
        both(1, (aside,))
    else:
        aside()

    def body(step, carry):
        @pl.when(step > 2)
        def _():
            leave(step - 3).wait()

        both(step)
        return carry

    lax.fori_loop(2, steps, body, 0)
    last = steps - 1
    if steps > 2:
        leave(last - 2).wait()
    for thunk in grad_dots(last, act_t_ref[...]):
        thunk()
    leave(last).start()
    for thunk in back_dots(last, act_ref[last], d_pre_ref[last]):
        thunk()
    sums = jnp.concatenate([out_acc[...], back_acc[...]], axis=0).astype(low)
    ret = jnp.dot(row_order(rows, 1), sums, preferred_element_type=jnp.float32)
    ret_ref[...] = ret.astype(low)
    if steps > 1:
        leave(last - 1).wait()
    leave(last).wait()


def product(out_ref, left, right, tall, wide):
    rows, cols = out_ref.shape
    for col in range(0, cols, wide):
        col_end = min(col + wide, cols)
        for row in range(0, rows, tall):
            row_end = min(row + tall, rows)
            out_ref[row:row_end, col:col_end] = jnp.dot(
                left[row:row_end], right[:, col:col_end], preferred_element_type=jnp.float32
            ).astype(jnp.bfloat16)


def grads_kernel(
    x_t_ref, g_ref, act_ref, d_pre_ref, _, d_in_hbm, d_out_hbm, d_in_stage, d_out_stage, sem
):
    steps, _, depth = act_ref.shape
    slots, strip, _ = d_in_stage.shape
    strips = x_t_ref.shape[0] // strip
    later = depth - EARLY

    def leave_in(step):
        slot = lax.rem(step, slots)
        copies = []
        for index in range(2):
            first = index * (strip // 2)
            here = pl.ds(first, strip // 2)
            there = pl.ds(pl.multiple_of(step * strip + first, 64), strip // 2)
            copies.append(
                pltpu.make_async_copy(
                    d_in_stage.at[slot, here], d_in_hbm.at[there], sem.at[slot, index]
                )
            )
        return copies

    def leave_out(step):
        slot = lax.rem(step, slots)
        copies = []
        for index in range(2):
            first = index * (later // 2)
            here = pl.ds(first, later // 2)
            there = pl.ds(pl.multiple_of(step * depth + EARLY + first, 64), later // 2)
            copies.append(
                pltpu.make_async_copy(
                    d_out_stage.at[slot, here], d_out_hbm.at[there], sem.at[slot, 2 + index]
                )
            )
        return copies

    def work(step, carry):
        @pl.when(step >= slots)
        def _():
            for copy in leave_in(step - slots):
                copy.wait()

        slot = lax.rem(step, slots)
        x_t = x_t_ref[pl.ds(pl.multiple_of(step * strip, strip), strip), :]
        for part in range(steps):
            cols = pl.ds(part * depth, depth)
            product(d_in_stage.at[slot, :, cols], x_t, d_pre_ref[part], strip, 256)
        for copy in leave_in(step):
            copy.start()

        @pl.when((step >= slots) & (step < steps + slots))
        def _():
            for copy in leave_out(step - slots):
                copy.wait()

        @pl.when(step < steps)
        def _():
            act_t = jnp.transpose(act_ref[step].astype(jnp.float32), (1, 0)).astype(jnp.bfloat16)
            product(d_out_stage.at[slot], act_t[EARLY:], g_ref[...], later, 256)
            for copy in leave_out(step):
                copy.start()

        return carry

    lax.fori_loop(0, strips, work, 0)
    for step in range(max(strips - slots, 0), strips):
        for copy in leave_in(step):
            copy.wait()
    for step in range(max(strips - slots, 0), steps):
        for copy in leave_out(step):
            copy.wait()


def combine_kernel(ret_ref, pick_ref, gate_ref, cot_ref, mixed_ref, d_tok_ref, d_gate_ref):
    count = cot_ref.shape[0]
    rows = pick_ref.shape[1]
    found = None
    for first in range(0, ret_ref.shape[0], rows):
        part = jnp.dot(
            pick_ref[...], ret_ref[first:first + rows, :], preferred_element_type=jnp.float32
        )
        found = part if found is None else found + part
    o_0, o_1 = found[:count], found[count:2 * count]
    mixed_ref[...] = (gate_ref[:, 2:3] * o_0 + gate_ref[:, 3:4] * o_1).astype(jnp.bfloat16)
    d_tok_ref[...] = found[2 * count:].astype(jnp.bfloat16)
    cot = cot_ref[...].astype(jnp.float32)
    d_0 = jnp.sum(cot * o_0, axis=1, keepdims=True)
    d_1 = jnp.sum(cot * o_1, axis=1, keepdims=True)
    lane = lax.broadcasted_iota(jnp.int32, (count, 8), 1)
    both = jnp.where(lane == 0, d_0, jnp.where(lane == 1, d_1, 0.0))
    d_gate_ref[...] = jnp.transpose(both, (1, 0))[0:2, :]


def params(mib):
    return pltpu.CompilerParams(vmem_limit_bytes=mib * 1024 * 1024)


def chunk_of(hidden, want):
    return max(size for size in range(128, want + 1, 128) if hidden % size == 0)


def per_device(tokens, expert_ids, priority, gates, w_in, w_out, cotangent):
    count, width = tokens.shape
    repl = lax.axis_size("expert") // EXPERTS
    slots = EXPERTS * PAIR
    hidden = w_in.shape[2]
    ids_t = jnp.transpose(expert_ids, (1, 0))
    gates_t = jnp.transpose(gates, (1, 0))
    low = jnp.bfloat16
    vmem = pl.BlockSpec(memory_space=pltpu.VMEM)
    hbm = pl.BlockSpec(memory_space=pl.ANY)
    chunk = chunk_of(hidden, 512)
    steps = hidden // chunk
    send, plan, w_in_0, w_out_0 = pl.pallas_call(
        dispatch_kernel,
        out_shape=(
            pltpu.VMEM((slots, width), low),
            pltpu.VMEM((8, count), jnp.float32),
            pltpu.VMEM((width, chunk), low),
            pltpu.VMEM((chunk, width), low),
        ),
        in_specs=[hbm] * 7,
        out_specs=(vmem,) * 4,
        scratch_shapes=[
            pltpu.VMEM((2, count), jnp.int32),
            pltpu.VMEM((1, count), jnp.int32),
            pltpu.VMEM((2, count), jnp.float32),
            pltpu.VMEM((2 * count, width), low),
            pltpu.SemaphoreType.DMA((7,)),
        ],
        compiler_params=params(50),
        name="dispatch",
    )(*(pltpu.with_memory_space_constraint(array, pltpu.HBM) for array in (
        ids_t, priority, gates_t, tokens, cotangent, w_in[0], w_out[0]
    )))
    send = jnp.tile(send.reshape(EXPERTS, PAIR, width), (repl, 1, 1))
    recv = lax.all_to_all(send, "expert", split_axis=0, concat_axis=0, tiled=True)
    rows = recv.shape[0] * PAIR
    recv = recv.reshape(rows, width)
    half = rows // 2
    ret, x_t, g_rows, act, d_pre, pick, gate_cols, d_w_out = pl.pallas_call(
        functools.partial(forward_kernel, steps),
        out_shape=(
            pltpu.VMEM((rows, width), low),
            jax.ShapeDtypeStruct((width, half), low),
            jax.ShapeDtypeStruct((half, width), low),
            jax.ShapeDtypeStruct((steps, half, chunk), low),
            jax.ShapeDtypeStruct((steps, half, chunk), low),
            jax.ShapeDtypeStruct((3 * count, slots), low),
            jax.ShapeDtypeStruct((count, 8), jnp.float32),
            jax.ShapeDtypeStruct((hidden, width), low),
        ),
        in_specs=[vmem] * 4 + [hbm] * 2,
        out_specs=(vmem,) * 7 + (hbm,),
        scratch_shapes=[
            pltpu.VMEM((max(steps - 1, 1), width, chunk), low),
            pltpu.VMEM((max(steps - 1, 1), chunk, width), low),
            pltpu.VMEM((half, width), low),
            pltpu.VMEM((EARLY, half), low),
            pltpu.VMEM((2, EARLY, width), low),
            pltpu.VMEM((half, width), jnp.float32),
            pltpu.VMEM((half, width), jnp.float32),
            pltpu.SemaphoreType.DMA((max(steps - 1, 1),)),
            pltpu.SemaphoreType.DMA((max(steps - 1, 1),)),
            pltpu.SemaphoreType.DMA((2,)),
        ],
        compiler_params=params(43),
        cost_estimate=pl.CostEstimate(
            flops=8 * half * width * hidden,
            bytes_accessed=4 * width * hidden,
            transcendentals=half * hidden,
        ),
        name="forward",
    )(recv, plan, w_in_0, w_out_0, w_in[0], w_out[0])
    ret = lax.all_to_all(
        ret.reshape(rows // PAIR, PAIR, width), "expert", split_axis=0, concat_axis=0, tiled=True
    ).reshape(rows, width)
    d_w_in, d_w_out = pl.pallas_call(
        grads_kernel,
        out_shape=(
            jax.ShapeDtypeStruct((width, hidden), low),
            jax.ShapeDtypeStruct((hidden, width), low),
        ),
        in_specs=[vmem] * 4 + [hbm],
        out_specs=(hbm,) * 2,
        input_output_aliases={4: 1},
        scratch_shapes=[
            pltpu.VMEM((3, 128, hidden), low),
            pltpu.VMEM((3, chunk - EARLY, width), low),
            pltpu.SemaphoreType.DMA((3, 4)),
        ],
        compiler_params=params(24),
        cost_estimate=pl.CostEstimate(
            flops=4 * half * width * hidden,
            bytes_accessed=4 * width * hidden,
            transcendentals=0,
        ),
        name="grads",
    )(x_t, g_rows, act, d_pre, d_w_out)
    mixed, d_tokens, d_gates_t = pl.pallas_call(
        combine_kernel,
        out_shape=(
            jax.ShapeDtypeStruct((count, width), low),
            jax.ShapeDtypeStruct((count, width), low),
            jax.ShapeDtypeStruct((2, count), jnp.float32),
        ),
        compiler_params=params(12),
        name="combine",
    )(ret, pick, gate_cols, cotangent)
    return (mixed, d_tokens, jnp.transpose(d_gates_t, (1, 0)), d_w_in[None], d_w_out[None])


def solution(mesh):
    rows = P(("groups", "expert"), None)
    return jax.shard_map(
        per_device,
        mesh=mesh,
        in_specs=(rows, rows, rows, rows, P("expert", None, None), P("expert", None, None), rows),
        out_specs=(
            rows,
            rows,
            rows,
            P(("groups", "expert"), None, None),
            P(("groups", "expert"), None, None),
        ),
        check_vma=False,
    )
```

```python
import functools
import math

import jax
import jax.numpy as jnp
from jax import lax
from jax.experimental import pallas as pl
from jax.experimental.pallas import tpu as pltpu
from jax.sharding import PartitionSpec as P

EXPERTS = 16
CAP = 4
PAIR = 2 * CAP
EARLY = 64
LAST_DIM = (((1,), (1,)), ((), ()))


def gelu_parts(value):
    coef = math.sqrt(2.0 / math.pi)
    square = value * value
    hyper = jnp.tanh(coef * value * (1.0 + 0.044715 * square))
    half = 0.5 * (1.0 + hyper)
    slope = half + 0.5 * value * (1.0 - hyper * hyper) * coef * (1.0 + 3.0 * 0.044715 * square)
    return (value * half, slope)


def place_rows(ids_t, prio):
    count = ids_t.shape[1]
    first = ids_t[0:1, :]
    second = ids_t[1:2, :]
    stack = jnp.concatenate([first, second, prio, jnp.zeros((5, count), jnp.int32)], axis=0)
    columns = jnp.transpose(stack.astype(jnp.float32), (1, 0)).astype(jnp.int32)
    first_c, second_c, prio_c = columns[:, 0:1], columns[:, 1:2], columns[:, 2:3]
    ahead = prio_c < prio
    one = jnp.float32(1.0)
    zero = jnp.float32(0.0)
    slot_0 = jnp.sum(jnp.where((first_c == first) & ahead, one, zero), axis=0, keepdims=True)
    slot_1 = jnp.sum(
        jnp.where((first_c == second) | ((second_c == second) & ahead), one, zero),
        axis=0,
        keepdims=True,
    )
    slot_0 = slot_0.astype(jnp.int32)
    slot_1 = slot_1.astype(jnp.int32)
    place_0 = jnp.where(slot_0 < CAP, first * CAP + slot_0, -1)
    place_1 = jnp.where(slot_1 < CAP, second * CAP + slot_1, -1)
    return place_0, place_1


def row_slots(count):
    row = lax.broadcasted_iota(jnp.int32, (EXPERTS * PAIR, count), 0)
    return ((row >> 3) << 2) | (row & (CAP - 1)), (row & CAP) == 0


def dispatch_kernel(
    ids_hbm, prio_hbm, gates_hbm, tok_hbm, cot_hbm, w_in_hbm, w_out_hbm,
    send_ref, plan_ref, w_in_ref, w_out_ref,
    ids_ref, prio_ref, gates_ref, both_ref, sem,
):
    count = tok_hbm.shape[0]
    depth = w_in_ref.shape[1]
    pairs = (
        (ids_hbm, ids_ref),
        (prio_hbm, prio_ref),
        (gates_hbm, gates_ref),
        (tok_hbm, both_ref.at[0:count]),
        (cot_hbm, both_ref.at[count:2 * count]),
        (w_in_hbm.at[:, 0:depth], w_in_ref),
        (w_out_hbm.at[0:depth, :], w_out_ref),
    )
    copies = [pltpu.make_async_copy(*pair, sem.at[index]) for index, pair in enumerate(pairs)]
    for copy in copies:
        copy.start()
    for copy in copies[:3]:
        copy.wait()
    place_0, place_1 = place_rows(ids_ref[...], prio_ref[...])
    slot, is_x = row_slots(count)
    hit_0 = slot == place_0
    hit_1 = slot == place_1
    hit = jnp.where(hit_0 | hit_1, 1.0, 0.0)
    pick = jnp.concatenate(
        [jnp.where(is_x, hit, 0.0), jnp.where(is_x, 0.0, hit)], axis=1
    ).astype(jnp.bfloat16)
    gate = jnp.where(hit_0, gates_ref[0:1, :], 0.0) + jnp.where(hit_1, gates_ref[1:2, :], 0.0)
    scale = jnp.sum(gate, axis=1, keepdims=True)
    scale = jnp.where(is_x[:, 0:1], 1.0, scale)
    plan_ref[...] = jnp.concatenate(
        [
            place_0.astype(jnp.float32),
            place_1.astype(jnp.float32),
            gates_ref[...],
            jnp.zeros((4, count), jnp.float32),
        ],
        axis=0,
    )
    for copy in copies[3:5]:
        copy.wait()
    found = jnp.dot(pick, both_ref[...], preferred_element_type=jnp.float32)
    send_ref[...] = (found * scale).astype(jnp.bfloat16)
    for copy in copies[5:]:
        copy.wait()


def tables(plan_ref, pick_ref, gate_ref):
    place_0 = plan_ref[0:1, :].astype(jnp.int32)
    place_1 = plan_ref[1:2, :].astype(jnp.int32)
    count = place_0.shape[1]
    slot, is_x = row_slots(count)
    hit_0 = jnp.where(slot == place_0, 1.0, 0.0)
    hit_1 = jnp.where(slot == place_1, 1.0, 0.0)
    pick_0 = jnp.transpose(jnp.where(is_x, hit_0, 0.0), (1, 0))
    pick_1 = jnp.transpose(jnp.where(is_x, hit_1, 0.0), (1, 0))
    pick_b = jnp.transpose(jnp.where(is_x, 0.0, hit_0 + hit_1), (1, 0))
    pick_ref[...] = jnp.concatenate([pick_0, pick_1, pick_b], axis=0).astype(jnp.bfloat16)
    gate_ref[...] = jnp.transpose(plan_ref[...], (1, 0))


def row_order(rows, dim):
    half = rows // 2
    out = lax.broadcasted_iota(jnp.int32, (rows, rows), dim)
    col = lax.broadcasted_iota(jnp.int32, (rows, rows), 1 - dim)
    place = jnp.where(out < half, out, out - half)
    source = ((place >> 2) << 3) | (place & (CAP - 1)) | jnp.where(out < half, 0, CAP)
    return jnp.where(col == source, 1.0, 0.0).astype(jnp.bfloat16)


def forward_kernel(
    steps, recv_ref, plan_ref, w_in_0, w_out_0, w_in_hbm, w_out_hbm,
    ret_ref, x_t_ref, g_ref, act_ref, d_pre_ref, pick_ref, gate_ref, d_out_hbm,
    w_in_ref, w_out_ref, x_ref, act_t_ref, stage, out_acc, back_acc, sem_in, sem_out, sem_left,
):
    width, depth = w_in_0.shape
    low = jnp.bfloat16

    def copies(step):
        cols = pl.ds(pl.multiple_of(step * depth, depth), depth)
        slot = step - 1
        return (
            pltpu.make_async_copy(w_in_hbm.at[:, cols], w_in_ref.at[slot], sem_in.at[slot]),
            pltpu.make_async_copy(w_out_hbm.at[cols, :], w_out_ref.at[slot], sem_out.at[slot]),
        )

    def leave(step):
        rows = pl.ds(pl.multiple_of(step * depth, depth), EARLY)
        slot = lax.rem(step, 2)
        return pltpu.make_async_copy(stage.at[slot], d_out_hbm.at[rows, :], sem_left.at[slot])

    def begin(step, carry):
        for copy in copies(step):
            copy.start()
        return carry

    lax.fori_loop(1, steps, begin, 0)
    rows = recv_ref.shape[0]
    half = rows // 2
    found = jnp.dot(row_order(rows, 0), recv_ref[...], preferred_element_type=jnp.float32)
    x_rows = found[:half]
    x_ref[...] = x_rows.astype(low)
    g_ref[...] = found[half:].astype(low)
    out_acc[...] = jnp.zeros_like(out_acc)
    back_acc[...] = jnp.zeros_like(back_acc)

    def weights(step):
        if isinstance(step, int) and step == 0:
            return w_in_0, w_out_0
        return w_in_ref.at[step - 1], w_out_ref.at[step - 1]

    def front_dots(step, found):
        w_first, w_second = weights(step)
        for first in range(0, depth, 256):
            cols = slice(first, min(first + 256, depth))
            pre = []

            def one(cols=cols, pre=pre):
                pre.append(
                    jnp.dot(
                        x_ref[...], w_first[:, cols], preferred_element_type=jnp.float32
                    )
                )

            def two(cols=cols, pre=pre):
                d_act = lax.dot_general(
                    g_ref[...],
                    w_second[cols, :],
                    LAST_DIM,
                    preferred_element_type=jnp.float32,
                )
                found.append((cols, pre[0], d_act))

            yield one
            yield two

    def back_dots(step, act, d_pre):
        w_first, w_second = weights(step)
        for first in range(0, width, 256):
            cols = slice(first, min(first + 256, width))

            def one(cols=cols):
                out_acc[:, cols] += jnp.dot(
                    act, w_second[:, cols], preferred_element_type=jnp.float32
                )

            def two(cols=cols):
                back_acc[:, cols] += lax.dot_general(
                    d_pre,
                    w_first[cols, :],
                    LAST_DIM,
                    preferred_element_type=jnp.float32,
                )

            yield one
            yield two

    def grad_dots(step, act_t):
        slot = lax.rem(step, 2)
        for first in range(0, width, 256):
            cols = slice(first, min(first + 256, width))

            def one(cols=cols):
                stage[slot, :, cols] = jnp.dot(
                    act_t, g_ref[:, cols], preferred_element_type=jnp.float32
                ).astype(low)

            yield one

    def middle(step, found):
        for cols, pre, d_act in found:
            value, slope = gelu_parts(pre)
            act_ref[step, :, cols] = value.astype(low)
            d_pre_ref[step, :, cols] = (d_act * slope).astype(low)
            if cols.start == 0:
                act_t_ref[...] = jnp.transpose(value[:, 0:EARLY], (1, 0)).astype(low)

    def run(first, second):
        done = 0
        for index, thunk in enumerate(first):
            thunk()
            due = (index + 1) * len(second) // len(first)
            for other in second[done:due]:
                other()
            done = due

    def both(step, extra=()):
        for copy in copies(step):
            copy.wait()
        act, act_t, d_pre = act_ref[step - 1], act_t_ref[...], d_pre_ref[step - 1]
        found = []
        fronts = [*front_dots(step, found)]
        backs = [*back_dots(step - 1, act, d_pre)]
        blocks = len(fronts) // 2
        share = len(backs) // (blocks + 1)
        turns = []
        for block in range(blocks):
            turns += fronts[2 * block:2 * block + 2]
            turns += backs[share * block:share * (block + 1)]
            turns.append(lambda block=block: middle(step, found[block:block + 1]))
        turns += [*extra, *backs[share * blocks:]]
        run(turns, [*grad_dots(step - 1, act_t)])
        leave(step - 1).start()

    found = []
    for thunk in front_dots(0, found):
        thunk()
    middle(0, found)

    def aside():
        x_t_ref[...] = jnp.transpose(x_rows, (1, 0)).astype(low)
        tables(plan_ref, pick_ref, gate_ref)

    if steps > 1:
        both(1, (aside,))
    else:
        aside()

    def body(step, carry):
        @pl.when(step > 2)
        def _():
            leave(step - 3).wait()

        both(step)
        return carry

    lax.fori_loop(2, steps, body, 0)
    last = steps - 1
    if steps > 2:
        leave(last - 2).wait()
    for thunk in grad_dots(last, act_t_ref[...]):
        thunk()
    leave(last).start()
    for thunk in back_dots(last, act_ref[last], d_pre_ref[last]):
        thunk()
    sums = jnp.concatenate([out_acc[...], back_acc[...]], axis=0).astype(low)
    ret = jnp.dot(row_order(rows, 1), sums, preferred_element_type=jnp.float32)
    ret_ref[...] = ret.astype(low)
    if steps > 1:
        leave(last - 1).wait()
    leave(last).wait()


def product(out_ref, left, right, tall, wide):
    rows, cols = out_ref.shape
    for col in range(0, cols, wide):
        col_end = min(col + wide, cols)
        for row in range(0, rows, tall):
            row_end = min(row + tall, rows)
            out_ref[row:row_end, col:col_end] = jnp.dot(
                left[row:row_end], right[:, col:col_end], preferred_element_type=jnp.float32
            ).astype(jnp.bfloat16)


def grads_kernel(
    x_t_ref, g_ref, act_ref, d_pre_ref, _, d_in_hbm, d_out_hbm, d_in_stage, d_out_stage, sem
):
    steps, _, depth = act_ref.shape
    width = x_t_ref.shape[0]
    slots = d_in_stage.shape[0]
    later = depth - EARLY

    def leave(step):
        slot = lax.rem(step, slots)
        cols = pl.ds(pl.multiple_of(step * depth, depth), depth)
        pairs = []
        for index in range(2):
            some = pl.ds(index * (width // 2), width // 2)
            pairs.append((d_in_stage.at[slot, some], d_in_hbm.at[some, cols]))
        for index in range(2):
            first = index * (later // 2)
            here = pl.ds(first, later // 2)
            there = pl.ds(pl.multiple_of(step * depth + EARLY + first, 32), later // 2)
            pairs.append((d_out_stage.at[slot, here], d_out_hbm.at[there]))
        return [
            pltpu.make_async_copy(*pair, sem.at[slot, index]) for index, pair in enumerate(pairs)
        ]

    def work(step, carry):
        @pl.when(step >= slots)
        def _():
            for copy in leave(step - slots):
                copy.wait()

        slot = lax.rem(step, slots)
        copies = leave(step)
        act_t = jnp.transpose(act_ref[step].astype(jnp.float32), (1, 0)).astype(jnp.bfloat16)
        product(d_in_stage.at[slot], x_t_ref[...], d_pre_ref[step], 208, 256)
        for copy in copies[:2]:
            copy.start()
        product(d_out_stage.at[slot], act_t[EARLY:], g_ref[...], 192, 256)
        for copy in copies[2:]:
            copy.start()
        return carry

    lax.fori_loop(0, steps, work, 0)
    for step in range(max(steps - slots, 0), steps):
        for copy in leave(step):
            copy.wait()


def combine_kernel(ret_ref, pick_ref, gate_ref, cot_ref, mixed_ref, d_tok_ref, d_gate_ref):
    count = cot_ref.shape[0]
    rows = pick_ref.shape[1]
    found = None
    for first in range(0, ret_ref.shape[0], rows):
        part = jnp.dot(
            pick_ref[...], ret_ref[first:first + rows, :], preferred_element_type=jnp.float32
        )
        found = part if found is None else found + part
    o_0, o_1 = found[:count], found[count:2 * count]
    mixed_ref[...] = (gate_ref[:, 2:3] * o_0 + gate_ref[:, 3:4] * o_1).astype(jnp.bfloat16)
    d_tok_ref[...] = found[2 * count:].astype(jnp.bfloat16)
    cot = cot_ref[...].astype(jnp.float32)
    d_0 = jnp.sum(cot * o_0, axis=1, keepdims=True)
    d_1 = jnp.sum(cot * o_1, axis=1, keepdims=True)
    lane = lax.broadcasted_iota(jnp.int32, (count, 8), 1)
    both = jnp.where(lane == 0, d_0, jnp.where(lane == 1, d_1, 0.0))
    d_gate_ref[...] = jnp.transpose(both, (1, 0))[0:2, :]


def params(mib):
    return pltpu.CompilerParams(vmem_limit_bytes=mib * 1024 * 1024)


def chunk_of(hidden, want):
    return max(size for size in range(128, want + 1, 128) if hidden % size == 0)


def per_device(tokens, expert_ids, priority, gates, w_in, w_out, cotangent):
    count, width = tokens.shape
    repl = lax.axis_size("expert") // EXPERTS
    slots = EXPERTS * PAIR
    hidden = w_in.shape[2]
    ids_t = jnp.transpose(expert_ids, (1, 0))
    gates_t = jnp.transpose(gates, (1, 0))
    low = jnp.bfloat16
    vmem = pl.BlockSpec(memory_space=pltpu.VMEM)
    hbm = pl.BlockSpec(memory_space=pl.ANY)
    chunk = chunk_of(hidden, 256)
    steps = hidden // chunk
    send, plan, w_in_0, w_out_0 = pl.pallas_call(
        dispatch_kernel,
        out_shape=(
            pltpu.VMEM((slots, width), low),
            pltpu.VMEM((8, count), jnp.float32),
            pltpu.VMEM((width, chunk), low),
            pltpu.VMEM((chunk, width), low),
        ),
        in_specs=[hbm] * 7,
        out_specs=(vmem,) * 4,
        scratch_shapes=[
            pltpu.VMEM((2, count), jnp.int32),
            pltpu.VMEM((1, count), jnp.int32),
            pltpu.VMEM((2, count), jnp.float32),
            pltpu.VMEM((2 * count, width), low),
            pltpu.SemaphoreType.DMA((7,)),
        ],
        compiler_params=params(50),
        name="dispatch",
    )(*(pltpu.with_memory_space_constraint(array, pltpu.HBM) for array in (
        ids_t, priority, gates_t, tokens, cotangent, w_in[0], w_out[0]
    )))
    send = jnp.tile(send.reshape(EXPERTS, PAIR, width), (repl, 1, 1))
    recv = lax.all_to_all(send, "expert", split_axis=0, concat_axis=0, tiled=True)
    rows = recv.shape[0] * PAIR
    recv = recv.reshape(rows, width)
    half = rows // 2
    ret, x_t, g_rows, act, d_pre, pick, gate_cols, d_w_out = pl.pallas_call(
        functools.partial(forward_kernel, steps),
        out_shape=(
            pltpu.VMEM((rows, width), low),
            jax.ShapeDtypeStruct((width, half), low),
            jax.ShapeDtypeStruct((half, width), low),
            jax.ShapeDtypeStruct((steps, half, chunk), low),
            jax.ShapeDtypeStruct((steps, half, chunk), low),
            jax.ShapeDtypeStruct((3 * count, slots), low),
            jax.ShapeDtypeStruct((count, 8), jnp.float32),
            jax.ShapeDtypeStruct((hidden, width), low),
        ),
        in_specs=[vmem] * 4 + [hbm] * 2,
        out_specs=(vmem,) * 7 + (hbm,),
        scratch_shapes=[
            pltpu.VMEM((max(steps - 1, 1), width, chunk), low),
            pltpu.VMEM((max(steps - 1, 1), chunk, width), low),
            pltpu.VMEM((half, width), low),
            pltpu.VMEM((EARLY, half), low),
            pltpu.VMEM((2, EARLY, width), low),
            pltpu.VMEM((half, width), jnp.float32),
            pltpu.VMEM((half, width), jnp.float32),
            pltpu.SemaphoreType.DMA((max(steps - 1, 1),)),
            pltpu.SemaphoreType.DMA((max(steps - 1, 1),)),
            pltpu.SemaphoreType.DMA((2,)),
        ],
        compiler_params=params(43),
        cost_estimate=pl.CostEstimate(
            flops=8 * half * width * hidden,
            bytes_accessed=4 * width * hidden,
            transcendentals=half * hidden,
        ),
        name="forward",
    )(recv, plan, w_in_0, w_out_0, w_in[0], w_out[0])
    ret = lax.all_to_all(
        ret.reshape(rows // PAIR, PAIR, width), "expert", split_axis=0, concat_axis=0, tiled=True
    ).reshape(rows, width)
    d_w_in, d_w_out = pl.pallas_call(
        grads_kernel,
        out_shape=(
            jax.ShapeDtypeStruct((width, hidden), low),
            jax.ShapeDtypeStruct((hidden, width), low),
        ),
        in_specs=[vmem] * 4 + [hbm],
        out_specs=(hbm,) * 2,
        input_output_aliases={4: 1},
        scratch_shapes=[
            pltpu.VMEM((3, width, chunk), low),
            pltpu.VMEM((3, chunk - EARLY, width), low),
            pltpu.SemaphoreType.DMA((3, 4)),
        ],
        compiler_params=params(24),
        cost_estimate=pl.CostEstimate(
            flops=4 * half * width * hidden,
            bytes_accessed=4 * width * hidden,
            transcendentals=0,
        ),
        name="grads",
    )(x_t, g_rows, act, d_pre, d_w_out)
    mixed, d_tokens, d_gates_t = pl.pallas_call(
        combine_kernel,
        out_shape=(
            jax.ShapeDtypeStruct((count, width), low),
            jax.ShapeDtypeStruct((count, width), low),
            jax.ShapeDtypeStruct((2, count), jnp.float32),
        ),
        compiler_params=params(12),
        name="combine",
    )(ret, pick, gate_cols, cotangent)
    return (mixed, d_tokens, jnp.transpose(d_gates_t, (1, 0)), d_w_in[None], d_w_out[None])


def solution(mesh):
    rows = P(("groups", "expert"), None)
    return jax.shard_map(
        per_device,
        mesh=mesh,
        in_specs=(rows, rows, rows, rows, P("expert", None, None), P("expert", None, None), rows),
        out_specs=(
            rows,
            rows,
            rows,
            P(("groups", "expert"), None, None),
            P(("groups", "expert"), None, None),
        ),
        check_vma=False,
    )
```

```python
import functools
import math

import jax
import jax.numpy as jnp
from jax import lax
from jax.experimental import pallas as pl
from jax.experimental.pallas import tpu as pltpu
from jax.sharding import PartitionSpec as P

EXPERTS = 16
CAP = 4
PAIR = 2 * CAP
EARLY = 256
LAST_DIM = (((1,), (1,)), ((), ()))


def gelu_parts(value):
    coef = math.sqrt(2.0 / math.pi)
    square = value * value
    hyper = jnp.tanh(coef * value * (1.0 + 0.044715 * square))
    half = 0.5 * (1.0 + hyper)
    slope = half + 0.5 * value * (1.0 - hyper * hyper) * coef * (1.0 + 3.0 * 0.044715 * square)
    return (value * half, slope)


def place_rows(ids_t, prio):
    count = ids_t.shape[1]
    first = ids_t[0:1, :]
    second = ids_t[1:2, :]
    stack = jnp.concatenate([first, second, prio, jnp.zeros((5, count), jnp.int32)], axis=0)
    columns = jnp.transpose(stack.astype(jnp.float32), (1, 0)).astype(jnp.int32)
    first_c, second_c, prio_c = columns[:, 0:1], columns[:, 1:2], columns[:, 2:3]
    ahead = prio_c < prio
    one = jnp.float32(1.0)
    zero = jnp.float32(0.0)
    slot_0 = jnp.sum(jnp.where((first_c == first) & ahead, one, zero), axis=0, keepdims=True)
    slot_1 = jnp.sum(
        jnp.where((first_c == second) | ((second_c == second) & ahead), one, zero),
        axis=0,
        keepdims=True,
    )
    slot_0 = slot_0.astype(jnp.int32)
    slot_1 = slot_1.astype(jnp.int32)
    place_0 = jnp.where(slot_0 < CAP, first * CAP + slot_0, -1)
    place_1 = jnp.where(slot_1 < CAP, second * CAP + slot_1, -1)
    return place_0, place_1


def row_slots(count):
    row = lax.broadcasted_iota(jnp.int32, (EXPERTS * PAIR, count), 0)
    return ((row >> 3) << 2) | (row & (CAP - 1)), (row & CAP) == 0


def dispatch_kernel(
    ids_hbm, prio_hbm, gates_hbm, tok_hbm, cot_hbm, w_in_hbm, w_out_hbm,
    send_ref, plan_ref, w_in_ref, w_out_ref,
    ids_ref, prio_ref, gates_ref, both_ref, sem,
):
    count = tok_hbm.shape[0]
    lead = w_in_ref.shape[1]
    pairs = (
        (ids_hbm, ids_ref),
        (prio_hbm, prio_ref),
        (gates_hbm, gates_ref),
        (tok_hbm, both_ref.at[0:count]),
        (cot_hbm, both_ref.at[count:2 * count]),
        (w_in_hbm.at[:, 0:lead], w_in_ref),
        (w_out_hbm.at[0:lead, :], w_out_ref),
    )
    copies = [pltpu.make_async_copy(*pair, sem.at[index]) for index, pair in enumerate(pairs)]
    for copy in copies:
        copy.start()
    for copy in copies[:3]:
        copy.wait()
    place_0, place_1 = place_rows(ids_ref[...], prio_ref[...])
    slot, is_x = row_slots(count)
    hit_0 = slot == place_0
    hit_1 = slot == place_1
    hit = jnp.where(hit_0 | hit_1, 1.0, 0.0)
    pick = jnp.concatenate(
        [jnp.where(is_x, hit, 0.0), jnp.where(is_x, 0.0, hit)], axis=1
    ).astype(jnp.bfloat16)
    gate = jnp.where(hit_0, gates_ref[0:1, :], 0.0) + jnp.where(hit_1, gates_ref[1:2, :], 0.0)
    scale = jnp.sum(gate, axis=1, keepdims=True)
    scale = jnp.where(is_x[:, 0:1], 1.0, scale)
    plan_ref[...] = jnp.concatenate(
        [
            place_0.astype(jnp.float32),
            place_1.astype(jnp.float32),
            gates_ref[...],
            jnp.zeros((4, count), jnp.float32),
        ],
        axis=0,
    )
    for copy in copies[3:5]:
        copy.wait()
    found = jnp.dot(pick, both_ref[...], preferred_element_type=jnp.float32)
    send_ref[...] = (found * scale).astype(jnp.bfloat16)
    for copy in copies[5:]:
        copy.wait()


def tables(plan_ref, pick_ref, gate_ref):
    place_0 = plan_ref[0:1, :].astype(jnp.int32)
    place_1 = plan_ref[1:2, :].astype(jnp.int32)
    count = place_0.shape[1]
    slot, is_x = row_slots(count)
    hit_0 = jnp.where(slot == place_0, 1.0, 0.0)
    hit_1 = jnp.where(slot == place_1, 1.0, 0.0)
    pick_0 = jnp.transpose(jnp.where(is_x, hit_0, 0.0), (1, 0))
    pick_1 = jnp.transpose(jnp.where(is_x, hit_1, 0.0), (1, 0))
    pick_b = jnp.transpose(jnp.where(is_x, 0.0, hit_0 + hit_1), (1, 0))
    pick_ref[...] = jnp.concatenate([pick_0, pick_1, pick_b], axis=0).astype(jnp.bfloat16)
    gate_ref[...] = jnp.transpose(plan_ref[...], (1, 0))


def row_order(rows, dim):
    half = rows // 2
    out = lax.broadcasted_iota(jnp.int32, (rows, rows), dim)
    col = lax.broadcasted_iota(jnp.int32, (rows, rows), 1 - dim)
    place = jnp.where(out < half, out, out - half)
    source = ((place >> 2) << 3) | (place & (CAP - 1)) | jnp.where(out < half, 0, CAP)
    return jnp.where(col == source, 1.0, 0.0).astype(jnp.bfloat16)


def forward_kernel(
    steps, recv_ref, plan_ref, w_in_0, w_out_0, w_in_hbm, w_out_hbm,
    ret_ref, x_t_ref, g_ref, act_ref, d_pre_ref, pick_ref, gate_ref, d_out_hbm,
    w_in_ref, w_out_ref, x_ref, act_t_ref, stage, out_acc, back_acc, sem_in, sem_out, sem_left,
):
    width, lead = w_in_0.shape
    depth = w_in_ref.shape[2]
    low = jnp.bfloat16

    def copies(step):
        if isinstance(step, int) and step == 0:
            cols = near = pl.ds(lead, depth - lead)
        else:
            cols = pl.ds(pl.multiple_of(step * depth, depth), depth)
            near = pl.ds(0, depth)
        return (
            pltpu.make_async_copy(
                w_in_hbm.at[:, cols], w_in_ref.at[step, :, near], sem_in.at[step]
            ),
            pltpu.make_async_copy(
                w_out_hbm.at[cols, :], w_out_ref.at[step, near, :], sem_out.at[step]
            ),
        )

    def leave(step):
        rows = pl.ds(pl.multiple_of(step * depth, depth), EARLY)
        slot = lax.rem(step, 2)
        return pltpu.make_async_copy(stage.at[slot], d_out_hbm.at[rows, :], sem_left.at[slot])

    def begin(step, carry):
        for copy in copies(step):
            copy.start()
        return carry

    begin(0, 0)
    lax.fori_loop(1, steps, begin, 0)
    rows = recv_ref.shape[0]
    half = rows // 2
    found = jnp.dot(row_order(rows, 0), recv_ref[...], preferred_element_type=jnp.float32)
    x_rows = found[:half]
    x_ref[...] = x_rows.astype(low)
    g_ref[...] = found[half:].astype(low)
    out_acc[...] = jnp.zeros_like(out_acc)
    back_acc[...] = jnp.zeros_like(back_acc)

    def spans(step):
        if isinstance(step, int) and step == 0:
            return [slice(0, lead), slice(lead, depth)]
        return [slice(0, depth)]

    def w_first(step, rows, cols):
        if isinstance(step, int) and step == 0 and cols.stop <= lead:
            return w_in_0[rows, cols]
        return w_in_ref[step, rows, cols]

    def w_second(step, rows, cols):
        if isinstance(step, int) and step == 0 and rows.stop <= lead:
            return w_out_0[rows, cols]
        return w_out_ref[step, rows, cols]

    every = slice(0, width)

    def front_dots(step, found, span):
        for first in range(span.start, span.stop, 256):
            cols = slice(first, min(first + 256, span.stop))
            pre = []

            def one(cols=cols, pre=pre):
                pre.append(
                    jnp.dot(
                        x_ref[...], w_first(step, every, cols), preferred_element_type=jnp.float32
                    )
                )

            def two(cols=cols, pre=pre):
                d_act = lax.dot_general(
                    g_ref[...],
                    w_second(step, cols, every),
                    LAST_DIM,
                    preferred_element_type=jnp.float32,
                )
                found.append((cols, pre[0], d_act))

            yield one
            yield two

    def back_dots(step, act, d_pre):
        for first in range(0, width, 256):
            cols = slice(first, min(first + 256, width))

            def one(cols=cols):
                for span in spans(step):
                    out_acc[:, cols] += jnp.dot(
                        act[:, span], w_second(step, span, cols), preferred_element_type=jnp.float32
                    )

            def two(cols=cols):
                for span in spans(step):
                    back_acc[:, cols] += lax.dot_general(
                        d_pre[:, span],
                        w_first(step, cols, span),
                        LAST_DIM,
                        preferred_element_type=jnp.float32,
                    )

            yield one
            yield two

    def grad_dots(step, act_t):
        slot = lax.rem(step, 2)
        for first in range(0, width, 256):
            cols = slice(first, min(first + 256, width))
            for top in range(0, EARLY, 128):
                some = slice(top, top + 128)

                def one(cols=cols, some=some):
                    stage[slot, some, cols] = jnp.dot(
                        act_t[some], g_ref[:, cols], preferred_element_type=jnp.float32
                    ).astype(low)

                yield one

    def middle(step, found):
        for cols, pre, d_act in found:
            value, slope = gelu_parts(pre)
            act_ref[step, :, cols] = value.astype(low)
            d_pre_ref[step, :, cols] = (d_act * slope).astype(low)
            if cols.start == 0:
                act_t_ref[...] = jnp.transpose(value[:, 0:EARLY], (1, 0)).astype(low)

    def run(first, second):
        done = 0
        for index, thunk in enumerate(first):
            thunk()
            due = (index + 1) * len(second) // len(first)
            for other in second[done:due]:
                other()
            done = due

    def both(step, extra=()):
        for copy in copies(step):
            copy.wait()
        act, act_t, d_pre = act_ref[step - 1], act_t_ref[...], d_pre_ref[step - 1]
        found = []
        fronts = [*front_dots(step, found, slice(0, depth))]
        backs = [*back_dots(step - 1, act, d_pre)]
        blocks = len(fronts) // 2
        share = len(backs) // (blocks + 1)
        turns = []
        for block in range(blocks):
            turns += fronts[2 * block:2 * block + 2]
            turns += backs[share * block:share * (block + 1)]
            turns.append(lambda block=block: middle(step, found[block:block + 1]))
        turns += [*extra, *backs[share * blocks:]]
        run(turns, [*grad_dots(step - 1, act_t)])
        leave(step - 1).start()

    for part, span in enumerate(spans(0)):
        if part:
            for copy in copies(0):
                copy.wait()
        found = []
        for thunk in front_dots(0, found, span):
            thunk()
        middle(0, found)

    def aside():
        x_t_ref[...] = jnp.transpose(x_rows, (1, 0)).astype(low)
        tables(plan_ref, pick_ref, gate_ref)

    if steps > 1:
        both(1, (aside,))
    else:
        aside()

    def body(step, carry):
        @pl.when(step > 2)
        def _():
            leave(step - 3).wait()

        both(step)
        return carry

    lax.fori_loop(2, steps, body, 0)
    last = steps - 1
    if steps > 2:
        leave(last - 2).wait()
    for thunk in grad_dots(last, act_t_ref[...]):
        thunk()
    leave(last).start()
    for thunk in back_dots(last, act_ref[last], d_pre_ref[last]):
        thunk()
    sums = jnp.concatenate([out_acc[...], back_acc[...]], axis=0).astype(low)
    ret = jnp.dot(row_order(rows, 1), sums, preferred_element_type=jnp.float32)
    ret_ref[...] = ret.astype(low)
    if steps > 1:
        leave(last - 1).wait()
    leave(last).wait()


def product(out_ref, left, right, tall, wide):
    rows, cols = out_ref.shape
    for col in range(0, cols, wide):
        col_end = min(col + wide, cols)
        for row in range(0, rows, tall):
            row_end = min(row + tall, rows)
            out_ref[row:row_end, col:col_end] = jnp.dot(
                left[row:row_end], right[:, col:col_end], preferred_element_type=jnp.float32
            ).astype(jnp.bfloat16)


def grads_kernel(
    x_t_ref, g_ref, act_ref, d_pre_ref, _, d_in_hbm, d_out_hbm, d_in_stage, d_out_stage, sem
):
    steps, _, depth = act_ref.shape
    width = x_t_ref.shape[0]
    slots = d_in_stage.shape[0]
    later = depth - EARLY

    def leave(step):
        slot = lax.rem(step, slots)
        cols = pl.ds(pl.multiple_of(step * depth, depth), depth)
        pairs = []
        for index in range(2):
            some = pl.ds(index * (width // 2), width // 2)
            pairs.append((d_in_stage.at[slot, some], d_in_hbm.at[some, cols]))
        for index in range(2):
            first = index * (later // 2)
            here = pl.ds(first, later // 2)
            there = pl.ds(pl.multiple_of(step * depth + EARLY + first, 64), later // 2)
            pairs.append((d_out_stage.at[slot, here], d_out_hbm.at[there]))
        return [
            pltpu.make_async_copy(*pair, sem.at[slot, index]) for index, pair in enumerate(pairs)
        ]

    def work(step, carry):
        @pl.when(step >= slots)
        def _():
            for copy in leave(step - slots):
                copy.wait()

        slot = lax.rem(step, slots)
        copies = leave(step)
        act_t = jnp.transpose(act_ref[step].astype(jnp.float32), (1, 0)).astype(jnp.bfloat16)
        product(d_in_stage.at[slot], x_t_ref[...], d_pre_ref[step], 208, 256)
        for copy in copies[:2]:
            copy.start()
        product(d_out_stage.at[slot], act_t[EARLY:], g_ref[...], 192, 256)
        for copy in copies[2:]:
            copy.start()
        return carry

    lax.fori_loop(0, steps, work, 0)
    for step in range(max(steps - slots, 0), steps):
        for copy in leave(step):
            copy.wait()


def combine_kernel(ret_ref, pick_ref, gate_ref, cot_ref, mixed_ref, d_tok_ref, d_gate_ref):
    count = cot_ref.shape[0]
    rows = pick_ref.shape[1]
    found = None
    for first in range(0, ret_ref.shape[0], rows):
        part = jnp.dot(
            pick_ref[...], ret_ref[first:first + rows, :], preferred_element_type=jnp.float32
        )
        found = part if found is None else found + part
    o_0, o_1 = found[:count], found[count:2 * count]
    mixed_ref[...] = (gate_ref[:, 2:3] * o_0 + gate_ref[:, 3:4] * o_1).astype(jnp.bfloat16)
    d_tok_ref[...] = found[2 * count:].astype(jnp.bfloat16)
    cot = cot_ref[...].astype(jnp.float32)
    d_0 = jnp.sum(cot * o_0, axis=1, keepdims=True)
    d_1 = jnp.sum(cot * o_1, axis=1, keepdims=True)
    lane = lax.broadcasted_iota(jnp.int32, (count, 8), 1)
    both = jnp.where(lane == 0, d_0, jnp.where(lane == 1, d_1, 0.0))
    d_gate_ref[...] = jnp.transpose(both, (1, 0))[0:2, :]


def params(mib):
    return pltpu.CompilerParams(vmem_limit_bytes=mib * 1024 * 1024)


def chunk_of(hidden, want):
    return max(size for size in range(128, want + 1, 128) if hidden % size == 0)


def per_device(tokens, expert_ids, priority, gates, w_in, w_out, cotangent):
    count, width = tokens.shape
    repl = lax.axis_size("expert") // EXPERTS
    slots = EXPERTS * PAIR
    hidden = w_in.shape[2]
    ids_t = jnp.transpose(expert_ids, (1, 0))
    gates_t = jnp.transpose(gates, (1, 0))
    low = jnp.bfloat16
    vmem = pl.BlockSpec(memory_space=pltpu.VMEM)
    hbm = pl.BlockSpec(memory_space=pl.ANY)
    chunk = chunk_of(hidden, 1024)
    steps = hidden // chunk
    send, plan, w_in_0, w_out_0 = pl.pallas_call(
        dispatch_kernel,
        out_shape=(
            pltpu.VMEM((slots, width), low),
            pltpu.VMEM((8, count), jnp.float32),
            pltpu.VMEM((width, chunk // 2), low),
            pltpu.VMEM((chunk // 2, width), low),
        ),
        in_specs=[hbm] * 7,
        out_specs=(vmem,) * 4,
        scratch_shapes=[
            pltpu.VMEM((2, count), jnp.int32),
            pltpu.VMEM((1, count), jnp.int32),
            pltpu.VMEM((2, count), jnp.float32),
            pltpu.VMEM((2 * count, width), low),
            pltpu.SemaphoreType.DMA((7,)),
        ],
        compiler_params=params(50),
        name="dispatch",
    )(*(pltpu.with_memory_space_constraint(array, pltpu.HBM) for array in (
        ids_t, priority, gates_t, tokens, cotangent, w_in[0], w_out[0]
    )))
    send = jnp.tile(send.reshape(EXPERTS, PAIR, width), (repl, 1, 1))
    recv = lax.all_to_all(send, "expert", split_axis=0, concat_axis=0, tiled=True)
    rows = recv.shape[0] * PAIR
    recv = recv.reshape(rows, width)
    half = rows // 2
    ret, x_t, g_rows, act, d_pre, pick, gate_cols, d_w_out = pl.pallas_call(
        functools.partial(forward_kernel, steps),
        out_shape=(
            pltpu.VMEM((rows, width), low),
            jax.ShapeDtypeStruct((width, half), low),
            jax.ShapeDtypeStruct((half, width), low),
            jax.ShapeDtypeStruct((steps, half, chunk), low),
            jax.ShapeDtypeStruct((steps, half, chunk), low),
            jax.ShapeDtypeStruct((3 * count, slots), low),
            jax.ShapeDtypeStruct((count, 8), jnp.float32),
            jax.ShapeDtypeStruct((hidden, width), low),
        ),
        in_specs=[vmem] * 4 + [hbm] * 2,
        out_specs=(vmem,) * 7 + (hbm,),
        scratch_shapes=[
            pltpu.VMEM((steps, width, chunk), low),
            pltpu.VMEM((steps, chunk, width), low),
            pltpu.VMEM((half, width), low),
            pltpu.VMEM((EARLY, half), low),
            pltpu.VMEM((2, EARLY, width), low),
            pltpu.VMEM((half, width), jnp.float32),
            pltpu.VMEM((half, width), jnp.float32),
            pltpu.SemaphoreType.DMA((steps,)),
            pltpu.SemaphoreType.DMA((steps,)),
            pltpu.SemaphoreType.DMA((2,)),
        ],
        compiler_params=params(45),
        cost_estimate=pl.CostEstimate(
            flops=8 * half * width * hidden,
            bytes_accessed=4 * width * hidden,
            transcendentals=half * hidden,
        ),
        name="forward",
    )(recv, plan, w_in_0, w_out_0, w_in[0], w_out[0])
    ret = lax.all_to_all(
        ret.reshape(rows // PAIR, PAIR, width), "expert", split_axis=0, concat_axis=0, tiled=True
    ).reshape(rows, width)
    d_w_in, d_w_out = pl.pallas_call(
        grads_kernel,
        out_shape=(
            jax.ShapeDtypeStruct((width, hidden), low),
            jax.ShapeDtypeStruct((hidden, width), low),
        ),
        in_specs=[vmem] * 4 + [hbm],
        out_specs=(hbm,) * 2,
        input_output_aliases={4: 1},
        scratch_shapes=[
            pltpu.VMEM((3, width, chunk), low),
            pltpu.VMEM((3, chunk - EARLY, width), low),
            pltpu.SemaphoreType.DMA((3, 4)),
        ],
        compiler_params=params(28),
        cost_estimate=pl.CostEstimate(
            flops=4 * half * width * hidden,
            bytes_accessed=4 * width * hidden,
            transcendentals=0,
        ),
        name="grads",
    )(x_t, g_rows, act, d_pre, d_w_out)
    mixed, d_tokens, d_gates_t = pl.pallas_call(
        combine_kernel,
        out_shape=(
            jax.ShapeDtypeStruct((count, width), low),
            jax.ShapeDtypeStruct((count, width), low),
            jax.ShapeDtypeStruct((2, count), jnp.float32),
        ),
        compiler_params=params(12),
        name="combine",
    )(ret, pick, gate_cols, cotangent)
    return (mixed, d_tokens, jnp.transpose(d_gates_t, (1, 0)), d_w_in[None], d_w_out[None])


def solution(mesh):
    rows = P(("groups", "expert"), None)
    return jax.shard_map(
        per_device,
        mesh=mesh,
        in_specs=(rows, rows, rows, rows, P("expert", None, None), P("expert", None, None), rows),
        out_specs=(
            rows,
            rows,
            rows,
            P(("groups", "expert"), None, None),
            P(("groups", "expert"), None, None),
        ),
        check_vma=False,
    )
```

```python
import functools
import math

import jax
import jax.numpy as jnp
from jax import lax
from jax.experimental import pallas as pl
from jax.experimental.pallas import tpu as pltpu
from jax.sharding import PartitionSpec as P

EXPERTS = 16
CAP = 4
PAIR = 2 * CAP
EARLY = 256
LAST_DIM = (((1,), (1,)), ((), ()))


def gelu_parts(value):
    coef = math.sqrt(2.0 / math.pi)
    square = value * value
    hyper = jnp.tanh(coef * value * (1.0 + 0.044715 * square))
    half = 0.5 * (1.0 + hyper)
    slope = half + 0.5 * value * (1.0 - hyper * hyper) * coef * (1.0 + 3.0 * 0.044715 * square)
    return (value * half, slope)


def place_rows(ids_t, prio):
    count = ids_t.shape[1]
    first = ids_t[0:1, :]
    second = ids_t[1:2, :]
    stack = jnp.concatenate([first, second, prio, jnp.zeros((5, count), jnp.int32)], axis=0)
    columns = jnp.transpose(stack.astype(jnp.float32), (1, 0)).astype(jnp.int32)
    first_c, second_c, prio_c = columns[:, 0:1], columns[:, 1:2], columns[:, 2:3]
    ahead = prio_c < prio
    one = jnp.float32(1.0)
    zero = jnp.float32(0.0)
    slot_0 = jnp.sum(jnp.where((first_c == first) & ahead, one, zero), axis=0, keepdims=True)
    slot_1 = jnp.sum(
        jnp.where((first_c == second) | ((second_c == second) & ahead), one, zero),
        axis=0,
        keepdims=True,
    )
    slot_0 = slot_0.astype(jnp.int32)
    slot_1 = slot_1.astype(jnp.int32)
    place_0 = jnp.where(slot_0 < CAP, first * CAP + slot_0, -1)
    place_1 = jnp.where(slot_1 < CAP, second * CAP + slot_1, -1)
    return place_0, place_1


def row_slots(count):
    row = lax.broadcasted_iota(jnp.int32, (EXPERTS * PAIR, count), 0)
    return ((row >> 3) << 2) | (row & (CAP - 1)), (row & CAP) == 0


def dispatch_kernel(
    ids_hbm, prio_hbm, gates_hbm, tok_hbm, cot_hbm, w_in_hbm, w_out_hbm,
    send_ref, plan_ref, w_in_ref, w_out_ref,
    ids_ref, prio_ref, gates_ref, both_ref, sem,
):
    count = tok_hbm.shape[0]
    lead = w_in_ref.shape[1]
    pairs = (
        (ids_hbm, ids_ref),
        (prio_hbm, prio_ref),
        (gates_hbm, gates_ref),
        (tok_hbm, both_ref.at[0:count]),
        (cot_hbm, both_ref.at[count:2 * count]),
        (w_in_hbm.at[:, 0:lead], w_in_ref),
        (w_out_hbm.at[0:lead, :], w_out_ref),
    )
    copies = [pltpu.make_async_copy(*pair, sem.at[index]) for index, pair in enumerate(pairs)]
    for copy in copies:
        copy.start()
    for copy in copies[:3]:
        copy.wait()
    place_0, place_1 = place_rows(ids_ref[...], prio_ref[...])
    slot, is_x = row_slots(count)
    hit_0 = slot == place_0
    hit_1 = slot == place_1
    hit = jnp.where(hit_0 | hit_1, 1.0, 0.0)
    pick = jnp.concatenate(
        [jnp.where(is_x, hit, 0.0), jnp.where(is_x, 0.0, hit)], axis=1
    ).astype(jnp.bfloat16)
    gate = jnp.where(hit_0, gates_ref[0:1, :], 0.0) + jnp.where(hit_1, gates_ref[1:2, :], 0.0)
    scale = jnp.sum(gate, axis=1, keepdims=True)
    scale = jnp.where(is_x[:, 0:1], 1.0, scale)
    plan_ref[...] = jnp.concatenate(
        [
            place_0.astype(jnp.float32),
            place_1.astype(jnp.float32),
            gates_ref[...],
            jnp.zeros((4, count), jnp.float32),
        ],
        axis=0,
    )
    for copy in copies[3:5]:
        copy.wait()
    found = jnp.dot(pick, both_ref[...], preferred_element_type=jnp.float32)
    send_ref[...] = (found * scale).astype(jnp.bfloat16)
    for copy in copies[5:]:
        copy.wait()


def tables(plan_ref, pick_ref, gate_ref):
    place_0 = plan_ref[0:1, :].astype(jnp.int32)
    place_1 = plan_ref[1:2, :].astype(jnp.int32)
    count = place_0.shape[1]
    slot, is_x = row_slots(count)
    hit_0 = jnp.where(slot == place_0, 1.0, 0.0)
    hit_1 = jnp.where(slot == place_1, 1.0, 0.0)
    pick_0 = jnp.transpose(jnp.where(is_x, hit_0, 0.0), (1, 0))
    pick_1 = jnp.transpose(jnp.where(is_x, hit_1, 0.0), (1, 0))
    pick_b = jnp.transpose(jnp.where(is_x, 0.0, hit_0 + hit_1), (1, 0))
    pick_ref[...] = jnp.concatenate([pick_0, pick_1, pick_b], axis=0).astype(jnp.bfloat16)
    gate_ref[...] = jnp.transpose(plan_ref[...], (1, 0))


def row_order(rows, dim):
    half = rows // 2
    out = lax.broadcasted_iota(jnp.int32, (rows, rows), dim)
    col = lax.broadcasted_iota(jnp.int32, (rows, rows), 1 - dim)
    place = jnp.where(out < half, out, out - half)
    source = ((place >> 2) << 3) | (place & (CAP - 1)) | jnp.where(out < half, 0, CAP)
    return jnp.where(col == source, 1.0, 0.0).astype(jnp.bfloat16)


def forward_kernel(
    steps, recv_ref, plan_ref, w_in_0, w_out_0, w_in_hbm, w_out_hbm,
    ret_ref, x_t_ref, g_ref, act_ref, d_pre_ref, pick_ref, gate_ref, d_out_hbm,
    w_in_ref, w_out_ref, x_ref, act_t_ref, stage, out_acc, back_acc, sem_in, sem_out, sem_left,
):
    width, lead = w_in_0.shape
    depth = w_in_ref.shape[2]
    low = jnp.bfloat16

    def copies(step):
        if isinstance(step, int) and step == 0:
            cols = near = pl.ds(lead, depth - lead)
        else:
            cols = pl.ds(pl.multiple_of(step * depth, depth), depth)
            near = pl.ds(0, depth)
        return (
            pltpu.make_async_copy(
                w_in_hbm.at[:, cols], w_in_ref.at[step, :, near], sem_in.at[step]
            ),
            pltpu.make_async_copy(
                w_out_hbm.at[cols, :], w_out_ref.at[step, near, :], sem_out.at[step]
            ),
        )

    def leave(step):
        rows = pl.ds(pl.multiple_of(step * depth, depth), EARLY)
        slot = lax.rem(step, 2)
        return pltpu.make_async_copy(stage.at[slot], d_out_hbm.at[rows, :], sem_left.at[slot])

    def begin(step, carry):
        for copy in copies(step):
            copy.start()
        return carry

    begin(0, 0)
    lax.fori_loop(1, steps, begin, 0)
    rows = recv_ref.shape[0]
    half = rows // 2
    found = jnp.dot(row_order(rows, 0), recv_ref[...], preferred_element_type=jnp.float32)
    x_rows = found[:half]
    x_ref[...] = x_rows.astype(low)
    g_ref[...] = found[half:].astype(low)
    out_acc[...] = jnp.zeros_like(out_acc)
    back_acc[...] = jnp.zeros_like(back_acc)

    def spans(step):
        if isinstance(step, int) and step == 0:
            return [slice(0, lead), slice(lead, depth)]
        return [slice(0, depth)]

    def w_first(step, rows, cols):
        if isinstance(step, int) and step == 0 and cols.stop <= lead:
            return w_in_0[rows, cols]
        return w_in_ref[step, rows, cols]

    def w_second(step, rows, cols):
        if isinstance(step, int) and step == 0 and rows.stop <= lead:
            return w_out_0[rows, cols]
        return w_out_ref[step, rows, cols]

    every = slice(0, width)

    def front_dots(step, found, span):
        for first in range(span.start, span.stop, 256):
            cols = slice(first, min(first + 256, span.stop))
            pre = []

            def one(cols=cols, pre=pre):
                pre.append(
                    jnp.dot(
                        x_ref[...], w_first(step, every, cols), preferred_element_type=jnp.float32
                    )
                )

            def two(cols=cols, pre=pre):
                d_act = lax.dot_general(
                    g_ref[...],
                    w_second(step, cols, every),
                    LAST_DIM,
                    preferred_element_type=jnp.float32,
                )
                found.append((cols, pre[0], d_act))

            yield one
            yield two

    def back_dots(step, act, d_pre):
        for first in range(0, width, 256):
            cols = slice(first, min(first + 256, width))

            def one(cols=cols):
                for span in spans(step):
                    out_acc[:, cols] += jnp.dot(
                        act[:, span], w_second(step, span, cols), preferred_element_type=jnp.float32
                    )

            def two(cols=cols):
                for span in spans(step):
                    back_acc[:, cols] += lax.dot_general(
                        d_pre[:, span],
                        w_first(step, cols, span),
                        LAST_DIM,
                        preferred_element_type=jnp.float32,
                    )

            yield one
            yield two

    def grad_dots(step, act_t):
        slot = lax.rem(step, 2)
        for first in range(0, width, 256):
            cols = slice(first, min(first + 256, width))
            for top in range(0, EARLY, 128):
                some = slice(top, top + 128)

                def one(cols=cols, some=some):
                    stage[slot, some, cols] = jnp.dot(
                        act_t[some], g_ref[:, cols], preferred_element_type=jnp.float32
                    ).astype(low)

                yield one

    def middle(step, found):
        for cols, pre, d_act in found:
            value, slope = gelu_parts(pre)
            act_ref[step, :, cols] = value.astype(low)
            d_pre_ref[step, :, cols] = (d_act * slope).astype(low)
            if cols.start == 0:
                act_t_ref[...] = jnp.transpose(value[:, 0:EARLY], (1, 0)).astype(low)

    def run(first, second):
        done = 0
        for index, thunk in enumerate(first):
            thunk()
            due = (index + 1) * len(second) // len(first)
            for other in second[done:due]:
                other()
            done = due

    def both(step, extra=()):
        for copy in copies(step):
            copy.wait()
        act, act_t, d_pre = act_ref[step - 1], act_t_ref[...], d_pre_ref[step - 1]
        found = []
        fronts = [*front_dots(step, found, slice(0, depth))]
        backs = [*back_dots(step - 1, act, d_pre)]
        blocks = len(fronts) // 2
        share = len(backs) // (blocks + 1)
        turns = []
        for block in range(blocks):
            turns += fronts[2 * block:2 * block + 2]
            turns += backs[share * block:share * (block + 1)]
            turns.append(lambda block=block: middle(step, found[block:block + 1]))
        turns += [*extra, *backs[share * blocks:]]
        run(turns, [*grad_dots(step - 1, act_t)])
        leave(step - 1).start()

    for part, span in enumerate(spans(0)):
        if part:
            for copy in copies(0):
                copy.wait()
        found = []
        for thunk in front_dots(0, found, span):
            thunk()
        middle(0, found)

    def aside():
        x_t_ref[...] = jnp.transpose(x_rows, (1, 0)).astype(low)
        tables(plan_ref, pick_ref, gate_ref)

    if steps > 1:
        both(1, (aside,))
    else:
        aside()

    def body(step, carry):
        @pl.when(step > 2)
        def _():
            leave(step - 3).wait()

        both(step)
        return carry

    lax.fori_loop(2, steps, body, 0)
    last = steps - 1
    if steps > 2:
        leave(last - 2).wait()
    for thunk in grad_dots(last, act_t_ref[...]):
        thunk()
    leave(last).start()
    for thunk in back_dots(last, act_ref[last], d_pre_ref[last]):
        thunk()
    sums = jnp.concatenate([out_acc[...], back_acc[...]], axis=0).astype(low)
    ret = jnp.dot(row_order(rows, 1), sums, preferred_element_type=jnp.float32)
    ret_ref[...] = ret.astype(low)
    if steps > 1:
        leave(last - 1).wait()
    leave(last).wait()


def product(out_ref, left, right, tall, wide):
    rows, cols = out_ref.shape
    for col in range(0, cols, wide):
        col_end = min(col + wide, cols)
        for row in range(0, rows, tall):
            row_end = min(row + tall, rows)
            out_ref[row:row_end, col:col_end] = jnp.dot(
                left[row:row_end], right[:, col:col_end], preferred_element_type=jnp.float32
            ).astype(jnp.bfloat16)


def grads_kernel(
    x_t_ref, g_ref, act_ref, d_pre_ref, _, d_in_hbm, d_out_hbm, d_in_stage, d_out_stage, sem
):
    steps, _, depth = act_ref.shape
    width = x_t_ref.shape[0]
    slots = d_in_stage.shape[0]
    later = depth - EARLY

    def leave(step):
        slot = lax.rem(step, slots)
        cols = pl.ds(pl.multiple_of(step * depth, depth), depth)
        pairs = []
        for index in range(2):
            some = pl.ds(index * (width // 2), width // 2)
            pairs.append((d_in_stage.at[slot, some], d_in_hbm.at[some, cols]))
        for index in range(2):
            first = index * (later // 2)
            here = pl.ds(first, later // 2)
            there = pl.ds(pl.multiple_of(step * depth + EARLY + first, 64), later // 2)
            pairs.append((d_out_stage.at[slot, here], d_out_hbm.at[there]))
        return [
            pltpu.make_async_copy(*pair, sem.at[slot, index]) for index, pair in enumerate(pairs)
        ]

    def work(step, carry):
        @pl.when(step >= slots)
        def _():
            for copy in leave(step - slots):
                copy.wait()

        slot = lax.rem(step, slots)
        copies = leave(step)
        act_t = jnp.transpose(act_ref[step].astype(jnp.float32), (1, 0)).astype(jnp.bfloat16)
        product(d_in_stage.at[slot], x_t_ref[...], d_pre_ref[step], 208, 256)
        for copy in copies[:2]:
            copy.start()
        product(d_out_stage.at[slot], act_t[EARLY:], g_ref[...], 192, 256)
        for copy in copies[2:]:
            copy.start()
        return carry

    lax.fori_loop(0, steps, work, 0)
    for step in range(max(steps - slots, 0), steps):
        for copy in leave(step):
            copy.wait()


def combine_kernel(
    ret_ref, pick_ref, gate_ref, cot_ref, mixed_hbm, d_tok_hbm, d_gate_ref,
    mixed_ref, d_tok_ref, sem,
):
    count = cot_ref.shape[0]
    rows = pick_ref.shape[1]

    def found(first, last):
        total = None
        for row in range(0, ret_ref.shape[0], rows):
            part = jnp.dot(
                pick_ref[first:last, :],
                ret_ref[row:row + rows, :],
                preferred_element_type=jnp.float32,
            )
            total = part if total is None else total + part
        return total

    d_tok_copy = pltpu.make_async_copy(d_tok_ref, d_tok_hbm, sem.at[0])
    mixed_copy = pltpu.make_async_copy(mixed_ref, mixed_hbm, sem.at[1])
    d_tok_ref[...] = found(2 * count, 3 * count).astype(jnp.bfloat16)
    d_tok_copy.start()
    picked = found(0, 2 * count)
    o_0, o_1 = picked[:count], picked[count:]
    mixed_ref[...] = (gate_ref[:, 2:3] * o_0 + gate_ref[:, 3:4] * o_1).astype(jnp.bfloat16)
    mixed_copy.start()
    cot = cot_ref[...].astype(jnp.float32)
    d_0 = jnp.sum(cot * o_0, axis=1, keepdims=True)
    d_1 = jnp.sum(cot * o_1, axis=1, keepdims=True)
    lane = lax.broadcasted_iota(jnp.int32, (count, 8), 1)
    both = jnp.where(lane == 0, d_0, jnp.where(lane == 1, d_1, 0.0))
    d_gate_ref[...] = jnp.transpose(both, (1, 0))[0:2, :]
    d_tok_copy.wait()
    mixed_copy.wait()


def params(mib):
    return pltpu.CompilerParams(vmem_limit_bytes=mib * 1024 * 1024)


def chunk_of(hidden, want):
    return max(size for size in range(128, want + 1, 128) if hidden % size == 0)


def per_device(tokens, expert_ids, priority, gates, w_in, w_out, cotangent):
    count, width = tokens.shape
    repl = lax.axis_size("expert") // EXPERTS
    slots = EXPERTS * PAIR
    hidden = w_in.shape[2]
    ids_t = jnp.transpose(expert_ids, (1, 0))
    gates_t = jnp.transpose(gates, (1, 0))
    low = jnp.bfloat16
    vmem = pl.BlockSpec(memory_space=pltpu.VMEM)
    hbm = pl.BlockSpec(memory_space=pl.ANY)
    chunk = chunk_of(hidden, 1024)
    steps = hidden // chunk
    send, plan, w_in_0, w_out_0 = pl.pallas_call(
        dispatch_kernel,
        out_shape=(
            pltpu.VMEM((slots, width), low),
            pltpu.VMEM((8, count), jnp.float32),
            pltpu.VMEM((width, chunk // 2), low),
            pltpu.VMEM((chunk // 2, width), low),
        ),
        in_specs=[hbm] * 7,
        out_specs=(vmem,) * 4,
        scratch_shapes=[
            pltpu.VMEM((2, count), jnp.int32),
            pltpu.VMEM((1, count), jnp.int32),
            pltpu.VMEM((2, count), jnp.float32),
            pltpu.VMEM((2 * count, width), low),
            pltpu.SemaphoreType.DMA((7,)),
        ],
        compiler_params=params(50),
        name="dispatch",
    )(*(pltpu.with_memory_space_constraint(array, pltpu.HBM) for array in (
        ids_t, priority, gates_t, tokens, cotangent, w_in[0], w_out[0]
    )))
    send = jnp.tile(send.reshape(EXPERTS, PAIR, width), (repl, 1, 1))
    recv = lax.all_to_all(send, "expert", split_axis=0, concat_axis=0, tiled=True)
    rows = recv.shape[0] * PAIR
    recv = recv.reshape(rows, width)
    half = rows // 2
    ret, x_t, g_rows, act, d_pre, pick, gate_cols, d_w_out = pl.pallas_call(
        functools.partial(forward_kernel, steps),
        out_shape=(
            pltpu.VMEM((rows, width), low),
            jax.ShapeDtypeStruct((width, half), low),
            jax.ShapeDtypeStruct((half, width), low),
            jax.ShapeDtypeStruct((steps, half, chunk), low),
            jax.ShapeDtypeStruct((steps, half, chunk), low),
            jax.ShapeDtypeStruct((3 * count, slots), low),
            jax.ShapeDtypeStruct((count, 8), jnp.float32),
            jax.ShapeDtypeStruct((hidden, width), low),
        ),
        in_specs=[vmem] * 4 + [hbm] * 2,
        out_specs=(vmem,) * 7 + (hbm,),
        scratch_shapes=[
            pltpu.VMEM((steps, width, chunk), low),
            pltpu.VMEM((steps, chunk, width), low),
            pltpu.VMEM((half, width), low),
            pltpu.VMEM((EARLY, half), low),
            pltpu.VMEM((2, EARLY, width), low),
            pltpu.VMEM((half, width), jnp.float32),
            pltpu.VMEM((half, width), jnp.float32),
            pltpu.SemaphoreType.DMA((steps,)),
            pltpu.SemaphoreType.DMA((steps,)),
            pltpu.SemaphoreType.DMA((2,)),
        ],
        compiler_params=params(45),
        cost_estimate=pl.CostEstimate(
            flops=8 * half * width * hidden,
            bytes_accessed=4 * width * hidden,
            transcendentals=half * hidden,
        ),
        name="forward",
    )(recv, plan, w_in_0, w_out_0, w_in[0], w_out[0])
    ret = lax.all_to_all(
        ret.reshape(rows // PAIR, PAIR, width), "expert", split_axis=0, concat_axis=0, tiled=True
    ).reshape(rows, width)
    d_w_in, d_w_out = pl.pallas_call(
        grads_kernel,
        out_shape=(
            jax.ShapeDtypeStruct((width, hidden), low),
            jax.ShapeDtypeStruct((hidden, width), low),
        ),
        in_specs=[vmem] * 4 + [hbm],
        out_specs=(hbm,) * 2,
        input_output_aliases={4: 1},
        scratch_shapes=[
            pltpu.VMEM((3, width, chunk), low),
            pltpu.VMEM((3, chunk - EARLY, width), low),
            pltpu.SemaphoreType.DMA((3, 4)),
        ],
        compiler_params=params(28),
        cost_estimate=pl.CostEstimate(
            flops=4 * half * width * hidden,
            bytes_accessed=4 * width * hidden,
            transcendentals=0,
        ),
        name="grads",
    )(x_t, g_rows, act, d_pre, d_w_out)
    mixed, d_tokens, d_gates_t = pl.pallas_call(
        combine_kernel,
        out_shape=(
            jax.ShapeDtypeStruct((count, width), low),
            jax.ShapeDtypeStruct((count, width), low),
            jax.ShapeDtypeStruct((2, count), jnp.float32),
        ),
        in_specs=[vmem] * 4,
        out_specs=(hbm, hbm, vmem),
        scratch_shapes=[
            pltpu.VMEM((count, width), low),
            pltpu.VMEM((count, width), low),
            pltpu.SemaphoreType.DMA((2,)),
        ],
        compiler_params=params(12),
        name="combine",
    )(ret, pick, gate_cols, cotangent)
    return (mixed, d_tokens, jnp.transpose(d_gates_t, (1, 0)), d_w_in[None], d_w_out[None])


def solution(mesh):
    rows = P(("groups", "expert"), None)
    return jax.shard_map(
        per_device,
        mesh=mesh,
        in_specs=(rows, rows, rows, rows, P("expert", None, None), P("expert", None, None), rows),
        out_specs=(
            rows,
            rows,
            rows,
            P(("groups", "expert"), None, None),
            P(("groups", "expert"), None, None),
        ),
        check_vma=False,
    )
```
